32 devices in a mesh: expert: 4 (over y, x), shard: 8 (over z, core).
Axes of the slice: x: 2, y: 2, z: 4, core: 2. Of those that a mesh axis runs over, the one named last changes fastest.
Arguments:
- tokens: float32 [4, 2048, 1024], P('expert', 'shard'), may hold values from -6 to 6
- block_ids: int32 [4, 2048], P('expert'), may hold values from 0 to 7, never falling along the last dimension, each value on 1 to 512 neighbouring positions
- routes: int32 [4, 2048, 8], P('expert', 'shard'), may hold values from 0 to 31, all different within a row; in each aligned block of 256 rows (0 to 255, 256 to 511, ..., all dimensions but the last counted through in order) at most 80 rows name the same one
- gates: float32 [4, 2048, 8], P('expert', 'shard'), may hold values from 0.3 to 1
- attn_gain: float32 [1024], P(('expert', 'shard')), may hold values from 0.5 to 1.5
- w_query: float32 [1024, 1024], P(('expert', 'shard')), may hold values from -0.1875 to 0.1875
- w_key: float32 [1024, 512], P(('expert', 'shard')), may hold values from -0.1875 to 0.1875
- w_value: float32 [1024, 512], P(('expert', 'shard')), may hold values from -0.1875 to 0.1875
- w_out: float32 [1024, 1024], P(('expert', 'shard')), may hold values from -6 to 6
- moe_gain: float32 [1024], P(('expert', 'shard')), may hold values from 0.5 to 1.5
- w_gate: float32 [32, 1024, 512], P('expert', 'shard'), may hold values from -0.1875 to 0.1875
- w_up: float32 [32, 1024, 512], P('expert', 'shard'), may hold values from -0.1875 to 0.1875
- w_down: float32 [32, 1024, 512], P('expert', 'shard'), may hold values from -0.25 to 0.25
- cotangent: float32 [4, 2048, 1024], P('expert', 'shard'), may hold values from -6 to 6
Outputs:
- output: float32 [4, 2048, 1024], P('expert', 'shard')
- token_grad: float32 [4, 2048, 1024], P('expert', 'shard')
- gate_grad: float32 [4, 2048, 8], P('expert', 'shard')
- attn_gain_grad: float32 [1024], P(('expert', 'shard'))
- w_query_grad: float32 [1024, 1024], P(('expert', 'shard'))
- w_key_grad: float32 [1024, 512], P(('expert', 'shard'))
- w_value_grad: float32 [1024, 512], P(('expert', 'shard'))
- w_out_grad: float32 [1024, 1024], P(('expert', 'shard'))
- moe_gain_grad: float32 [1024], P(('expert', 'shard'))
- w_gate_grad: float32 [32, 1024, 512], P('expert', 'shard')
- w_up_grad: float32 [32, 1024, 512], P('expert', 'shard')
- w_down_grad: float32 [32, 1024, 512], P('expert', 'shard')
The draws below stay inside these ranges and needn't reach their ends.
Inputs may be any that keep to these rules, and one draw needn't show every extreme that they name: `routes`: each token names 8 different experts. In the rows of one device no expert is named more than 80 times, and in some device's rows one expert is named exactly 80 times. `block_ids`: along each sequence the numbers start at 0, never fall and rise by at most one; each number covers 1 to 512 positions, one exactly 512.
All inputs are finite; a program needn't handle non-finite values.
Results may differ from the reference program's by a relative error of at most 0.023.
Values may be sent and summed in bfloat16 or wider, within the bound.
No kernel may reach another device: no remote copies, remote signals or barrier semaphores. Data moves between devices by JAX's collectives and lax.ppermute only.
A program may use at most 192 MiB of HBM per device.

```python
import math
import jax
import jax.numpy as jnp
import numpy as np
from jax import lax

D = 1024
H = 16
KVH = 8
HD = 64
EXPERTS = 32
F = 512
TOP = 8
TOK_DEV = 256
BLOCK = 256
SEQLEN = 2048
SEQS = 4
CAP = 80
N_EXPERT = 4
N_SHARD = 8


def steps_of(rng, dims, split, least, high):
    def one(dim, blocks):
        steps = jax.random.uniform(jax.random.fold_in(jax.random.fold_in(rng, 6), dim), (blocks,), jnp.float32, least / len(split), high / len(split))
        return jnp.repeat(jnp.exp(steps), dims[dim] // blocks).reshape((-1,) + (1,) * (len(dims) - dim - 1))

    level = one(*split[0])
    for cut in split[1:]:
        level = level * one(*cut)
    return level


def length_profile(count, total, limit, lean):
    weights = [(1 << 20) // math.isqrt(standing ** lean) + 1 for standing in range(2, count + 1)]
    surplus, given = total - limit - (count - 1), [1] * (count - 1)
    while surplus > 0:
        free = [i for i in range(count - 1) if given[i] < limit]
        mass, remaining = sum([weights[i] for i in free]), surplus
        for i in free:
            extra = min(limit - given[i], max(1, remaining * weights[i] // mass), surplus)
            given[i] = given[i] + extra
            surplus = surplus - extra
    return np.array([limit] + given)


def uneven(key, amount, total, limit, skew):
    if amount == 2:
        one = jax.random.randint(key, (), max(1, total - limit), min(limit, total - 1) + 1)
        return jnp.stack([one, total - one])
    sizes = jnp.asarray(length_profile(amount, total, limit, skew), jnp.int32)
    pairs = (amount - 1) // 2
    source_of, receiver = sizes[1:1 + 2 * pairs:2], sizes[2:2 + 2 * pairs:2]
    room = jnp.minimum(source_of - 1, limit - receiver)
    shifted = jax.random.randint(jax.random.fold_in(key, 1), (pairs,), 0, 1 << 20) % (room + 1)
    sizes = sizes.at[1:1 + 2 * pairs:2].set(source_of - shifted).at[2:2 + 2 * pairs:2].set(receiver + shifted)
    return sizes[jax.random.permutation(jax.random.fold_in(key, 2), amount)]


def shared_out(stream_key, own, number, rows, amount, top, bound, lean):
    order = jax.random.permutation(stream_key, amount)
    crowded, usual = portions_of(amount, rows * top, bound, lean, True), portions_of(amount, rows * top, bound, lean, False)
    places = jnp.arange(amount)

    def named(sizes, turn):
        used = int((sizes > 0).sum())
        fixed = max(1, used // 4)
        moved = fixed + (places - fixed + turn * (used - fixed)) % max(1, amount - fixed)
        return jnp.zeros((amount,), jnp.int32).at[order[jnp.where(places < fixed, places, moved)]].set(jnp.asarray(sizes, jnp.int32))

    sizes = jnp.where(number % 4 == 0, named(crowded, number // 4), named(usual, number - number // 4 - 1))
    mixed = jax.random.permutation(jax.random.fold_in(own, 3), amount)
    source_of, taker = mixed[0:amount // 2 * 2:2], mixed[1:amount // 2 * 2:2]
    slack = jnp.minimum(sizes[source_of] - 1, bound - sizes[taker]) // 2
    slack = jnp.where((source_of == order[0]) | (taker == order[0]) | (sizes[taker] == 0), 0, jnp.maximum(slack, 0))
    moved = jax.random.randint(jax.random.fold_in(own, 4), (amount // 2,), 0, 1 << 20) % (slack + 1)
    sizes = sizes.at[source_of].add(-moved).at[taker].add(moved)
    labels = jnp.searchsorted(jnp.cumsum(sizes), jnp.arange(rows * top), side="right").astype(jnp.int32)
    listing = labels.reshape(top, rows).T
    listing = listing[jax.random.permutation(jax.random.fold_in(own, 1), rows)]
    turn = jax.random.randint(jax.random.fold_in(own, 2), (rows, 1), 0, top)
    return jnp.take_along_axis(listing, (jnp.arange(top)[None, :] + turn) % top, axis=1)


def portions_of(count, total, most, skew, full):
    loads = [(1 << 20) // math.isqrt(rank ** skew) + 1 for rank in range(1, count + 1)]
    largest = most if full else min(most, max(-(-total // count), total * loads[0] // sum(loads)))
    least = 1 if total - largest >= count - 1 else 0
    holding, spare = [largest] + [least] * (count - 1), total - largest - least * (count - 1)
    while spare > 0:
        movable = [i for i in range(1, count) if holding[i] < largest] or [i for i in range(1, count) if holding[i] < most]
        whole, remaining = sum([loads[i] for i in movable]), spare
        for i in movable:
            more = min(most - holding[i], max(1, remaining * loads[i] // whole), spare)
            holding[i] = holding[i] + more
            spare = spare - more
    return np.array(holding)


def noise(key, extent, scale, most, cuts=(), held_as=jnp.bfloat16):
    level = steps_of(key, extent, cuts, -0.22, 0.18) if cuts else 1.0
    array = jax.random.normal(key, extent, jnp.float32) * scale * level
    return jnp.minimum(jnp.maximum(array, -most), most).astype(held_as)


def setup_inputs(seed: int = 0) -> dict:
    key_of = jax.random.split(jax.random.key(seed), 15)
    tokens = noise(key_of[0], (SEQS, SEQLEN, D), 1.0, 6.0, ((0, 4), (1, 8)), jnp.float32)
    block_ids = jax.vmap(lambda own: jnp.searchsorted(jnp.cumsum(uneven(own, TOK_DEV * N_SHARD // BLOCK, SEQLEN, 2 * BLOCK, 1)), jnp.arange(SEQLEN), side="right"))(jax.random.split(key_of[1], SEQS)).reshape((SEQS, SEQLEN)).astype(jnp.int32)
    routes_keys = jax.random.split(jax.random.fold_in(key_of[2], 1), SEQS * SEQLEN // TOK_DEV)
    routes_turns = jax.random.permutation(jax.random.fold_in(key_of[2], 3), SEQS * SEQLEN // TOK_DEV)
    routes = jax.vmap(lambda own, number: shared_out(jax.random.fold_in(key_of[2], 2), own, number, TOK_DEV, EXPERTS, TOP, CAP, 2))(routes_keys, routes_turns).reshape((SEQS, SEQLEN, TOP))
    gates = jnp.clip(jnp.exp(math.log(1.0) - 1.2039728 * jax.random.uniform(key_of[3], (SEQS, SEQLEN, TOP), jnp.float32) ** steps_of(key_of[3], (SEQS, SEQLEN, TOP), ((0, 4), (1, 8)), -0.2, 0.2)), 0.3, 1.0)
    attn_gain = jnp.clip(1.0 + 0.1 * jax.random.normal(key_of[4], (D,), jnp.float32), 0.5, 1.5)
    w_query = noise(key_of[5], (D, H * HD), D ** -0.5, 0.1875, ((0, 32),), jnp.float32)
    w_key = noise(key_of[6], (D, KVH * HD), D ** -0.5, 0.1875, ((0, 32),), jnp.float32)
    w_value = noise(key_of[7], (D, KVH * HD), D ** -0.5, 0.1875, ((0, 32),), jnp.float32)
    w_out = noise(key_of[8], (H * HD, D), 1 ** -0.5, 6.0, ((0, 32),), jnp.float32)
    moe_gain = jnp.clip(1.0 + 0.1 * jax.random.normal(key_of[9], (D,), jnp.float32), 0.5, 1.5)
    w_gate = noise(key_of[10], (EXPERTS, D, F), D ** -0.5, 0.1875, ((0, 4), (1, 8)), jnp.float32)
    w_up = noise(key_of[11], (EXPERTS, D, F), D ** -0.5, 0.1875, ((0, 4), (1, 8)), jnp.float32)
    w_down = noise(key_of[12], (EXPERTS, D, F), F ** -0.5, 0.25, ((0, 4), (1, 8)), jnp.float32)
    cotangent = noise(key_of[13], (SEQS, SEQLEN, D), 1.0, 6.0, ((0, 4), (1, 8)), jnp.float32)
    return {"tokens": tokens, "block_ids": block_ids, "routes": routes, "gates": gates, "attn_gain": attn_gain, "w_query": w_query, "w_key": w_key, "w_value": w_value, "w_out": w_out, "moe_gain": moe_gain, "w_gate": w_gate, "w_up": w_up, "w_down": w_down, "cotangent": cotangent}


@jax.custom_vjp
def low(v):
    return lax.optimization_barrier(v.astype(jnp.bfloat16)).astype(jnp.float32)

@jax.custom_vjp
def low_back(v):
    return v

def low_keep(v):
    return (low(v), None)

def low_pass(kept, grad):
    return (grad,)

def back_keep(v):
    return (v, None)

def back_low(kept, grad):
    return (low(grad),)
low.defvjp(low_keep, low_pass)
low_back.defvjp(back_keep, back_low)
EPSILON = 1e-06
PRECISE = lax.Precision.HIGHEST

def rope_tables(length, offset, width):
    half = width // 2
    freqs = 10000.0 ** (-(jnp.arange(half, dtype=jnp.float32) * 2.0 / width))
    places = offset + jnp.arange(length, dtype=jnp.float32)
    angles = places[:, None] * freqs[None, :]
    return (jnp.cos(angles), jnp.sin(angles))

def rotate(value, cosine, sine):
    half = value.shape[-1] // 2
    first = value[..., :half]
    second = value[..., half:]
    cosine = cosine[:, None, :]
    sine = sine[:, None, :]
    return jnp.concatenate([first * cosine - second * sine, second * cosine + first * sine], axis=-1)

def rms_norm(values, gain):
    return values * lax.rsqrt(lax.optimization_barrier(jnp.mean(values * values, axis=-1, keepdims=True)) + EPSILON) * gain

def matmul(left, right):
    return jnp.dot(left, right, precision=PRECISE, preferred_element_type=jnp.float32)

def attend_block(queries, query_blocks, keys, values, key_blocks, scale):
    scores = low_back(jnp.einsum('bkgd,skd->kgbs', queries, keys, precision=PRECISE) * scale)
    allowed = key_blocks[None, :] <= query_blocks[:, None]
    scores = jnp.where(allowed, scores, -1e+30)
    highest = lax.optimization_barrier(jnp.max(scores, axis=-1, keepdims=True))
    weights = jnp.exp(scores - highest)
    probs = low(weights / lax.optimization_barrier(jnp.sum(weights, axis=-1, keepdims=True)))
    return jnp.einsum('kgbs,skd->bkgd', probs, values, precision=PRECISE)

def sequence_attention(queries, keys, values, blocks, scale):
    length = queries.shape[0]
    block_rows = 512 if length % 512 == 0 else length
    number = length // block_rows
    query_split = queries.reshape(number, block_rows, KVH, H // KVH, HD)
    block_split = blocks.reshape(number, block_rows)

    def one_block(couple):
        return attend_block(couple[0], couple[1], keys, values, blocks, scale)
    result = lax.map(jax.checkpoint(one_block), (query_split, block_split))
    return result.reshape(length, H * HD)

def one_expert(bundle):
    rows_in, gate_matrix, up_matrix, down_matrix = bundle
    gate_pre = low_back(matmul(rows_in, gate_matrix))
    up_pre = low_back(matmul(rows_in, up_matrix))
    hidden = low(jax.nn.silu(gate_pre) * up_pre)
    return low(low_back(jnp.einsum('rf,df->rd', hidden, down_matrix, precision=PRECISE)))

def reference(tokens, block_ids, routes, gates, attn_gain, w_query, w_key, w_value, w_out, moe_gain, w_gate, w_up, w_down, cotangent):
    devices = N_EXPERT * N_SHARD
    total_rows = SEQS * SEQLEN
    flat_routes = routes.reshape(total_rows * TOP)
    matches = (flat_routes[:, None] == jnp.arange(EXPERTS, dtype=jnp.int32)[None, :]).astype(jnp.int32)
    grouped = matches.reshape(devices, TOK_DEV * TOP, EXPERTS)
    earlier = jnp.cumsum(grouped, axis=1) - grouped
    ranks = lax.optimization_barrier(jnp.sum(earlier * grouped, axis=-1)).reshape(total_rows * TOP)
    senders = jnp.arange(total_rows * TOP, dtype=jnp.int32) // (TOK_DEV * TOP)
    slots = flat_routes * (devices * CAP) + senders * CAP + ranks
    token_of = jnp.arange(total_rows * TOP, dtype=jnp.int32) // TOP
    scale = HD ** (-0.5)
    cosine, sine = rope_tables(SEQLEN, 0.0, HD)

    def forward(tokens_in, gates_in, gain_one, query_w, key_w, value_w, out_w, gain_two, gate_w, up_w, down_w):
        flat = tokens_in.reshape(total_rows, D)
        normed = low(rms_norm(flat, low(gain_one)))
        query_pre = low_back(matmul(normed, low(query_w)))
        key_pre = low_back(matmul(normed, low(key_w)))
        values = low(low_back(matmul(normed, low(value_w))))
        queries = low(rotate(query_pre.reshape(SEQS, SEQLEN, H, HD), cosine, sine))
        keys = low(rotate(key_pre.reshape(SEQS, SEQLEN, KVH, HD), cosine, sine))
        queries = queries.reshape(SEQS, SEQLEN, KVH, H // KVH, HD)
        values = values.reshape(SEQS, SEQLEN, KVH, HD)

        def one_sequence(bundle):
            return sequence_attention(bundle[0], bundle[1], bundle[2], bundle[3], scale)
        mixed = lax.map(one_sequence, (queries, keys, values, block_ids))
        mixed = low(low_back(mixed.reshape(total_rows, H * HD)))
        branch = low_back(matmul(mixed, low(out_w)))
        middle = flat + branch
        normed_two = low(rms_norm(middle, low(gain_two)))
        buffer = jnp.zeros((EXPERTS * devices * CAP, D), dtype=jnp.float32).at[slots].set(normed_two[token_of])
        buffer = low_back(buffer).reshape(EXPERTS, devices * CAP, D)
        results = lax.map(jax.checkpoint(one_expert), (buffer, low(gate_w), low(up_w), low(down_w)))
        picked = results.reshape(EXPERTS * devices * CAP, D)[slots].reshape(total_rows, TOP, D)
        mixture = jnp.einsum('rkd,rk->rd', picked, gates_in.reshape(total_rows, TOP), precision=PRECISE)
        return (middle + mixture).reshape(SEQS, SEQLEN, D)
    output, pullback = jax.vjp(forward, tokens, gates, attn_gain, w_query, w_key, w_value, w_out, moe_gain, w_gate, w_up, w_down)
    grads = pullback(cotangent)
    return (output, grads[0], grads[1], grads[2], grads[3], grads[4], grads[5], grads[6], grads[7], grads[8], grads[9], grads[10])
```

```python
import functools

import jax
import jax.numpy as jnp
from jax import lax
from jax.experimental import pallas as pl
from jax.experimental.pallas import tpu as pltpu
from jax.sharding import PartitionSpec as P

H = 16
KVH = 8
HD = 64
EXPERTS = 32
TOP = 8
CAP = 80
EPSILON = 1e-06
LANES = 128
PAIRS = KVH // 2
GATE_ROWS = 16

BF = jnp.bfloat16
F32 = jnp.float32
VMEM_BYTES = 56 * 1024 * 1024


def dot(left, right):
    return lax.dot_general(left, right, (((1,), (0,)), ((), ())), preferred_element_type=F32)


def dot_nt(left, right):
    return lax.dot_general(left, right, (((1,), (1,)), ((), ())), preferred_element_type=F32)


def dot_tn(left, right):
    return lax.dot_general(left, right, (((0,), (0,)), ((), ())), preferred_element_type=F32)


def call(kernel, grid, scalars, inputs, in_specs, out_shapes, out_specs, scratch=(), flops=0):
    moved = sum(x.size * x.dtype.itemsize for x in inputs)
    moved += sum(x.size * x.dtype.itemsize for x in jax.tree.leaves(out_shapes))
    return pl.pallas_call(
        kernel,
        grid_spec=pltpu.PrefetchScalarGridSpec(
            num_scalar_prefetch=1,
            grid=grid,
            in_specs=in_specs,
            out_specs=out_specs,
            scratch_shapes=list(scratch),
        ),
        out_shape=out_shapes,
        compiler_params=pltpu.CompilerParams(vmem_limit_bytes=VMEM_BYTES),
        cost_estimate=pl.CostEstimate(flops=int(flops), bytes_accessed=int(moved), transcendentals=0),
    )(scalars, *inputs)


def whole_spec(shape):
    return pl.BlockSpec(tuple(shape), lambda *_: (0,) * len(shape))


def lane_ids(rows):
    return lax.broadcasted_iota(jnp.int32, (rows, LANES), 1)


def swap_halves(tile):
    first = lane_ids(tile.shape[0]) % HD < HD // 2
    return jnp.where(first, pltpu.roll(tile, LANES - HD // 2, 1), pltpu.roll(tile, HD // 2, 1))


def turn(value, cosine, signed_sine, direction):
    tiles = []
    for i in range(value.shape[1] // LANES):
        tile = value[:, i * LANES : (i + 1) * LANES]
        tiles.append(tile * cosine + direction * (swap_halves(tile) * signed_sine))
    return tiles[0] if len(tiles) == 1 else jnp.concatenate(tiles, axis=1)


def row_chunk(ids, r, count):
    return ids[0] ^ r if count > 1 else 0


def z_chunk(ids, r, count):
    return ids[1] ^ r if count > 1 else 0


def half_chunk(ids, h, count):
    return ids[2] ^ h if count > 1 else 0


def span(index, size):
    return pl.ds(pl.multiple_of(index * size, size), size)


def qkv_kernel(nr, nh, ids, rows_ref, gain_ref, cos_ref, sin_ref, *rest):
    weights = rest[: nr * nh]
    q_ref, k_ref, v_ref, normed_ref = rest[nr * nh :]
    width = rows_ref.shape[-1]
    chunk = width // nr
    qn, kn = H * HD // nh, KVH * HD // nh
    normed_ref[...] = (rows_ref[0].astype(F32) * gain_ref[...]).astype(BF)
    cosine, sine = cos_ref[...], sin_ref[...]
    for h in range(nh):
        total = None
        for r in range(nr):
            part = dot(
                normed_ref[:, span(row_chunk(ids, r, nr), chunk)],
                weights[r * nh + h][:, qn : qn + 2 * kn],
            )
            total = part if total is None else total + part
        here = span(half_chunk(ids, h, nh), kn)
        k_ref[:, here] = turn(total[:, :kn], cosine, sine, 1.0).astype(BF)
        v_ref[:, here] = total[:, kn:].astype(BF)

    @pl.when(pl.program_id(0) == 0)
    def _():
        for h in range(nh):
            total = None
            for r in range(nr):
                part = dot(
                    normed_ref[:, span(row_chunk(ids, r, nr), chunk)], weights[r * nh + h][:, :qn]
                )
                total = part if total is None else total + part
            turned = turn(total, cosine, sine, 1.0).astype(BF).astype(F32) * HD**-0.5
            q_ref[:, span(half_chunk(ids, h, nh), qn)] = turned.astype(BF)


def project(ids, rows, gain, cosine, sine, weights):
    slots, length, width = rows.shape
    nr, nh = len(weights), len(weights[0])
    flat = [w for row in weights for w in row]
    return call(
        functools.partial(qkv_kernel, nr, nh),
        (slots,),
        ids,
        [rows, gain, cosine, sine, *flat],
        [
            pl.BlockSpec((1, length, width), lambda i, _: (i, 0, 0)),
            whole_spec(gain.shape),
            pl.BlockSpec((length, LANES), lambda i, _: (i, 0)),
            pl.BlockSpec((length, LANES), lambda i, _: (i, 0)),
            *[whole_spec(w.shape) for w in flat],
        ],
        [
            jax.ShapeDtypeStruct((length, H * HD), BF),
            jax.ShapeDtypeStruct((slots * length, KVH * HD), BF),
            jax.ShapeDtypeStruct((slots * length, KVH * HD), BF),
        ],
        [
            whole_spec((length, H * HD)),
            pl.BlockSpec((length, KVH * HD), lambda i, _: (i, 0)),
            pl.BlockSpec((length, KVH * HD), lambda i, _: (i, 0)),
        ],
        [pltpu.VMEM((length, width), BF)],
        2 * slots * length * width * 2 * KVH * HD,
    )


def to_half(tile, which, wanted):
    if which != wanted:
        tile = pltpu.roll(tile, HD, 1)
    return jnp.where(lane_ids(tile.shape[0]) // HD == wanted, tile, 0.0)


def attend_kernel(ids, q_ref, k_ref, v_ref, kx_ref, qx_ref, o_ref, low_ref, lse_ref):
    keys = jnp.concatenate([k_ref[...], kx_ref[...]], axis=1)
    values = v_ref[...]
    extra = qx_ref[...]
    rows = q_ref.shape[0]
    lanes = lane_ids(rows)
    sums = jnp.zeros((rows, LANES), F32)
    for t in range(2):
        tile = q_ref[:, t * LANES : (t + 1) * LANES].astype(F32)
        mixed = jnp.zeros((rows, LANES), F32)
        for w in range(2):
            query = jnp.concatenate([to_half(tile, w, t).astype(BF), extra], axis=1)
            scores = dot_nt(query, keys)
            highest = jnp.max(scores, axis=1, keepdims=True)
            weights = jnp.exp(scores - highest)
            total = jnp.sum(weights, axis=1, keepdims=True)
            out = dot(weights.astype(BF), values) / total
            mixed = mixed + to_half(out, t, w)
            sums = jnp.where(lanes == 2 * t + w, highest + jnp.log(total), sums)
        o_ref[:, t * LANES : (t + 1) * LANES] = mixed
        low_ref[:, t * LANES : (t + 1) * LANES] = mixed.astype(BF)
    lse_ref[0] = sums


def attend(ids, q, k, v, key_extra, query_extra):
    length, keys = q.shape[0], k.shape[0]
    quad = pl.BlockSpec((length, 2 * LANES), lambda p, _: (0, p))
    pair = pl.BlockSpec((keys, LANES), lambda p, _: (0, p))
    return call(
        attend_kernel,
        (PAIRS,),
        ids,
        [q, k, v, key_extra, query_extra],
        [quad, pair, pair, whole_spec(key_extra.shape), whole_spec(query_extra.shape)],
        [
            jax.ShapeDtypeStruct((length, H * HD), F32),
            jax.ShapeDtypeStruct((length, H * HD), BF),
            jax.ShapeDtypeStruct((PAIRS, length, LANES), F32),
        ],
        [quad, quad, pl.BlockSpec((1, length, LANES), lambda p, _: (p, 0, 0))],
        (),
        H * length * keys * (2 * LANES + LANES) * 2,
    )


def three_parts(value):
    high = value.astype(BF)
    rest = value - high.astype(F32)
    middle = rest.astype(BF)
    return high.astype(F32), middle.astype(F32), (rest - middle.astype(F32))


def with_parts(base, value, lanes):
    high, middle, low = three_parts(value)
    base = jnp.where(lanes == 16, high, base)
    base = jnp.where(lanes == 17, middle, base)
    return jnp.where(lanes == 18, low, base).astype(BF)


def attend_back_kernel(
    span_rows, ids, q_ref, do_ref, o_ref, lse_ref, k_ref, v_ref, kx_ref, qx_ref, cos_ref, sin_ref,
    dq_ref, dk_ref, dv_ref, sum_ref,
):
    rows = q_ref.shape[0]
    lanes = lane_ids(rows)
    extra = qx_ref[...].astype(F32)
    nothing = jnp.zeros((rows, LANES), F32)
    sums = lse_ref[0]
    queries, outs, pads_q, pads_o = [], [], [], []
    for t in range(2):
        at = slice(t * LANES, (t + 1) * LANES)
        tile, grad = q_ref[:, at].astype(F32), do_ref[:, at].astype(F32)
        product = grad * o_ref[:, at]
        for w in range(2):
            here = lanes // HD == w
            delta = jnp.sum(jnp.where(here, product, 0.0), axis=1, keepdims=True)
            log_sum = jnp.sum(jnp.where(lanes == 2 * t + w, sums, 0.0), axis=1, keepdims=True)
            q_pad = to_half(tile, w, t).astype(BF)
            o_pad = to_half(grad, w, t).astype(BF)
            queries.append(jnp.concatenate([q_pad, with_parts(extra, -log_sum, lanes)], axis=1))
            outs.append(jnp.concatenate([o_pad, with_parts(nothing, -delta, lanes)], axis=1))
            pads_q.append(q_pad)
            pads_o.append(o_pad)
    all_q = jnp.concatenate(pads_q, axis=0)
    all_o = jnp.concatenate(pads_o, axis=0)
    sum_ref[...] = jnp.zeros_like(sum_ref)

    def one_span(i, _):
        at = pl.ds(pl.multiple_of(i * span_rows, span_rows), span_rows)
        k_here, x_here = k_ref[at, :], kx_ref[at, :]
        keys = jnp.concatenate([k_here, x_here], axis=1)
        values = jnp.concatenate([v_ref[at, :], x_here], axis=1)
        probs, d_scores = [], []
        for n in range(4):
            prob = jnp.exp(dot_nt(keys, queries[n]))
            d_score = (prob * dot_nt(values, outs[n])).astype(BF)
            probs.append(prob.astype(BF))
            d_scores.append(d_score)
            sum_ref[n] += dot_tn(d_score, k_here)
        dv_ref[at, :] = dot(jnp.concatenate(probs, axis=1), all_o).astype(BF)
        d_key = dot(jnp.concatenate(d_scores, axis=1), all_q)
        dk_ref[at, :] = turn(d_key, cos_ref[at, :], sin_ref[at, :], -1.0).astype(BF)
        return 0

    lax.fori_loop(0, k_ref.shape[0] // span_rows, one_span, 0)
    cosine, sine = cos_ref[:rows, :], sin_ref[:rows, :]
    for t in range(2):
        tile = to_half(sum_ref[2 * t], t, 0) + to_half(sum_ref[2 * t + 1], t, 1)
        turned = turn(tile * HD**-0.5, cosine, sine, -1.0)
        dq_ref[:, t * LANES : (t + 1) * LANES] = turned.astype(BF)


def attend_back(ids, q, d_out, out, lse, k, v, key_extra, query_extra, cosine, sine):
    length, keys = q.shape[0], k.shape[0]
    quad = pl.BlockSpec((length, 2 * LANES), lambda p, _: (0, p))
    pair = pl.BlockSpec((keys, LANES), lambda p, _: (0, p))
    return call(
        functools.partial(attend_back_kernel, 512),
        (PAIRS,),
        ids,
        [q, d_out, out, lse, k, v, key_extra, query_extra, cosine, sine],
        [
            quad,
            quad,
            quad,
            pl.BlockSpec((1, length, LANES), lambda p, _: (p, 0, 0)),
            pair,
            pair,
            whole_spec(key_extra.shape),
            whole_spec(query_extra.shape),
            whole_spec(cosine.shape),
            whole_spec(sine.shape),
        ],
        [
            jax.ShapeDtypeStruct((length, H * HD), BF),
            jax.ShapeDtypeStruct((keys, KVH * HD), BF),
            jax.ShapeDtypeStruct((keys, KVH * HD), BF),
        ],
        [quad, pair, pair],
        [pltpu.VMEM((4, length, LANES), F32)],
        H * length * keys * 2 * (4 * LANES + 3 * LANES),
    )


def out_kernel(nr, nh, ids, x_ref, o_ref, gain_ref, *rest):
    weights = rest[: nr * nh]
    x2_ref, n2_ref = rest[nr * nh :]
    width = x_ref.shape[1]
    chunk, cols = H * HD // nr, width // nh
    for h in range(nh):
        at = span(half_chunk(ids, h, nh), cols)
        total = x_ref[:, at]
        for r in range(nr):
            total = total + dot(
                o_ref[:, span(row_chunk(ids, r, nr), chunk)], weights[r * nh + h][:, :cols]
            )
        x2_ref[:, at] = total
    middle = x2_ref[...]
    inverse = lax.rsqrt(jnp.mean(middle * middle, axis=1, keepdims=True) + EPSILON)
    n2_ref[...] = (middle * inverse * gain_ref[...]).astype(BF)


def project_out(ids, x, low, gain, weights):
    nr, nh = len(weights), len(weights[0])
    flat = [w for row in weights for w in row]
    ins = [x, low, gain, *flat]
    outs = [jax.ShapeDtypeStruct(x.shape, F32), jax.ShapeDtypeStruct(x.shape, BF)]
    return call(
        functools.partial(out_kernel, nr, nh),
        (1,),
        ids,
        ins,
        [whole_spec(i.shape) for i in ins],
        outs,
        [whole_spec(o.shape) for o in outs],
        (),
        2 * x.shape[0] * x.shape[1] * H * HD,
    )


def out_back_kernel(nr, nh, ids, c_ref, x2_ref, gain_ref, dn2_ref, low_ref, *rest):
    weights = rest[: nr * nh]
    dx2_ref, do_ref = rest[nr * nh : nr * nh + 2]
    grads = rest[nr * nh + 2 : 2 * nr * nh + 2]
    dr_ref, term_ref = rest[2 * nr * nh + 2 :]
    width = c_ref.shape[1]
    chunk, cols = H * HD // nr, width // nh
    middle, d_normed = x2_ref[...], dn2_ref[...]
    inverse = lax.rsqrt(jnp.mean(middle * middle, axis=1, keepdims=True) + EPSILON)
    scaled = d_normed * gain_ref[...]
    inner = jnp.mean(scaled * middle, axis=1, keepdims=True)
    d_middle = c_ref[...] + inverse * scaled - middle * (inverse * inverse * inverse * inner)
    dx2_ref[...] = d_middle
    dr_ref[...] = d_middle.astype(BF)
    term_ref[...] = (d_normed * middle * inverse).astype(BF)
    ones = jnp.ones((middle.shape[0], LANES), BF)
    for r in range(nr):
        at = span(row_chunk(ids, r, nr), chunk)
        low = low_ref[:, at]
        gain_grad = dot_tn(term_ref[:, at], ones).astype(BF)
        total = None
        for h in range(nh):
            branch = dr_ref[:, span(half_chunk(ids, h, nh), cols)]
            part = dot_nt(branch, weights[r * nh + h][:, :cols])
            total = part if total is None else total + part
            grads[r * nh + h][:, :cols] = dot_tn(low, branch).astype(BF)
            grads[r * nh + h][:, cols:] = gain_grad
        do_ref[:, at] = total.astype(BF)


def project_out_back(ids, c, x2, gain, dn2, low, weights):
    nr, nh = len(weights), len(weights[0])
    flat = [w for row in weights for w in row]
    ins = [c, x2, gain, dn2, low, *flat]
    rows, cols = H * HD // nr, c.shape[1] // nh
    outs = [jax.ShapeDtypeStruct(c.shape, F32), jax.ShapeDtypeStruct((c.shape[0], H * HD), BF)]
    outs += [jax.ShapeDtypeStruct((rows, cols + LANES), BF)] * (nr * nh)
    got = call(
        functools.partial(out_back_kernel, nr, nh),
        (1,),
        ids,
        ins,
        [whole_spec(i.shape) for i in ins],
        outs,
        [whole_spec(o.shape) for o in outs],
        [pltpu.VMEM(c.shape, BF), pltpu.VMEM(c.shape, BF)],
        4 * c.shape[0] * c.shape[1] * H * HD,
    )
    return got[0], got[1], [[got[2 + r * nh + h] for h in range(nh)] for r in range(nr)]


def picks(slot_ref, experts):
    tokens = slot_ref.shape[-1]
    places = lax.broadcasted_iota(jnp.int32, (CAP, tokens), 0).astype(F32)
    rows = [places == slot_ref[0, j : j + 1, :] for j in range(experts)]
    return rows[0] if experts == 1 else jnp.concatenate(rows, axis=0)


def gather_kernel(groups, per, experts, with_gates, ids, slot_ref, *rest):
    if with_gates:
        gate_ref, rest = rest[0], rest[1:]
    tokens, out_ref = rest[:groups], rest[groups]
    chosen = picks(slot_ref, experts)
    low = chosen.astype(F32).astype(BF)
    for g in range(groups):

        @pl.when(pl.program_id(0) // per == g)
        def _(g=g):
            rows = dot(low, tokens[g][0]).astype(BF)
            for j in range(experts):
                out_ref[j, 0] = rows[j * CAP : (j + 1) * CAP]

    if with_gates:
        for j in range(experts):
            mine = chosen[j * CAP : (j + 1) * CAP]
            gates = jnp.sum(jnp.where(mine, gate_ref[0, j : j + 1, :], 0.0), axis=1, keepdims=True)
            rest[groups + 1][j, 0] = jnp.broadcast_to(gates, (CAP, LANES))


def gather_rows(ids, slots, groups, gates=None):
    blocks, experts, length = slots.shape
    per, width = groups[0].shape[0], groups[0].shape[-1]
    ins, specs = [slots], [pl.BlockSpec((1, experts, length), lambda i, _: (i, 0, 0))]
    if gates is not None:
        ins.append(gates)
        specs.append(specs[0])
    for g, tokens in enumerate(groups):
        ins.append(tokens)
        specs.append(
            pl.BlockSpec(
                (1, length, width), lambda i, _, g=g: (jnp.clip(i - g * per, 0, per - 1), 0, 0)
            )
        )
    outs = [jax.ShapeDtypeStruct((experts, blocks, CAP, width), BF)]
    out_specs = [pl.BlockSpec((experts, 1, CAP, width), lambda i, _: (0, i, 0, 0))]
    if gates is not None:
        outs.append(jax.ShapeDtypeStruct((experts, blocks, CAP, LANES), F32))
        out_specs.append(pl.BlockSpec((experts, 1, CAP, LANES), lambda i, _: (0, i, 0, 0)))
    return call(
        functools.partial(gather_kernel, len(groups), per, experts, gates is not None),
        (blocks,),
        ids,
        ins,
        specs,
        outs,
        out_specs,
        (),
        2 * blocks * experts * CAP * length * width,
    )


def expert_kernel(nz, ids, x_ref, c_ref, gate_ref, *rest):
    weights, rest = rest[:nz], rest[nz:]
    y_ref, dx_ref, gg_ref = rest[:3]
    grads, acc_ref = rest[3 : 3 + nz], rest[3 + nz]
    chunk = x_ref.shape[-1] // nz
    step, last = pl.program_id(1), pl.num_programs(1) - 1
    a = b = ch = None
    for r in range(nz):
        at = span(z_chunk(ids, r, nz), chunk)
        x, c = x_ref[0, :, at], c_ref[0, :, at]
        parts = (
            dot(x, weights[r][0, 0]),
            dot(x, weights[r][0, 1]),
            dot(c, weights[r][0, 2]),
        )
        a, b, ch = parts if a is None else (a + parts[0], b + parts[1], ch + parts[2])
    gate = gate_ref[0][:, :1]
    sig = 1.0 / (1.0 + jnp.exp(-a))
    act = a * sig
    hidden = (act * b).astype(BF).astype(F32)
    gg_ref[0] = jnp.broadcast_to(jnp.sum(hidden * ch, axis=1, keepdims=True), gg_ref.shape[1:])
    hg = (hidden * gate).astype(BF)
    dh = ch * gate
    da = (dh * b * sig * (1.0 + a * (1.0 - sig))).astype(BF)
    db = (dh * act).astype(BF)

    @pl.when(step == 0)
    def _():
        acc_ref[...] = jnp.zeros_like(acc_ref)

    for r in range(nz):
        at = span(z_chunk(ids, r, nz), chunk)
        x, c = x_ref[0, :, at], c_ref[0, :, at]
        y_ref[0, :, at] = dot_nt(hg, weights[r][0, 2]).astype(BF)
        dx_ref[0, :, at] = (dot_nt(da, weights[r][0, 0]) + dot_nt(db, weights[r][0, 1])).astype(BF)
        acc_ref[r, 0] += dot_tn(x, da)
        acc_ref[r, 1] += dot_tn(x, db)
        acc_ref[r, 2] += dot_tn(c, hg)

    @pl.when(step == last)
    def _():
        for r in range(nz):
            grads[r][0] = acc_ref[r].astype(BF)


def run_experts(ids, x_rows, c_rows, gate_rows, weights):
    experts, rows, width = x_rows.shape
    nz = len(weights)
    hidden = weights[0].shape[-1]
    tile = 256
    block = pl.BlockSpec((1, tile, width), lambda j, i, _: (j, i, 0))
    narrow = pl.BlockSpec((1, tile, LANES), lambda j, i, _: (j, i, 0))
    matrix = pl.BlockSpec((1,) + weights[0].shape[1:], lambda j, i, _: (j, 0, 0, 0))
    got = call(
        functools.partial(expert_kernel, nz),
        (experts, rows // tile),
        ids,
        [x_rows, c_rows, gate_rows, *weights],
        [block, block, narrow] + [matrix] * nz,
        [
            jax.ShapeDtypeStruct(x_rows.shape, BF),
            jax.ShapeDtypeStruct(x_rows.shape, BF),
            jax.ShapeDtypeStruct((experts, rows, LANES), F32),
        ]
        + [jax.ShapeDtypeStruct(w.shape, BF) for w in weights],
        [block, block, narrow] + [matrix] * nz,
        [pltpu.VMEM((nz,) + weights[0].shape[1:], F32)],
        2 * 9 * experts * rows * width * hidden,
    )
    return got[0], got[1], got[2], got[3:]


def spread_kernel(groups, per, experts, with_grads, ids, slot_ref, rows_ref, *rest):
    if with_grads:
        grad_ref, rest = rest[0], rest[1:]
    chosen = picks(slot_ref, experts)
    low = chosen.astype(F32).astype(BF)
    rows = [rows_ref[j, 0] for j in range(experts)]
    rows = rows[0] if experts == 1 else jnp.concatenate(rows, axis=0)
    total = dot_tn(low, rows).astype(BF)
    length, width = total.shape
    tail = None
    if with_grads:
        fit = width // length
        line = lax.broadcasted_iota(jnp.int32, (GATE_ROWS, width), 0)
        place = lax.broadcasted_iota(jnp.int32, (GATE_ROWS, width), 1) // length
        tail = jnp.zeros((GATE_ROWS, width), F32)
        for j in range(experts):
            mine = chosen[j * CAP : (j + 1) * CAP]
            sums = jnp.sum(jnp.where(mine, grad_ref[j, 0][:, :1], 0.0), axis=0, keepdims=True)
            wide = jnp.concatenate([sums] * fit, axis=1)
            number = ids[3] + j
            tail = tail + jnp.where((line == number // fit) & (place == number % fit), wide, 0.0)
    for g in range(groups):

        @pl.when(pl.program_id(0) // per == g)
        def _(g=g):
            rest[g][0, :length] = total
            if with_grads:
                rest[g][0, length:] = tail.astype(BF)


def spread_rows(ids, slots, rows, groups, grads=None):
    blocks, experts, length = slots.shape
    per, width = blocks // groups, rows.shape[-1]
    high = length + (GATE_ROWS if grads is not None else 0)
    ins = [slots, rows]
    specs = [
        pl.BlockSpec((1, experts, length), lambda i, _: (i, 0, 0)),
        pl.BlockSpec((experts, 1, CAP, width), lambda i, _: (0, i, 0, 0)),
    ]
    if grads is not None:
        ins.append(grads)
        specs.append(pl.BlockSpec((experts, 1, CAP, LANES), lambda i, _: (0, i, 0, 0)))
    return call(
        functools.partial(spread_kernel, groups, per, experts, grads is not None),
        (blocks,),
        ids,
        ins,
        specs,
        [jax.ShapeDtypeStruct((per, high, width), BF)] * groups,
        [
            pl.BlockSpec(
                (1, high, width), lambda i, _, g=g: (jnp.clip(i - g * per, 0, per - 1), 0, 0)
            )
            for g in range(groups)
        ],
        (),
        2 * blocks * experts * CAP * length * width,
    )


def qkv_grad_kernel(nr, nh, ids, rows_ref, gain_ref, dq_ref, dk_ref, dv_ref, *rest):
    grads, (normed_ref, acc_ref) = rest[: nr * nh], rest[nr * nh :]
    width = rows_ref.shape[-1]
    chunk = width // nr
    qn, kn = H * HD // nh, KVH * HD // nh
    step, last = pl.program_id(0), pl.num_programs(0) - 1
    normed_ref[...] = (rows_ref[0].astype(F32) * gain_ref[...]).astype(BF)

    @pl.when(step == 0)
    def _():
        for r in range(nr):
            x = normed_ref[:, span(row_chunk(ids, r, nr), chunk)]
            for h in range(nh):
                n = r * nh + h
                d_query = dq_ref[:, span(half_chunk(ids, h, nh), qn)]
                grads[n][:, :qn] = dot_tn(x, d_query).astype(BF)
        acc_ref[...] = jnp.zeros_like(acc_ref)

    for r in range(nr):
        x = normed_ref[:, span(row_chunk(ids, r, nr), chunk)]
        for h in range(nh):
            here = span(half_chunk(ids, h, nh), kn)
            acc_ref[r * nh + h, :, :kn] += dot_tn(x, dk_ref[:, here])
            acc_ref[r * nh + h, :, kn:] += dot_tn(x, dv_ref[:, here])

    @pl.when(step == last)
    def _():
        for n in range(nr * nh):
            grads[n][:, qn:] = acc_ref[n].astype(BF)


def project_grads(ids, rows, gain, dq, dk, dv, nr, nh):
    slots, length, width = rows.shape
    cols = (H + 2 * KVH) * HD // nh
    outs = [jax.ShapeDtypeStruct((width // nr, cols), BF)] * (nr * nh)
    keys = pl.BlockSpec((length, KVH * HD), lambda i, _: (i, 0))
    got = call(
        functools.partial(qkv_grad_kernel, nr, nh),
        (slots,),
        ids,
        [rows, gain, dq, dk, dv],
        [
            pl.BlockSpec((1, length, width), lambda i, _: (i, 0, 0)),
            whole_spec(gain.shape),
            whole_spec(dq.shape),
            keys,
            keys,
        ],
        outs,
        [whole_spec(o.shape) for o in outs],
        [
            pltpu.VMEM((length, width), BF),
            pltpu.VMEM((nr * nh, width // nr, 2 * KVH * HD // nh), F32),
        ],
        2 * slots * length * width * 2 * KVH * HD,
    )
    return [[got[r * nh + h] for h in range(nh)] for r in range(nr)]


def rows_back_kernel(nr, nh, ids, dq_ref, dkv_ref, x_ref, dx2_ref, gain_ref, *rest):
    weights = rest[: nr * nh]
    out_ref, grad_ref, low_ref = rest[nr * nh :]
    width = x_ref.shape[1]
    chunk = width // nr
    qn, kn = H * HD // nh, KVH * HD // nh
    low_ref[...] = dkv_ref[...].astype(BF)
    for r in range(nr):
        total = None
        for h in range(nh):
            at = half_chunk(ids, h, nh)
            weight = weights[r * nh + h]
            part = dot_nt(dq_ref[:, span(at, qn)], weight[:, :qn])
            part = part + dot_nt(low_ref[:, span(at, kn)], weight[:, qn : qn + kn])
            values = pl.ds(pl.multiple_of(KVH * HD + at * kn, kn), kn)
            part = part + dot_nt(low_ref[:, values], weight[:, qn + kn : qn + 2 * kn])
            total = part if total is None else total + part
        grad_ref[:, span(row_chunk(ids, r, nr), chunk)] = total
    x = x_ref[...]
    scaled = grad_ref[...] * gain_ref[...]
    inverse = lax.rsqrt(jnp.mean(x * x, axis=1, keepdims=True) + EPSILON)
    inner = jnp.mean(scaled * x, axis=1, keepdims=True)
    out_ref[...] = dx2_ref[...] + inverse * scaled - x * (inverse * inverse * inverse * inner)


def rows_back(ids, dq, dkv, x, dx2, gain, weights):
    nr, nh = len(weights), len(weights[0])
    ins = [dq, dkv, x, dx2, gain, *[w for row in weights for w in row]]
    return call(
        functools.partial(rows_back_kernel, nr, nh),
        (1,),
        ids,
        ins,
        [whole_spec(i.shape) for i in ins],
        jax.ShapeDtypeStruct(x.shape, F32),
        whole_spec(x.shape),
        [pltpu.VMEM(x.shape, F32), pltpu.VMEM(dkv.shape, BF)],
        2 * x.shape[0] * x.shape[1] * 2048,
    )


def swap(value, axis, distance):
    count = lax.axis_size(axis)
    return lax.ppermute(value, axis, [(i, i ^ distance) for i in range(count)])


def pick(array, index):
    return lax.dynamic_index_in_dim(array, index, 0, keepdims=False)


def gather_z(value):
    chips = lax.axis_size("shard") // 2
    if chips != 4:
        return [value] + [swap(value, "shard", 2 * r) for r in range(1, chips)]
    near, far = swap(value, "shard", 2), swap(value, "shard", 4)
    return [value, near, far, swap(far, "shard", 2)]


def scatter_z(parts):
    chips = len(parts)
    if chips != 4:
        got = [swap(parts[r], "shard", 2 * r) for r in range(1, chips)]
    else:
        step = swap(parts[3], "shard", 2)
        near = swap(parts[1], "shard", 2)
        far = (parts[2].astype(F32) + step.astype(F32)).astype(BF)
        got = [near, swap(far, "shard", 4)]
    total = parts[0].astype(F32)
    for one in got:
        total = total + one.astype(F32)
    return total


def in_order(mine, other, core, axis):
    return jnp.where(
        core == 0,
        jnp.concatenate([mine, other], axis=axis),
        jnp.concatenate([other, mine], axis=axis),
    )


def gather_matrix(halves, z, core, fast):
    if not fast:
        joined = jnp.concatenate([halves[0], halves[1]], axis=1)
        return [[lax.all_gather(joined, ("expert", "shard"), axis=0, tiled=True)]]
    mine, other = pick(halves, core), pick(halves, 1 - core)
    chip = in_order(mine, swap(other, "shard", 1), core, 0)
    stacked = jnp.stack(gather_z(chip))
    rows = jnp.concatenate([pick(stacked, z ^ i) for i in range(stacked.shape[0])], axis=0)
    blocks = [rows] + [swap(rows, "expert", r) for r in range(1, lax.axis_size("expert"))]
    return [[block, swap(block, "shard", 1)] for block in blocks]


def scatter_matrix(blocks, z, core, fast):
    if not fast:
        total = lax.psum_scatter(blocks[0][0], ("expert", "shard"), scatter_dimension=0, tiled=True)
        return total.astype(F32)
    sums = [
        (block[0].astype(F32) + swap(block[1], "shard", 1).astype(F32)).astype(BF)
        for block in blocks
    ]
    total = sums[0].astype(F32)
    for r in range(1, len(sums)):
        total = total + swap(sums[r], "expert", r).astype(F32)
    chips = lax.axis_size("shard") // 2
    parts = total.astype(BF).reshape(chips, total.shape[0] // chips, total.shape[1])
    rows = scatter_z([pick(parts, z ^ r) for r in range(chips)])
    rows = rows.reshape(2, rows.shape[0] // 2, rows.shape[1])
    mine = pick(rows, core)
    other = swap(pick(rows, 1 - core).astype(BF), "shard", 1).astype(F32)
    return jnp.where(core == 0, mine, other), jnp.where(core == 0, other, mine)


def gather_tokens(value, paired):
    bases = [value] + ([swap(value, "shard", 4)] if paired else [])
    groups = []
    for base in bases:
        count = lax.axis_size("expert")
        own = jnp.stack([base] + [swap(base, "expert", r) for r in range(1, count)])
        groups += [own, swap(own, "shard", 1)]
    return groups


def scatter_tokens(groups, paired):
    totals = []
    for n in range(len(groups) // 2):
        own, other = groups[2 * n], swap(groups[2 * n + 1], "shard", 1)
        sums = [
            (own[r].astype(F32) + other[r].astype(F32)).astype(BF) for r in range(own.shape[0])
        ]
        total = sums[0].astype(F32)
        for r in range(1, len(sums)):
            total = total + swap(sums[r], "expert", r).astype(F32)
        totals.append(total)
    if paired:
        return totals[0] + swap(totals[1].astype(BF), "shard", 4).astype(F32)
    return totals[0]


def body(
    tokens,
    block_ids,
    routes,
    gates,
    attn_gain,
    w_query,
    w_key,
    w_value,
    w_out,
    moe_gain,
    w_gate,
    w_up,
    w_down,
    cotangent,
):
    length, width = tokens.shape[1], tokens.shape[2]
    n_expert, n_shard = lax.axis_size("expert"), lax.axis_size("shard")
    chips = n_shard // 2
    local = w_gate.shape[0]
    fast = n_expert == 4 and n_shard == 8
    paired = chips == 4 and local % 4 == 0
    sides = 2 if paired else 1
    experts = local // (2 * sides)
    e, s = lax.axis_index("expert"), lax.axis_index("shard")
    z, core = s // 2, s % 2
    side = z // 2 if paired else 0
    first_expert = e * local + core * (local // 2) + side * experts
    ids = jnp.stack([e, z, core, first_expert]).astype(jnp.int32)

    x = tokens[0]
    c = cotangent[0]

    inverse_one = lax.rsqrt(jnp.mean(x * x, axis=-1, keepdims=True) + EPSILON)
    scaled_rows = (x * inverse_one).astype(BF)
    own_core = jnp.stack(gather_z(scaled_rows))
    rows = jnp.concatenate([own_core, swap(own_core, "shard", 1)], axis=0)

    def halves(matrix):
        low = matrix.astype(BF)
        return low.reshape(low.shape[0], 2, low.shape[1] // 2).transpose(1, 0, 2)

    def column(gain):
        return jnp.broadcast_to(gain.astype(BF)[None, :, None], (1, gain.shape[0], LANES // 2))

    if fast:
        gain_cols = jnp.concatenate([column(attn_gain), column(moe_gain)], axis=2)
        gain_cols = jnp.concatenate([gain_cols, gain_cols], axis=0)
        packed = jnp.concatenate([halves(w_query), halves(w_key), halves(w_value), gain_cols], axis=2)
        qkv_w = gather_matrix(packed, z, core, fast)
        blocks = jnp.stack([w[0][:, (H + 2 * KVH) * HD // 2 :] for w in qkv_w])
        blocks = jnp.concatenate([pick(blocks, e ^ i) for i in range(n_expert)], axis=0)
        gain_one = blocks[:, 0].astype(F32)[None]
        gain_two = blocks[:, LANES // 2].astype(F32)[None]
    else:
        packed = jnp.concatenate(
            [w_query.astype(BF), w_key.astype(BF), w_value.astype(BF)], axis=1
        )
        packed = lax.all_gather(packed, ("expert", "shard"), axis=0, tiled=True)
        qkv_w = [[packed]]
        both = jnp.stack([attn_gain.astype(BF), moe_gain.astype(BF)], axis=1)
        both = lax.all_gather(both, ("expert", "shard"), axis=0, tiled=True).astype(F32)
        gain_one, gain_two = both[:, 0][None], both[:, 1][None]
    nr, nh = len(qkv_w), len(qkv_w[0])
    out_w = gather_matrix(halves(w_out), z, core, fast)

    numbers = jnp.arange(EXPERTS, dtype=jnp.int32)
    named = routes[0][None, :, :] == numbers[:, None, None]
    dense = jnp.sum(jnp.where(named, gates[0][None, :, :], 0.0), axis=-1)
    dense = jnp.concatenate(gather_tokens(dense, paired), axis=0)
    gate_here = lax.dynamic_slice_in_dim(dense, first_expert, experts, 1)
    chosen = gate_here > 0.0
    before = jnp.triu(jnp.ones((length, length), BF), 1)
    ranks = jnp.einsum("net,tu->neu", chosen.astype(BF), before, preferred_element_type=F32)
    slots = jnp.where(chosen, ranks, -1.0)

    low = jnp.stack([w_gate.astype(BF), w_up.astype(BF), w_down.astype(BF)], axis=1)
    low = low.reshape((2, local // 2) + low.shape[1:])
    chip_w = in_order(pick(low, core), swap(pick(low, 1 - core), "shard", 1), core, 2)
    if paired:
        chip_w = chip_w.reshape((2, experts) + chip_w.shape[1:])
        here, there = pick(chip_w, side), pick(chip_w, 1 - side)
        far = swap(there, "shard", 4)
        expert_w = [here, swap(here, "shard", 2), far, swap(far, "shard", 2)]
    else:
        expert_w = gather_z(chip_w)

    c_groups = gather_tokens(c.astype(BF), paired)
    c_rows, gate_rows = gather_rows(ids, slots, c_groups, gate_here)

    owners = jnp.stack([s ^ (2 * r + k) for k in range(2) for r in range(chips)])
    places = (owners[:, None] * length + jnp.arange(length)[None, :]).reshape(n_shard * length)
    freqs = 10000.0 ** (-(jnp.arange(HD // 2, dtype=F32) * 2.0 / HD))
    angles = places.astype(F32)[:, None] * freqs[None, :]
    cosine, sine = jnp.cos(angles), jnp.sin(angles)
    cosine = jnp.concatenate([cosine] * 4, axis=1)
    sine = jnp.concatenate([-sine, sine] * 2, axis=1)
    every = block_ids[0].reshape(n_shard, length)
    key_blocks = jnp.concatenate([pick(every, s ^ (2 * r + k)) for k in range(2) for r in range(chips)])
    own_blocks = pick(every, s)
    lanes = jnp.arange(LANES, dtype=jnp.int32)[None, :]
    key_extra = ((lanes == key_blocks[:, None]) | ((lanes >= 16) & (lanes < 19))).astype(BF)
    query_extra = jnp.where((lanes < 16) & (lanes > own_blocks[:, None]), -1e30, 0.0).astype(BF)

    q, k, v = project(ids, rows, gain_one, cosine, sine, qkv_w)
    mixed, mixed_low, lse = attend(ids, q, k, v, key_extra, query_extra)
    x2, n2 = project_out(ids, x, mixed_low, gain_two, out_w)

    n2_groups = gather_tokens(n2, paired)
    (x_rows,) = gather_rows(ids, slots, n2_groups)
    flat = (experts, slots.shape[0] * CAP)
    y_rows, dx_rows, grad_rows, d_experts = run_experts(
        ids,
        x_rows.reshape(flat + (width,)),
        c_rows.reshape(flat + (width,)),
        gate_rows.reshape(flat + (LANES,)),
        expert_w,
    )
    split = (experts, slots.shape[0], CAP)
    count = len(n2_groups)
    dn2_parts = spread_rows(ids, slots, dx_rows.reshape(split + (width,)), count)
    dn2 = scatter_tokens(dn2_parts, paired)
    out_parts = spread_rows(
        ids, slots, y_rows.reshape(split + (width,)), count, grad_rows.reshape(split + (LANES,))
    )
    out_sum = scatter_tokens(out_parts, paired)
    output = x2 + out_sum[:length]
    gate_sums = out_sum[length : length + EXPERTS * length // width].reshape(EXPERTS, length)
    gate_grad = jnp.sum(jnp.where(named, gate_sums[:, :, None], 0.0), axis=0)

    if paired:
        step = swap(d_experts[3], "shard", 2)
        near = swap(d_experts[1], "shard", 2)
        far = (d_experts[2].astype(F32) + step.astype(F32)).astype(BF)
        there = swap(far, "shard", 4).astype(F32)
        here = d_experts[0].astype(F32) + near.astype(F32)
        d_chip = jnp.where(
            side == 0, jnp.concatenate([here, there], axis=0), jnp.concatenate([there, here], axis=0)
        )
    else:
        d_chip = scatter_z(d_experts)
    half = d_chip.shape[2] // 2
    d_chip = d_chip.astype(BF)
    mine = lax.dynamic_slice_in_dim(d_chip, core * half, half, 2)
    other = swap(lax.dynamic_slice_in_dim(d_chip, (1 - core) * half, half, 2), "shard", 1)
    d_expert = in_order(mine, other, core, 0).astype(F32)

    dx2, d_mixed, d_out_w = project_out_back(ids, c, x2, gain_two, dn2, mixed_low, out_w)
    dq, dk, dv = attend_back(
        ids, q, d_mixed, mixed, lse, k, v, key_extra, query_extra, cosine, sine
    )
    d_qkv_w = project_grads(ids, rows, gain_one, dq, dk, dv, nr, nh)
    dkv = jnp.concatenate([dk, dv], axis=1).reshape(2, chips, length, 2 * KVH * HD)
    dkv_core = swap(dkv[1], "shard", 1)
    dkv_sums = (dkv[0].astype(F32) + dkv_core.astype(F32)).astype(BF)
    dkv_own = scatter_z([dkv_sums[r] for r in range(chips)])
    token_grad = rows_back(ids, dq, dkv_own, x, dx2, gain_one, qkv_w)

    d_out = scatter_matrix(d_out_w, z, core, fast)
    d_qkv = scatter_matrix(d_qkv_w, z, core, fast)
    if fast:
        cols = width // 2
        d_out_full = jnp.concatenate([d_out[0][:, :cols], d_out[1][:, :cols]], axis=1)
        d_gain_two = d_out[0][:, cols]
        qn, kn = H * HD // 2, KVH * HD // 2
        d_query_w = jnp.concatenate([d[:, :qn] for d in d_qkv], axis=1)
        d_key_w = jnp.concatenate([d[:, qn : qn + kn] for d in d_qkv], axis=1)
        d_value_w = jnp.concatenate([d[:, qn + kn :] for d in d_qkv], axis=1)
    else:
        d_out_full, d_gain_two = d_out[:, :width], d_out[:, width]
        qn, kn = H * HD, KVH * HD
        d_query_w, d_key_w, d_value_w = d_qkv[:, :qn], d_qkv[:, qn : qn + kn], d_qkv[:, qn + kn :]
    row_sums = (
        jnp.sum(w_query.astype(BF).astype(F32) * d_query_w, axis=1)
        + jnp.sum(w_key.astype(BF).astype(F32) * d_key_w, axis=1)
        + jnp.sum(w_value.astype(BF).astype(F32) * d_value_w, axis=1)
    )
    d_gain_one = row_sums / attn_gain.astype(BF).astype(F32)

    return (
        output[None],
        token_grad[None],
        gate_grad[None],
        d_gain_one,
        d_query_w,
        d_key_w,
        d_value_w,
        d_out_full,
        d_gain_two,
        d_expert[:, 0],
        d_expert[:, 1],
        d_expert[:, 2],
    )


def solution(mesh):
    rows = P("expert", "shard", None)
    split = P(("expert", "shard"), None)
    gain = P(("expert", "shard"))
    in_specs = (
        rows, P("expert", None), rows, rows, gain, split, split, split, split, gain, rows, rows, rows, rows,
    )
    out_specs = (rows, rows, rows, gain, split, split, split, split, gain, rows, rows, rows)
    return jax.shard_map(body, mesh=mesh, in_specs=in_specs, out_specs=out_specs, check_vma=False)
```

```python
import functools

import jax
import jax.numpy as jnp
from jax import lax
from jax.experimental import pallas as pl
from jax.experimental.pallas import tpu as pltpu
from jax.sharding import PartitionSpec as P

H = 16
KVH = 8
HD = 64
EXPERTS = 32
TOP = 8
CAP = 80
EPSILON = 1e-06
LANES = 128
PAIRS = KVH // 2
GATE_ROWS = 16

BF = jnp.bfloat16
F32 = jnp.float32
VMEM_BYTES = 56 * 1024 * 1024


def dot(left, right):
    return lax.dot_general(left, right, (((1,), (0,)), ((), ())), preferred_element_type=F32)


def dot_nt(left, right):
    return lax.dot_general(left, right, (((1,), (1,)), ((), ())), preferred_element_type=F32)


def dot_tn(left, right):
    return lax.dot_general(left, right, (((0,), (0,)), ((), ())), preferred_element_type=F32)


def call(kernel, grid, scalars, inputs, in_specs, out_shapes, out_specs, scratch=(), aliases=None):
    return pl.pallas_call(
        kernel,
        grid_spec=pltpu.PrefetchScalarGridSpec(
            num_scalar_prefetch=1,
            grid=grid,
            in_specs=in_specs,
            out_specs=out_specs,
            scratch_shapes=list(scratch),
        ),
        out_shape=out_shapes,
        input_output_aliases=aliases or {},
        compiler_params=pltpu.CompilerParams(vmem_limit_bytes=VMEM_BYTES),
        cost_estimate=pl.CostEstimate(flops=0, bytes_accessed=0, transcendentals=0),
    )(scalars, *inputs)


def whole_spec(shape):
    return pl.BlockSpec(tuple(shape), lambda *_: (0,) * len(shape))


def lane_ids(rows):
    return lax.broadcasted_iota(jnp.int32, (rows, LANES), 1)


def swap_halves(tile):
    first = lane_ids(tile.shape[0]) % HD < HD // 2
    return jnp.where(first, pltpu.roll(tile, LANES - HD // 2, 1), pltpu.roll(tile, HD // 2, 1))


def turn(value, cosine, signed_sine, direction):
    tiles = []
    for i in range(value.shape[1] // LANES):
        tile = value[:, i * LANES : (i + 1) * LANES]
        tiles.append(tile * cosine + direction * (swap_halves(tile) * signed_sine))
    return tiles[0] if len(tiles) == 1 else jnp.concatenate(tiles, axis=1)


def row_chunk(ids, r, count):
    return ids[0] ^ r if count > 1 else 0


def z_chunk(ids, r, count):
    return ids[1] ^ r if count > 1 else 0


def half_chunk(ids, h, count):
    return ids[2] ^ h if count > 1 else 0


def span(index, size):
    return pl.ds(pl.multiple_of(index * size, size), size)


def columns(nh, width):
    on, qn, kn = width // nh, H * HD // nh, KVH * HD // nh
    return on, on + qn, on + qn + kn, on + qn + 2 * kn


def qkv_kernel(nr, nh, ids, rows_ref, gain_ref, cos_ref, sin_ref, *rest):
    weights = rest[:nh]
    q_ref, k_ref, v_ref, normed_ref = rest[nh:]
    width = rows_ref.shape[-1]
    chunk = width // nr
    qn, kn = H * HD // nh, KVH * HD // nh
    at_q, at_k, _, at_end = columns(nh, width)
    normed_ref[...] = (rows_ref[0].astype(F32) * gain_ref[...]).astype(BF)
    cosine, sine = cos_ref[...], sin_ref[...]
    for h in range(nh):
        total = None
        for r in range(nr):
            part = dot(
                normed_ref[:, span(row_chunk(ids, r, nr), chunk)],
                weights[h][r, :, at_k:at_end],
            )
            total = part if total is None else total + part
        here = span(half_chunk(ids, h, nh), kn)
        k_ref[:, here] = turn(total[:, :kn], cosine, sine, 1.0).astype(BF)
        v_ref[:, here] = total[:, kn:].astype(BF)

    @pl.when(pl.program_id(0) == 0)
    def _():
        for h in range(nh):
            total = None
            for r in range(nr):
                part = dot(
                    normed_ref[:, span(row_chunk(ids, r, nr), chunk)], weights[h][r, :, at_q:at_k]
                )
                total = part if total is None else total + part
            turned = turn(total, cosine, sine, 1.0).astype(BF).astype(F32) * HD**-0.5
            q_ref[:, span(half_chunk(ids, h, nh), qn)] = turned.astype(BF)


def project(ids, rows, gain, cosine, sine, weights):
    slots, length, width = rows.shape
    nr, nh = weights[0].shape[0], len(weights)
    flat = weights
    return call(
        functools.partial(qkv_kernel, nr, nh),
        (slots,),
        ids,
        [rows, gain, cosine, sine, *flat],
        [
            pl.BlockSpec((1, length, width), lambda i, _: (i, 0, 0)),
            whole_spec(gain.shape),
            pl.BlockSpec((length, LANES), lambda i, _: (i, 0)),
            pl.BlockSpec((length, LANES), lambda i, _: (i, 0)),
            *[whole_spec(w.shape) for w in flat],
        ],
        [
            jax.ShapeDtypeStruct((length, H * HD), BF),
            jax.ShapeDtypeStruct((slots * length, KVH * HD), BF),
            jax.ShapeDtypeStruct((slots * length, KVH * HD), BF),
        ],
        [
            whole_spec((length, H * HD)),
            pl.BlockSpec((length, KVH * HD), lambda i, _: (i, 0)),
            pl.BlockSpec((length, KVH * HD), lambda i, _: (i, 0)),
        ],
        [pltpu.VMEM((length, width), BF)],
    )


def to_half(tile, which, wanted):
    if which != wanted:
        tile = pltpu.roll(tile, HD, 1)
    return jnp.where(lane_ids(tile.shape[0]) // HD == wanted, tile, 0.0)


def attend_kernel(ids, q_ref, k_ref, v_ref, kx_ref, qx_ref, o_ref, low_ref, lse_ref):
    keys = jnp.concatenate([k_ref[...], kx_ref[...]], axis=1)
    values = v_ref[...]
    extra = qx_ref[...]
    rows = q_ref.shape[0]
    lanes = lane_ids(rows)
    sums = jnp.zeros((rows, LANES), F32)
    for t in range(2):
        tile = q_ref[:, t * LANES : (t + 1) * LANES].astype(F32)
        mixed = jnp.zeros((rows, LANES), F32)
        for w in range(2):
            query = jnp.concatenate([to_half(tile, w, t).astype(BF), extra], axis=1)
            scores = dot_nt(query, keys)
            highest = jnp.max(scores, axis=1, keepdims=True)
            weights = jnp.exp(scores - highest)
            total = jnp.sum(weights, axis=1, keepdims=True)
            out = dot(weights.astype(BF), values) / total
            mixed = mixed + to_half(out, t, w)
            sums = jnp.where(lanes == 2 * t + w, highest + jnp.log(total), sums)
        o_ref[:, t * LANES : (t + 1) * LANES] = mixed
        low_ref[:, t * LANES : (t + 1) * LANES] = mixed.astype(BF)
    lse_ref[0] = sums


def attend(ids, q, k, v, key_extra, query_extra):
    length, keys = q.shape[0], k.shape[0]
    quad = pl.BlockSpec((length, 2 * LANES), lambda p, _: (0, p))
    pair = pl.BlockSpec((keys, LANES), lambda p, _: (0, p))
    return call(
        attend_kernel,
        (PAIRS,),
        ids,
        [q, k, v, key_extra, query_extra],
        [quad, pair, pair, whole_spec(key_extra.shape), whole_spec(query_extra.shape)],
        [
            jax.ShapeDtypeStruct((length, H * HD), F32),
            jax.ShapeDtypeStruct((length, H * HD), BF),
            jax.ShapeDtypeStruct((PAIRS, length, LANES), F32),
        ],
        [quad, quad, pl.BlockSpec((1, length, LANES), lambda p, _: (p, 0, 0))],
    )


def three_parts(value):
    high = value.astype(BF)
    rest = value - high.astype(F32)
    middle = rest.astype(BF)
    return high.astype(F32), middle.astype(F32), (rest - middle.astype(F32))


def with_parts(base, value, lanes):
    high, middle, low = three_parts(value)
    base = jnp.where(lanes == 16, high, base)
    base = jnp.where(lanes == 17, middle, base)
    return jnp.where(lanes == 18, low, base).astype(BF)


def attend_back_kernel(
    span_rows, ids, q_ref, do_ref, o_ref, lse_ref, k_ref, v_ref, kx_ref, qx_ref, cos_ref, sin_ref,
    dq_ref, own_ref, other_ref, sum_ref,
):
    rows = q_ref.shape[0]
    lanes = lane_ids(rows)
    extra = qx_ref[...].astype(F32)
    nothing = jnp.zeros((rows, LANES), F32)
    sums = lse_ref[0]
    queries, outs, pads_q, pads_o = [], [], [], []
    for t in range(2):
        at = slice(t * LANES, (t + 1) * LANES)
        tile, grad = q_ref[:, at].astype(F32), do_ref[:, at].astype(F32)
        product = grad * o_ref[:, at]
        for w in range(2):
            here = lanes // HD == w
            delta = jnp.sum(jnp.where(here, product, 0.0), axis=1, keepdims=True)
            log_sum = jnp.sum(jnp.where(lanes == 2 * t + w, sums, 0.0), axis=1, keepdims=True)
            q_pad = to_half(tile, w, t).astype(BF)
            o_pad = to_half(grad, w, t).astype(BF)
            queries.append(jnp.concatenate([q_pad, with_parts(extra, -log_sum, lanes)], axis=1))
            outs.append(jnp.concatenate([o_pad, with_parts(nothing, -delta, lanes)], axis=1))
            pads_q.append(q_pad)
            pads_o.append(o_pad)
    all_q = jnp.concatenate(pads_q, axis=0)
    all_o = jnp.concatenate(pads_o, axis=0)
    sum_ref[...] = jnp.zeros_like(sum_ref)

    spans = k_ref.shape[0] // 2 // span_rows

    def one_span(i, _, part, out_ref):
        put = pl.ds(pl.multiple_of(i * span_rows, span_rows), span_rows)
        first = part * spans * span_rows
        at = pl.ds(pl.multiple_of(first + i * span_rows, span_rows), span_rows)
        k_here, x_here = k_ref[at, :], kx_ref[at, :]
        keys = jnp.concatenate([k_here, x_here], axis=1)
        values = jnp.concatenate([v_ref[at, :], x_here], axis=1)
        probs, d_scores = [], []
        for n in range(4):
            prob = jnp.exp(dot_nt(keys, queries[n]))
            d_score = (prob * dot_nt(values, outs[n])).astype(BF)
            probs.append(prob.astype(BF))
            d_scores.append(d_score)
            sum_ref[n] += dot_tn(d_score, k_here)
        out_ref[1, put, :] = dot(jnp.concatenate(probs, axis=1), all_o).astype(BF)
        d_key = dot(jnp.concatenate(d_scores, axis=1), all_q)
        d_key = turn(d_key, cos_ref[at, :], sin_ref[at, :], -1.0)
        out_ref[0, put, :] = d_key.astype(BF)
        return 0

    for part, out_ref in enumerate((own_ref, other_ref)):
        lax.fori_loop(0, spans, functools.partial(one_span, part=part, out_ref=out_ref), 0)
    cosine, sine = cos_ref[:rows, :], sin_ref[:rows, :]
    for t in range(2):
        tile = to_half(sum_ref[2 * t], t, 0) + to_half(sum_ref[2 * t + 1], t, 1)
        turned = turn(tile * HD**-0.5, cosine, sine, -1.0)
        dq_ref[:, t * LANES : (t + 1) * LANES] = turned.astype(BF)


def attend_back_part(*refs):
    attend_back_kernel(512, *refs[:11], *refs[14:])


def attend_back(ids, q, d_out, out, lse, k, v, key_extra, query_extra, cosine, sine, first, count, done):
    length, keys = q.shape[0], k.shape[0]
    quad = pl.BlockSpec((length, 2 * LANES), lambda p, _: (0, first + p))
    pair = pl.BlockSpec((keys, LANES), lambda p, _: (0, first + p))
    ins = [q, d_out, out, lse, k, v, key_extra, query_extra, cosine, sine]
    specs = [
        quad,
        quad,
        quad,
        pl.BlockSpec((1, length, LANES), lambda p, _: (first + p, 0, 0)),
        pair,
        pair,
        whole_spec(key_extra.shape),
        whole_spec(query_extra.shape),
        whole_spec(cosine.shape),
        whole_spec(sine.shape),
    ]
    if done is not None:
        ins += done
        specs += [pl.BlockSpec(memory_space=pl.ANY)] * 3
    return call(
        attend_back_part if done is not None else functools.partial(attend_back_kernel, 512),
        (count,),
        ids,
        ins,
        specs,
        [
            jax.ShapeDtypeStruct((length, H * HD), BF),
            jax.ShapeDtypeStruct((2, keys // 2, KVH * HD), BF),
            jax.ShapeDtypeStruct((2, keys // 2, KVH * HD), BF),
        ],
        [quad] + [pl.BlockSpec((2, keys // 2, LANES), lambda p, _: (0, 0, first + p))] * 2,
        [pltpu.VMEM((4, length, LANES), F32)],
        aliases={11: 0, 12: 1, 13: 2} if done is not None else None,
    )


def out_kernel(nr, nh, ids, x_ref, o_ref, gain_ref, *rest):
    weights = rest[:nh]
    x2_ref, n2_ref = rest[nh:]
    width = x_ref.shape[1]
    chunk, cols = H * HD // nr, width // nh
    for h in range(nh):
        at = span(half_chunk(ids, h, nh), cols)
        total = x_ref[:, at]
        for r in range(nr):
            total = total + dot(
                o_ref[:, span(row_chunk(ids, r, nr), chunk)], weights[h][r]
            )
        x2_ref[:, at] = total
    middle = x2_ref[...]
    inverse = lax.rsqrt(jnp.mean(middle * middle, axis=1, keepdims=True) + EPSILON)
    n2_ref[...] = (middle * inverse * gain_ref[...]).astype(BF)


def out_spec(weight, cols):
    return pl.BlockSpec(weight.shape[:2] + (cols,), lambda *_: (0, 0, 0))


def project_out(ids, x, low, gain, weights):
    nr, nh = weights[0].shape[0], len(weights)
    ins = [x, low, gain, *weights]
    outs = [jax.ShapeDtypeStruct(x.shape, F32), jax.ShapeDtypeStruct(x.shape, BF)]
    return call(
        functools.partial(out_kernel, nr, nh),
        (1,),
        ids,
        ins,
        [whole_spec(i.shape) for i in ins[:3]] + [out_spec(w, x.shape[1] // nh) for w in weights],
        outs,
        [whole_spec(o.shape) for o in outs],
    )


def out_back_kernel(nr, nh, ids, c_ref, x2_ref, gain_ref, dn2_ref, low_ref, *rest):
    weights = rest[:nh]
    dx2_ref, do_ref = rest[nh : nh + 2]
    grads = rest[nh + 2 : 2 * nh + 2]
    dr_ref, term_ref = rest[2 * nh + 2 :]
    width = c_ref.shape[1]
    chunk, cols = H * HD // nr, width // nh
    middle, d_normed = x2_ref[...], dn2_ref[...]
    inverse = lax.rsqrt(jnp.mean(middle * middle, axis=1, keepdims=True) + EPSILON)
    scaled = d_normed * gain_ref[...]
    inner = jnp.mean(scaled * middle, axis=1, keepdims=True)
    d_middle = c_ref[...] + inverse * scaled - middle * (inverse * inverse * inverse * inner)
    dx2_ref[...] = d_middle
    dr_ref[...] = d_middle.astype(BF)
    term_ref[...] = (d_normed * middle * inverse).astype(BF)
    ones = jnp.ones((middle.shape[0], LANES), BF)
    for r in range(nr):
        at = span(row_chunk(ids, r, nr), chunk)
        low = low_ref[:, at]
        gain_grad = dot_tn(term_ref[:, at], ones).astype(BF)
        total = None
        for h in range(nh):
            branch = dr_ref[:, span(half_chunk(ids, h, nh), cols)]
            part = dot_nt(branch, weights[h][r])
            total = part if total is None else total + part
            grads[h][r, :, :cols] = dot_tn(low, branch).astype(BF)
            grads[h][r, :, cols:] = gain_grad
        do_ref[:, at] = total.astype(BF)


def project_out_back(ids, c, x2, gain, dn2, low, weights):
    nr, nh = weights[0].shape[0], len(weights)
    ins = [c, x2, gain, dn2, low, *weights]
    rows, cols = H * HD // nr, c.shape[1] // nh
    outs = [jax.ShapeDtypeStruct(c.shape, F32), jax.ShapeDtypeStruct((c.shape[0], H * HD), BF)]
    outs += [jax.ShapeDtypeStruct((nr, rows, cols + LANES), BF)] * nh
    got = call(
        functools.partial(out_back_kernel, nr, nh),
        (1,),
        ids,
        ins,
        [whole_spec(i.shape) for i in ins[:5]] + [out_spec(w, cols) for w in weights],
        outs,
        [whole_spec(o.shape) for o in outs],
        [pltpu.VMEM(c.shape, BF), pltpu.VMEM(c.shape, BF)],
    )
    return got[0], got[1], got[2:]


def picks(slot_ref, experts):
    tokens = slot_ref.shape[-1]
    places = lax.broadcasted_iota(jnp.int32, (CAP, tokens), 0).astype(F32)
    rows = [places == slot_ref[0, j : j + 1, :] for j in range(experts)]
    return rows[0] if experts == 1 else jnp.concatenate(rows, axis=0)


def gather_kernel(groups, per, experts, with_gates, ids, slot_ref, *rest):
    if with_gates:
        gate_ref, rest = rest[0], rest[1:]
    tokens, out_ref = rest[:groups], rest[groups]
    chosen = picks(slot_ref, experts)
    low = chosen.astype(F32).astype(BF)
    for g in range(groups):

        @pl.when(pl.program_id(0) // per == g)
        def _(g=g):
            rows = dot(low, tokens[g][0, : slot_ref.shape[-1]]).astype(BF)
            for j in range(experts):
                out_ref[j, 0] = rows[j * CAP : (j + 1) * CAP]

    if with_gates:
        for j in range(experts):
            mine = chosen[j * CAP : (j + 1) * CAP]
            gates = jnp.sum(jnp.where(mine, gate_ref[0, j : j + 1, :], 0.0), axis=1, keepdims=True)
            rest[groups + 1][j, 0] = jnp.broadcast_to(gates, (CAP, LANES))


def gather_rows(ids, slots, groups, gates=None):
    blocks, experts, length = slots.shape
    per, width = groups[0].shape[0], groups[0].shape[-1]
    ins, specs = [slots], [pl.BlockSpec((1, experts, length), lambda i, _: (i, 0, 0))]
    if gates is not None:
        ins.append(gates)
        specs.append(specs[0])
    for g, tokens in enumerate(groups):
        ins.append(tokens)
        specs.append(
            pl.BlockSpec(
                (1,) + tokens.shape[1:], lambda i, _, g=g: (jnp.clip(i - g * per, 0, per - 1), 0, 0)
            )
        )
    outs = [jax.ShapeDtypeStruct((experts, blocks, CAP, width), BF)]
    out_specs = [pl.BlockSpec((experts, 1, CAP, width), lambda i, _: (0, i, 0, 0))]
    if gates is not None:
        outs.append(jax.ShapeDtypeStruct((experts, blocks, CAP, LANES), F32))
        out_specs.append(pl.BlockSpec((experts, 1, CAP, LANES), lambda i, _: (0, i, 0, 0)))
    return call(
        functools.partial(gather_kernel, len(groups), per, experts, gates is not None),
        (blocks,),
        ids,
        ins,
        specs,
        outs,
        out_specs,
    )


def expert_kernel(nz, ids, x_ref, c_ref, gate_ref, *rest):
    weights, rest = rest[:nz], rest[nz:]
    y_ref, dx_ref, gg_ref = rest[:3]
    grads, acc_ref = rest[3 : 3 + nz], rest[3 + nz]
    chunk = x_ref.shape[-1] // nz
    step, last = pl.program_id(1), pl.num_programs(1) - 1
    a = b = ch = None
    for r in range(nz):
        at = span(z_chunk(ids, r, nz), chunk)
        x, c = x_ref[0, :, at], c_ref[0, :, at]
        parts = (
            dot(x, weights[r][0, 0]),
            dot(x, weights[r][0, 1]),
            dot(c, weights[r][0, 2]),
        )
        a, b, ch = parts if a is None else (a + parts[0], b + parts[1], ch + parts[2])
    gate = gate_ref[0][:, :1]
    sig = 1.0 / (1.0 + jnp.exp(-a))
    act = a * sig
    hidden = (act * b).astype(BF).astype(F32)
    gg_ref[0] = jnp.broadcast_to(jnp.sum(hidden * ch, axis=1, keepdims=True), gg_ref.shape[1:])
    hg = (hidden * gate).astype(BF)
    dh = ch * gate
    da = (dh * b * sig * (1.0 + a * (1.0 - sig))).astype(BF)
    db = (dh * act).astype(BF)

    @pl.when(step == 0)
    def _():
        acc_ref[...] = jnp.zeros_like(acc_ref)

    for r in range(nz):
        at = span(z_chunk(ids, r, nz), chunk)
        x, c = x_ref[0, :, at], c_ref[0, :, at]
        y_ref[0, :, at] = dot_nt(hg, weights[r][0, 2]).astype(BF)
        dx_ref[0, :, at] = (dot_nt(da, weights[r][0, 0]) + dot_nt(db, weights[r][0, 1])).astype(BF)
        acc_ref[r, 0] += dot_tn(x, da)
        acc_ref[r, 1] += dot_tn(x, db)
        acc_ref[r, 2] += dot_tn(c, hg)

    @pl.when(step == last)
    def _():
        for r in range(nz):
            grads[r][0] = acc_ref[r].astype(BF)


def run_experts(ids, x_rows, c_rows, gate_rows, weights):
    experts, rows, width = x_rows.shape
    nz = len(weights)
    hidden = weights[0].shape[-1]
    tile = 256
    block = pl.BlockSpec((1, tile, width), lambda j, i, _: (j, i, 0))
    narrow = pl.BlockSpec((1, tile, LANES), lambda j, i, _: (j, i, 0))
    matrix = pl.BlockSpec((1,) + weights[0].shape[1:], lambda j, i, _: (j, 0, 0, 0))
    got = call(
        functools.partial(expert_kernel, nz),
        (experts, rows // tile),
        ids,
        [x_rows, c_rows, gate_rows, *weights],
        [block, block, narrow] + [matrix] * nz,
        [
            jax.ShapeDtypeStruct(x_rows.shape, BF),
            jax.ShapeDtypeStruct(x_rows.shape, BF),
            jax.ShapeDtypeStruct((experts, rows, LANES), F32),
        ]
        + [jax.ShapeDtypeStruct(w.shape, BF) for w in weights],
        [block, block, narrow] + [matrix] * nz,
        [pltpu.VMEM((nz,) + weights[0].shape[1:], F32)],
    )
    return got[0], got[1], got[2], got[3:]


def spread_kernel(groups, per, experts, with_grads, ids, slot_ref, rows_ref, *rest):
    if with_grads:
        grad_ref, rest = rest[0], rest[1:]
    chosen = picks(slot_ref, experts)
    low = chosen.astype(F32).astype(BF)
    rows = [rows_ref[j, 0] for j in range(experts)]
    rows = rows[0] if experts == 1 else jnp.concatenate(rows, axis=0)
    total = dot_tn(low, rows).astype(BF)
    length, width = total.shape
    tail = None
    if with_grads:
        fit = width // length
        line = lax.broadcasted_iota(jnp.int32, (GATE_ROWS, width), 0)
        place = lax.broadcasted_iota(jnp.int32, (GATE_ROWS, width), 1) // length
        tail = jnp.zeros((GATE_ROWS, width), F32)
        for j in range(experts):
            mine = chosen[j * CAP : (j + 1) * CAP]
            sums = jnp.sum(jnp.where(mine, grad_ref[j, 0][:, :1], 0.0), axis=0, keepdims=True)
            wide = jnp.concatenate([sums] * fit, axis=1)
            number = ids[3] + j
            tail = tail + jnp.where((line == number // fit) & (place == number % fit), wide, 0.0)
    for g in range(groups):

        @pl.when(pl.program_id(0) // per == g)
        def _(g=g):
            rest[g][0, :length] = total
            if with_grads:
                rest[g][0, length:] = tail.astype(BF)


def spread_rows(ids, slots, rows, groups, grads=None):
    blocks, experts, length = slots.shape
    per, width = blocks // groups, rows.shape[-1]
    high = length + (GATE_ROWS if grads is not None else 0)
    ins = [slots, rows]
    specs = [
        pl.BlockSpec((1, experts, length), lambda i, _: (i, 0, 0)),
        pl.BlockSpec((experts, 1, CAP, width), lambda i, _: (0, i, 0, 0)),
    ]
    if grads is not None:
        ins.append(grads)
        specs.append(pl.BlockSpec((experts, 1, CAP, LANES), lambda i, _: (0, i, 0, 0)))
    return call(
        functools.partial(spread_kernel, groups, per, experts, grads is not None),
        (blocks,),
        ids,
        ins,
        specs,
        [jax.ShapeDtypeStruct((per, high, width), BF)] * groups,
        [
            pl.BlockSpec(
                (1, high, width), lambda i, _, g=g: (jnp.clip(i - g * per, 0, per - 1), 0, 0)
            )
            for g in range(groups)
        ],
    )


def mixture_kernel(nz, groups, per, experts, tile, ids, slot_ref, gate_ref, *rest):
    n2_in, rest = rest[:groups], rest[groups:]
    c_in, rest = rest[:groups], rest[groups:]
    w_in, rest = rest[: 3 * nz], rest[3 * nz :]
    dn2_out, rest = rest[:groups], rest[groups:]
    y_out, rest = rest[: groups // 2], rest[groups // 2 :]
    dw_out, rest = rest[:nz], rest[nz:]
    n2_ref, c_ref, w_ref, x_rows, c_rows, gate_rows, grad_rows, inner_ref, dw_ref = rest[:9]
    n2_sem, c_sem, w_sem, dn2_sem, y_sem, dw_sem = rest[9:]
    length = slot_ref.shape[-1]
    width = n2_ref.shape[-1]
    chunk = width // nz
    blocks = groups * per

    def n2_copy(g):
        return pltpu.make_async_copy(n2_in[g], n2_ref.at[pl.ds(g * per, per)], n2_sem.at[g])

    def c_copy(g):
        return pltpu.make_async_copy(c_in[g], c_ref.at[pl.ds(g * per, per)], c_sem.at[g])

    def w_copy(r, k):
        return pltpu.make_async_copy(w_in[3 * r + k], w_ref.at[r, :, k], w_sem.at[r, k])

    for g in range(groups):
        c_copy(g).start()
        n2_copy(g).start()
    for r in range(nz):
        for k in range(3):
            w_copy(r, k).start()

    def chosen_rows(i):
        places = lax.broadcasted_iota(jnp.int32, (CAP, length), 0).astype(F32)
        return [places == slot_ref[i, j : j + 1, :] for j in range(experts)]

    def one_hot(chosen):
        chosen = [jnp.where(c, 1.0, 0.0).astype(BF) for c in chosen]
        return chosen[0] if experts == 1 else jnp.concatenate(chosen, axis=0)

    def gather(i, _):
        chosen = chosen_rows(i)
        low = one_hot(chosen)
        at = pl.ds(pl.multiple_of(i * CAP, CAP), CAP)
        got_x = dot(low, n2_ref[i]).astype(BF)
        got_c = dot(low, c_ref[i, :length]).astype(BF)
        for j in range(experts):
            x_rows[j, at] = got_x[j * CAP : (j + 1) * CAP]
            c_rows[j, at] = got_c[j * CAP : (j + 1) * CAP]
            gates = jnp.where(chosen[j], gate_ref[i, j : j + 1, :], 0.0)
            gate_rows[j, at] = jnp.broadcast_to(jnp.sum(gates, axis=1, keepdims=True), (CAP, LANES))
        return 0

    for g in range(groups):
        c_copy(g).wait()
        n2_copy(g).wait()
        lax.fori_loop(g * per, (g + 1) * per, gather, 0)
    for r in range(nz):
        for k in range(3):
            w_copy(r, k).wait()

    def dw_copy(j, r):
        return pltpu.make_async_copy(dw_ref.at[j, r], dw_out[r].at[j], dw_sem.at[j, r])

    for j in range(experts):

        def one_tile(i, _, j=j):
            at = pl.ds(pl.multiple_of(i * tile, tile), tile)
            a = b = ch = None
            for r in range(nz):
                cols = span(z_chunk(ids, r, nz), chunk)
                x, c = x_rows[j, at, cols], c_rows[j, at, cols]
                parts = (dot(x, w_ref[r, j, 0]), dot(x, w_ref[r, j, 1]), dot(c, w_ref[r, j, 2]))
                a, b, ch = parts if a is None else (a + parts[0], b + parts[1], ch + parts[2])
            gate = gate_rows[j, at][:, :1]
            sig = 1.0 / (1.0 + jnp.exp(-a))
            act = a * sig
            hidden = (act * b).astype(BF).astype(F32)
            grad = jnp.sum(hidden * ch, axis=1, keepdims=True)
            grad_rows[j, at] = jnp.broadcast_to(grad, (tile, LANES))
            hg = (hidden * gate).astype(BF)
            dh = ch * gate
            da = (dh * b * sig * (1.0 + a * (1.0 - sig))).astype(BF)
            db = (dh * act).astype(BF)
            inner_ref[0, at], inner_ref[1, at], inner_ref[2, at] = da, db, hg
            return 0

        lax.fori_loop(0, blocks * CAP // tile, one_tile, 0)
        for r in range(nz):
            cols = span(z_chunk(ids, r, nz), chunk)
            x, c = x_rows[j, :, cols], c_rows[j, :, cols]
            for k in range(3):
                dw_ref[j, r, k] = dot_tn(c if k == 2 else x, inner_ref[k]).astype(BF)
            dw_copy(j, r).start()

        def back_tile(i, _, j=j):
            at = pl.ds(pl.multiple_of(i * tile, tile), tile)
            da, db, hg = inner_ref[0, at], inner_ref[1, at], inner_ref[2, at]
            for r in range(nz):
                cols = span(z_chunk(ids, r, nz), chunk)
                c_rows[j, at, cols] = dot_nt(hg, w_ref[r, j, 2]).astype(BF)
                x_rows[j, at, cols] = (dot_nt(da, w_ref[r, j, 0]) + dot_nt(db, w_ref[r, j, 1])).astype(BF)
            return 0

        lax.fori_loop(0, blocks * CAP // tile, back_tile, 0)

    fit = width // length
    line = lax.broadcasted_iota(jnp.int32, (GATE_ROWS, width), 0)
    place = lax.broadcasted_iota(jnp.int32, (GATE_ROWS, width), 1) // length

    def spread(i, _):
        chosen = chosen_rows(i)
        low = one_hot(chosen)
        at = pl.ds(pl.multiple_of(i * CAP, CAP), CAP)
        both = []
        for rows_ref in (x_rows, c_rows):
            rows = [rows_ref[j, at] for j in range(experts)]
            both.append(rows[0] if experts == 1 else jnp.concatenate(rows, axis=0))
        n2_ref[i] = dot_tn(low, both[0]).astype(BF)
        c_ref[i, :length] = dot_tn(low, both[1]).astype(BF)
        tail = jnp.zeros((GATE_ROWS, width), F32)
        for j in range(experts):
            sums = jnp.where(chosen[j], grad_rows[j, at][:, :1], 0.0)
            wide = jnp.concatenate([jnp.sum(sums, axis=0, keepdims=True)] * fit, axis=1)
            number = ids[3] + j
            tail = tail + jnp.where((line == number // fit) & (place == number % fit), wide, 0.0)
        c_ref[i, length:] = tail.astype(BF)
        return 0

    def dn2_copy(g):
        return pltpu.make_async_copy(n2_ref.at[pl.ds(g * per, per)], dn2_out[g], dn2_sem.at[g])

    def y_copy(g):
        here = pl.ds((g % (groups // 2)) * per, per)
        return pltpu.make_async_copy(
            c_ref.at[pl.ds(g * per, per)], y_out[g // (groups // 2)].at[here], y_sem.at[g]
        )

    for g in range(groups):
        lax.fori_loop(g * per, (g + 1) * per, spread, 0)
        dn2_copy(g).start()
        y_copy(g).start()
    for g in range(groups):
        dn2_copy(g).wait()
        y_copy(g).wait()
    for j in range(experts):
        for r in range(nz):
            dw_copy(j, r).wait()


def mixture(ids, slots, gates, n2_groups, c_groups, weights):
    groups, nz = len(n2_groups), len(weights)
    per, length, width = n2_groups[0].shape
    blocks, experts, _ = slots.shape
    high, rows = c_groups[0].shape[1], blocks * CAP
    part = weights[0][0].shape
    matrices = (part[0], 3) + part[1:]
    anywhere = pl.BlockSpec(memory_space=pl.ANY)
    outs = [jax.ShapeDtypeStruct((per, length, width), BF)] * groups
    outs += [jax.ShapeDtypeStruct((groups // 2 * per, high, width), BF)] * 2
    outs += [jax.ShapeDtypeStruct(matrices, BF)] * nz
    got = call(
        functools.partial(mixture_kernel, nz, groups, per, experts, 256),
        (1,),
        ids,
        [slots, gates, *n2_groups, *c_groups, *[w for row in weights for w in row]],
        [whole_spec(slots.shape), whole_spec(gates.shape)] + [anywhere] * (2 * groups + 3 * nz),
        outs,
        [anywhere] * len(outs),
        [
            pltpu.VMEM((blocks, length, width), BF),
            pltpu.VMEM((blocks, high, width), BF),
            pltpu.VMEM((nz,) + matrices, BF),
            pltpu.VMEM((experts, rows, width), BF),
            pltpu.VMEM((experts, rows, width), BF),
            pltpu.VMEM((experts, rows, LANES), F32),
            pltpu.VMEM((experts, rows, LANES), F32),
            pltpu.VMEM((3, rows, part[-1]), BF),
            pltpu.VMEM((experts, nz) + matrices[1:], BF),
            pltpu.SemaphoreType.DMA((groups,)),
            pltpu.SemaphoreType.DMA((groups,)),
            pltpu.SemaphoreType.DMA((nz, 3)),
            pltpu.SemaphoreType.DMA((groups,)),
            pltpu.SemaphoreType.DMA((groups,)),
            pltpu.SemaphoreType.DMA((experts, nz)),
        ],
    )
    return got[:groups], got[groups : groups + 2], got[groups + 2 :]


def keys_grad_kernel(nr, nh, ids, rows_ref, gain_ref, own_ref, other_ref, *rest):
    grads, (normed_ref, acc_ref) = rest[:nh], rest[nh:]
    chunk, kn = rows_ref.shape[-1] // nr, KVH * HD // nh
    step, last = pl.program_id(0), pl.num_programs(0) - 1
    normed_ref[...] = (rows_ref[0].astype(F32) * gain_ref[...]).astype(BF)

    @pl.when(step == 0)
    def _():
        acc_ref[...] = jnp.zeros_like(acc_ref)

    def add(dkv_ref):
        for r in range(nr):
            x = normed_ref[:, span(row_chunk(ids, r, nr), chunk)]
            for h in range(nh):
                here = span(half_chunk(ids, h, nh), kn)
                acc_ref[r * nh + h, :, :kn] += dot_tn(x, dkv_ref[0, :, here])
                acc_ref[r * nh + h, :, kn:] += dot_tn(x, dkv_ref[1, :, here])

    half = pl.num_programs(0) // 2
    pl.when(step < half)(lambda: add(own_ref))
    pl.when(step >= half)(lambda: add(other_ref))

    @pl.when(step == last)
    def _():
        for n in range(nr * nh):
            grads[n % nh][n // nh] = acc_ref[n].astype(BF)


def keys_grads(ids, rows, gain, dkv, nr, nh):
    slots, length, width = rows.shape
    cols, half = 2 * KVH * HD // nh, slots // 2
    outs = [jax.ShapeDtypeStruct((nr, width // nr, cols), BF)] * nh
    return call(
        functools.partial(keys_grad_kernel, nr, nh),
        (slots,),
        ids,
        [rows, gain, *dkv],
        [
            pl.BlockSpec((1, length, width), lambda i, _: (i, 0, 0)),
            whole_spec(gain.shape),
            pl.BlockSpec((2, length, KVH * HD), lambda i, _: (0, jnp.minimum(i, half - 1), 0)),
            pl.BlockSpec((2, length, KVH * HD), lambda i, _: (0, jnp.maximum(i - half, 0), 0)),
        ],
        outs,
        [whole_spec(o.shape) for o in outs],
        [pltpu.VMEM((length, width), BF), pltpu.VMEM((nr * nh, width // nr, cols), F32)],
    )


def queries_grad_kernel(nr, nh, ids, rows_ref, gain_ref, dq_ref, *rest):
    grads, normed_ref = rest[:nh], rest[nh]
    chunk, qn = rows_ref.shape[-1] // nr, H * HD // nh
    normed_ref[...] = (rows_ref[...].astype(F32) * gain_ref[...]).astype(BF)
    for r in range(nr):
        x = normed_ref[:, span(row_chunk(ids, r, nr), chunk)]
        for h in range(nh):
            grads[h][r] = dot_tn(x, dq_ref[:, span(half_chunk(ids, h, nh), qn)]).astype(BF)


def queries_grads(ids, rows, gain, dq, nr, nh):
    ins = [rows, gain, dq]
    outs = [jax.ShapeDtypeStruct((nr, rows.shape[1] // nr, H * HD // nh), BF)] * nh
    return call(
        functools.partial(queries_grad_kernel, nr, nh),
        (1,),
        ids,
        ins,
        [whole_spec(i.shape) for i in ins],
        outs,
        [whole_spec(o.shape) for o in outs],
        [pltpu.VMEM(rows.shape, BF)],
    )


def rows_back_kernel(nr, nh, ids, dq_ref, dkv_ref, x_ref, dx2_ref, gain_ref, *rest):
    weights = rest[:nh]
    out_ref, grad_ref, low_ref = rest[nh:]
    width = x_ref.shape[1]
    chunk = width // nr
    qn, kn = H * HD // nh, KVH * HD // nh
    at_q, at_k, at_v, at_end = columns(nh, width)
    low_ref[...] = dkv_ref[...].astype(BF)
    for r in range(nr):
        total = None
        for h in range(nh):
            at = half_chunk(ids, h, nh)
            weight = weights[h]
            part = dot_nt(dq_ref[:, span(at, qn)], weight[r, :, at_q:at_k])
            part = part + dot_nt(low_ref[0, :, span(at, kn)], weight[r, :, at_k:at_v])
            part = part + dot_nt(low_ref[1, :, span(at, kn)], weight[r, :, at_v:at_end])
            total = part if total is None else total + part
        grad_ref[:, span(row_chunk(ids, r, nr), chunk)] = total
    x = x_ref[...]
    scaled = grad_ref[...] * gain_ref[...]
    inverse = lax.rsqrt(jnp.mean(x * x, axis=1, keepdims=True) + EPSILON)
    inner = jnp.mean(scaled * x, axis=1, keepdims=True)
    out_ref[...] = dx2_ref[...] + inverse * scaled - x * (inverse * inverse * inverse * inner)


def rows_back(ids, dq, dkv, x, dx2, gain, weights):
    nr, nh = weights[0].shape[0], len(weights)
    ins = [dq, dkv, x, dx2, gain, *weights]
    return call(
        functools.partial(rows_back_kernel, nr, nh),
        (1,),
        ids,
        ins,
        [whole_spec(i.shape) for i in ins],
        jax.ShapeDtypeStruct(x.shape, F32),
        whole_spec(x.shape),
        [pltpu.VMEM(x.shape, F32), pltpu.VMEM(dkv.shape, BF)],
    )


def swap(value, axis, distance):
    count = lax.axis_size(axis)
    return lax.ppermute(value, axis, [(i, i ^ distance) for i in range(count)])


def after(value, *done):
    return lax.optimization_barrier((value,) + done)[0]


def pick(array, index):
    return lax.dynamic_index_in_dim(array, index, 0, keepdims=False)


def gather_z(value):
    chips = lax.axis_size("shard") // 2
    if chips != 4:
        return [value] + [swap(value, "shard", 2 * r) for r in range(1, chips)]
    near, far = swap(value, "shard", 2), swap(value, "shard", 4)
    return [value, near, far, swap(far, "shard", 2)]


def scatter_z(parts):
    total = parts[0].astype(F32)
    for r in range(1, len(parts)):
        total = total + swap(parts[r], "shard", 2 * r).astype(F32)
    return total


def in_order(mine, other, core, axis):
    return jnp.where(
        core == 0,
        jnp.concatenate([mine, other], axis=axis),
        jnp.concatenate([other, mine], axis=axis),
    )


def add_low(*values):
    total = values[0].astype(F32)
    for value in values[1:]:
        total = total + value.astype(F32)
    return total.astype(BF)


def scatter_rows(total, z, core):
    chips = lax.axis_size("shard") // 2
    parts = total.reshape(chips, total.shape[0] // chips, total.shape[1])
    parts = [pick(parts, z ^ r) for r in range(chips)]
    step, near = swap(parts[3], "shard", 2), swap(parts[1], "shard", 2)
    far = add_low(parts[2], step)
    rows = parts[0].astype(F32) + near.astype(F32) + swap(far, "shard", 4).astype(F32)
    rows = rows.reshape(2, rows.shape[0] // 2, rows.shape[1])
    mine = pick(rows, core)
    other = swap(pick(rows, 1 - core).astype(BF), "shard", 1).astype(F32)
    return (jnp.where(core == 0, mine, other), jnp.where(core == 0, other, mine)), far


def body(
    tokens,
    block_ids,
    routes,
    gates,
    attn_gain,
    w_query,
    w_key,
    w_value,
    w_out,
    moe_gain,
    w_gate,
    w_up,
    w_down,
    cotangent,
):
    length, width = tokens.shape[1], tokens.shape[2]
    n_expert, n_shard = lax.axis_size("expert"), lax.axis_size("shard")
    chips = n_shard // 2
    local = w_gate.shape[0]
    fast = n_expert == 4 and n_shard == 8 and local % 4 == 0
    sides = 2 if fast else 1
    experts = local // (2 * sides)
    e, s = lax.axis_index("expert"), lax.axis_index("shard")
    z, core = s // 2, s % 2
    side = z // 2 if fast else 0
    first_expert = e * local + core * (local // 2) + side * experts
    ids = jnp.stack([e, z, core, first_expert]).astype(jnp.int32)
    nh = 2 if fast else 1

    x = tokens[0]
    c = cotangent[0]

    inverse_one = lax.rsqrt(jnp.mean(x * x, axis=-1, keepdims=True) + EPSILON)
    scaled_rows = (x * inverse_one).astype(BF)

    def halves(matrix):
        low = matrix.astype(BF)
        return low.reshape(low.shape[0], nh, low.shape[1] // nh).transpose(1, 0, 2)

    def column(gain):
        return jnp.broadcast_to(gain.astype(BF)[None, :, None], (nh, gain.shape[0], LANES // 2))

    packed = jnp.concatenate(
        [halves(w_out), halves(w_query), halves(w_key), halves(w_value), column(attn_gain), column(moe_gain)],
        axis=2,
    )
    at_q, at_k, at_v, at_end = columns(nh, width)

    numbers = jnp.arange(EXPERTS, dtype=jnp.int32)
    lines = EXPERTS * length // width

    def named_experts(routed):
        return routed[0][None, :, :] == numbers[:, None, None]

    def cotangent_rows(start):
        value, routed, gated = after((c, routes, gates), start)
        dense = jnp.sum(jnp.where(named_experts(routed), gated[0][None, :, :], 0.0), axis=-1)
        dense = dense.reshape(lines, width)
        high = dense.astype(BF)
        low = (dense - high.astype(F32)).astype(BF)
        return jnp.concatenate([value.astype(BF), high, low], axis=0)

    def own_experts(start):
        low = jnp.stack([m.astype(BF) for m in after((w_gate, w_up, w_down), start)], axis=1)
        low = low.reshape((2, local // 2) + low.shape[1:])
        return in_order(pick(low, core), swap(pick(low, 1 - core), "shard", 1), core, 2)

    def over_columns(value):
        return [swap(value, "expert", r) for r in range(1, n_expert)]

    if fast:
        mine, other = pick(packed, core), pick(packed, 1 - core)
        chip = in_order(mine, swap(other, "shard", 1), core, 0)

    s_late = after(s, chip) if fast else s
    owners = jnp.stack([s_late ^ (2 * r + k) for k in range(2) for r in range(chips)])
    places = (owners[:, None] * length + jnp.arange(length)[None, :]).reshape(n_shard * length)
    freqs = 10000.0 ** (-(jnp.arange(HD // 2, dtype=F32) * 2.0 / HD))
    angles = places.astype(F32)[:, None] * freqs[None, :]
    cosine, sine = jnp.cos(angles), jnp.sin(angles)
    cosine = jnp.concatenate([cosine] * 4, axis=1)
    sine = jnp.concatenate([-sine, sine] * 2, axis=1)
    every = block_ids[0].reshape(n_shard, length)
    key_blocks = jnp.concatenate(
        [pick(every, s_late ^ (2 * r + k)) for k in range(2) for r in range(chips)]
    )
    own_blocks = pick(every, s_late)
    lanes = jnp.arange(LANES, dtype=jnp.int32)[None, :]
    key_extra = ((lanes == key_blocks[:, None]) | ((lanes >= 16) & (lanes < 19))).astype(BF)
    query_extra = jnp.where((lanes < 16) & (lanes > own_blocks[:, None]), -1e30, 0.0).astype(BF)

    if fast:
        w_near, w_far = swap(chip, "shard", 2), swap(chip, "shard", 4)
        x_near = swap(scaled_rows, "shard", 2)
        x_far = swap(after(scaled_rows, w_far), "shard", 4)
        stacked = jnp.stack([chip, w_near, w_far, swap(w_far, "shard", 2)])
        block = jnp.concatenate([pick(stacked, z ^ i) for i in range(chips)], axis=0)
        c_pack = cotangent_rows(chip)
        chip_w = own_experts(chip).reshape((2, experts, 3, 2 * w_gate.shape[1], w_gate.shape[2]))
        here = [pick(chip_w, side)[:, k] for k in range(3)]
        there = [pick(chip_w, 1 - side)[:, k] for k in range(3)]
        w_got = over_columns(after(block, x_near, *here, *there))
        x_cross = swap(x_far, "shard", 2)
        c_far = swap(after(c_pack, x_far), "shard", 4)
        own_core = jnp.stack([scaled_rows, x_near, x_far, x_cross])
        x_other = swap(own_core, "shard", 1)
        rows = jnp.concatenate([own_core, x_other], axis=0)
        w_got = [after(got, own_core, c_far, cosine, sine, key_extra, query_extra) for got in w_got]
        blocks = jnp.stack([block] + w_got)
        attn_w = [blocks, swap(blocks, "shard", 1)]
        gain_cols = blocks[:, :, at_end:]
        gain_cols = jnp.concatenate([pick(gain_cols, e ^ i) for i in range(n_expert)], axis=0)
        near_a = swap(after(here[0], blocks), "shard", 2)
        far_a = swap(after(there[0], blocks), "shard", 4)
        c_own_got = over_columns(after(c_pack, attn_w[1]))
    else:
        c_pack = cotangent_rows(packed)
        own_core = jnp.stack(gather_z(scaled_rows))
        rows = jnp.concatenate([own_core, swap(own_core, "shard", 1)], axis=0)
        blocks = lax.all_gather(packed[0], ("expert", "shard"), axis=0, tiled=True)
        attn_w = [blocks[None]]
        gain_cols = blocks[:, at_end:]
        expert_w = gather_z(own_experts(packed))
    gain_one = gain_cols[:, 0].astype(F32)[None]
    gain_two = gain_cols[:, LANES // 2].astype(F32)[None]
    nr = attn_w[0].shape[0]

    q, k, v = project(ids, rows, gain_one, cosine, sine, attn_w)
    if fast:
        c_far_got = over_columns(after(c_far, q))
        near_b = swap(after(jnp.stack(here[1:], axis=1), near_a, q), "shard", 2)
        far_b = swap(after(there[1], far_a, q), "shard", 4)
        c_own = jnp.stack([c_pack] + c_own_got)
        q = after(q, near_a, far_a, c_own)
    mixed, mixed_low, lse = attend(ids, q, k, v, key_extra, query_extra)
    x2, n2 = project_out(ids, x, mixed_low, gain_two, attn_w)

    def places_of(groups):
        tails = jnp.concatenate([group[:, length:] for group in groups], axis=0).astype(F32)
        dense = (tails[:, :lines] + tails[:, lines:]).reshape(-1, EXPERTS, length)
        gate_here = lax.dynamic_slice_in_dim(dense, first_expert, experts, 1)
        chosen = gate_here > 0.0
        before = jnp.triu(jnp.ones((length, length), BF), 1)
        ranks = jnp.einsum("net,tu->neu", chosen.astype(BF), before, preferred_element_type=F32)
        return gate_here, jnp.where(chosen, ranks, -1.0)

    if fast:
        n2 = after(n2, near_b, far_b, *c_far_got)
        n2_far = swap(n2, "shard", 4)
        n2_own_got = over_columns(n2)
        cross_b = swap(after(jnp.stack([far_a, far_b], axis=1), n2), "shard", 2)
        n2_far_got = over_columns(after(n2_far, *n2_own_got))
        c_across = jnp.stack([after(piece, *n2_own_got) for piece in [c_far, *c_far_got]])
        c_own_other = swap(after(c_own, n2_far), "shard", 1)
        far_c = swap(after(there[2], n2_far), "shard", 4)
        cross_c = swap(far_c, "shard", 2)
        n2_own = jnp.stack([n2] + n2_own_got)
        n2_own_other = swap(n2_own, "shard", 1)
        n2_far_got = [after(got, far_c, cross_b, n2_own, c_own_other, c_across) for got in n2_far_got]
        n2_across = jnp.stack([n2_far] + n2_far_got)
        c_groups = [c_own, c_across, c_own_other, swap(after(c_across, n2_across), "shard", 1)]
        gate_here, slots = places_of(c_groups)
        n2_groups = [n2_own, n2_across, n2_own_other, swap(n2_across, "shard", 1)]
        expert_w = [here, [near_a, near_b[:, 0], near_b[:, 1]], [far_a, far_b, far_c], [cross_b[:, 0], cross_b[:, 1], cross_c]]
        dn2_parts, y_parts, d_experts = mixture(
            ids, slots, gate_here, n2_groups, c_groups, expert_w
        )
        step = swap(d_experts[3], "shard", 2)
        dn2_other = [swap(dn2_parts[3], "shard", 1), swap(dn2_parts[2], "shard", 1)][::-1]
        far_sums = add_low(dn2_parts[1], dn2_other[1])
        own_sums = add_low(dn2_parts[0], dn2_other[0])
        far_got = [swap(far_sums[r], "expert", r) for r in range(1, n_expert)]
        dn2_far = add_low(far_sums[0], *[after(got, own_sums, step) for got in far_got])
        dn2_got = swap(dn2_far, "shard", 4)
        own_got = [swap(after(own_sums[r], dn2_far), "expert", r) for r in range(1, n_expert)]
        d_far = add_low(d_experts[2], after(step, dn2_far))
        y_sum = add_low(y_parts[0], swap(after(y_parts[1], dn2_far), "shard", 1))
        y_sum = y_sum.reshape((2, n_expert) + y_sum.shape[1:])
        own_got = [after(got, d_far, y_sum) for got in own_got]
        dn2 = sum([g.astype(F32) for g in own_got + [dn2_got]], own_sums[0].astype(F32))
    else:
        c_own = jnp.stack([c_pack] + over_columns(c_pack))
        c_groups = [c_own, swap(c_own, "shard", 1)]
        gate_here, slots = places_of(c_groups)
        n2_own = jnp.stack([n2] + over_columns(n2))
        n2_groups = [n2_own, swap(n2_own, "shard", 1)]
        c_rows, gate_rows = gather_rows(ids, slots, c_groups, gate_here)
        (x_rows,) = gather_rows(ids, slots, n2_groups)
        flat = (experts, slots.shape[0] * CAP)
        y_rows, dx_rows, grad_rows, d_experts = run_experts(
            ids,
            x_rows.reshape(flat + (width,)),
            c_rows.reshape(flat + (width,)),
            gate_rows.reshape(flat + (LANES,)),
            expert_w,
        )
        split = (experts, slots.shape[0], CAP)
        dn2_parts = spread_rows(ids, slots, dx_rows.reshape(split + (width,)), 2)
        y_parts = spread_rows(
            ids, slots, y_rows.reshape(split + (width,)), 2, grad_rows.reshape(split + (LANES,))
        )
        own_sums = add_low(dn2_parts[0], swap(dn2_parts[1], "shard", 1))
        own_got = [swap(own_sums[r], "expert", r) for r in range(1, n_expert)]
        dn2 = sum([g.astype(F32) for g in own_got], own_sums[0].astype(F32))
        y_sum = add_low(y_parts[0], swap(y_parts[1], "shard", 1))[None]

    dx2, d_mixed, d_out_w = project_out_back(ids, c, x2, gain_two, dn2, mixed_low, attn_w)
    args = (mixed, lse, k, v, key_extra, query_extra, cosine, sine)
    if fast:
        far_a = swap(after(d_far[:, :2], dn2_got), "shard", 4)
        near_a = swap(after(d_experts[1][:, :1], dn2_got), "shard", 2)
        y_across_got = [swap(after(y_sum[1, r], dn2), "expert", r) for r in range(1, n_expert)]
        done = attend_back(ids, q, d_mixed, *args, 0, PAIRS // 2, None)
        y_across = add_low(y_sum[1, 0], *[after(got, done[0]) for got in y_across_got])
        far_b = swap(after(d_far[:, 2:], far_a, done[0]), "shard", 4)
        near_b = swap(after(d_experts[1][:, 1:], near_a, done[0]), "shard", 2)
        y_got = [swap(after(y_sum[0, r], y_across), "expert", r) for r in range(1, n_expert)]
        d_mixed = after(d_mixed, far_a, near_a, y_across)
        dq, *dkv = attend_back(ids, q, d_mixed, *args, PAIRS // 2, PAIRS // 2, done)
        y_got = [after(got, dq) for got in y_got]
        dkv[1] = after(dkv[1], far_b, near_b, *y_got)
        d_out_sums = add_low(d_out_w[0], swap(after(d_out_w[1], dkv[1]), "shard", 1))
        d_out_got = [swap(d_out_sums[r], "expert", r) for r in range(1, n_expert)]
    else:
        dq, *dkv = attend_back(ids, q, d_mixed, *args, 0, PAIRS, None)
        y_got = [swap(y_sum[0, r], "expert", r) for r in range(1, n_expert)]
    dkv_core = swap(dkv[1], "shard", 1)
    dkv_sums = add_low(dkv[0], dkv_core)
    dkv_parts = [dkv_sums[:, r * length : (r + 1) * length] for r in range(chips)]
    if fast:
        dkv_step, dkv_near = swap(dkv_parts[3], "shard", 2), swap(dkv_parts[1], "shard", 2)
        d_keys = keys_grads(ids, after(rows, dkv_sums, d_out_sums), gain_one, dkv, nr, nh)
        dq = after(dq, dkv_step, dkv_near, *d_out_got, *d_keys)
        d_queries = queries_grads(ids, scaled_rows, gain_one, dq, nr, nh)
        dkv_far = swap(after(add_low(dkv_parts[2], dkv_step), d_queries[0]), "shard", 4)
        y_far = swap(after(y_across, d_queries[0]), "shard", 4)
        d_halves = [swap(d_queries[1], "shard", 1), swap(d_keys[1], "shard", 1)]
        sums = jnp.concatenate(
            [add_low(d_queries[0], d_halves[0]), add_low(d_keys[0], d_halves[1])], axis=2
        )
        got = [swap(sums[r], "expert", r) for r in range(1, n_expert)]
        d_total = add_low(sums[0], *got)
        d_out_total = add_low(d_out_sums[0], *[after(g, sums) for g in d_out_got])
        dkv_own = sum([g.astype(F32) for g in (dkv_near, dkv_far)], dkv_parts[0].astype(F32))
        out_sum = sum([after(g, d_total).astype(F32) for g in y_got + [y_far]], y_sum[0, 0].astype(F32))
        parts, far_part = scatter_rows(jnp.concatenate([d_out_total, d_total], axis=1), z, core)
        dkv_own = after(dkv_own, far_part)
    else:
        out_sum = sum([g.astype(F32) for g in y_got], y_sum[0, 0].astype(F32))
        d_queries = queries_grads(ids, scaled_rows, gain_one, dq, nr, nh)
        d_keys = keys_grads(ids, rows, gain_one, dkv, nr, nh)
        dkv_own = scatter_z(dkv_parts)
        joined = jnp.concatenate([d_out_w[0][0], d_queries[0][0], d_keys[0][0]], axis=1)
        joined = lax.psum_scatter(joined, ("expert", "shard"), scatter_dimension=0, tiled=True)
        parts = [joined.astype(F32)]
    token_grad = rows_back(ids, dq, dkv_own, x, dx2, gain_one, attn_w)

    on, qn, kn = width // nh, H * HD // nh, KVH * HD // nh
    start = on + LANES
    d_out_full = jnp.concatenate([p[:, :on] for p in parts], axis=1)
    d_gain_two = parts[0][:, on]
    d_query_w = jnp.concatenate([p[:, start : start + qn] for p in parts], axis=1)
    d_key_w = jnp.concatenate([p[:, start + qn : start + qn + kn] for p in parts], axis=1)
    d_value_w = jnp.concatenate([p[:, start + qn + kn :] for p in parts], axis=1)
    row_sums = (
        jnp.sum(w_query.astype(BF).astype(F32) * d_query_w, axis=1)
        + jnp.sum(w_key.astype(BF).astype(F32) * d_key_w, axis=1)
        + jnp.sum(w_value.astype(BF).astype(F32) * d_value_w, axis=1)
    )
    d_gain_one = row_sums / attn_gain.astype(BF).astype(F32)

    output = x2 + out_sum[:length]
    gate_sums = out_sum[length : length + lines].reshape(EXPERTS, length)
    gate_grad = jnp.sum(jnp.where(named_experts(routes), gate_sums[:, :, None], 0.0), axis=0)

    if fast:
        there_sum = jnp.concatenate([far_a, far_b], axis=1).astype(F32)
        here_sum = d_experts[0].astype(F32)
        here_sum = here_sum + jnp.concatenate([near_a, near_b], axis=1).astype(F32)
        d_chip = jnp.where(
            side == 0,
            jnp.concatenate([here_sum, there_sum], axis=0),
            jnp.concatenate([there_sum, here_sum], axis=0),
        )
    else:
        d_chip = scatter_z(d_experts)
    half = d_chip.shape[2] // 2
    d_chip = d_chip.astype(BF)
    if fast:
        d_chip = after(d_chip, d_total)
    mine = lax.dynamic_slice_in_dim(d_chip, core * half, half, 2)
    other = swap(lax.dynamic_slice_in_dim(d_chip, (1 - core) * half, half, 2), "shard", 1)
    if fast:
        other = after(other, dkv_own)
    d_expert = in_order(mine, other, core, 0).astype(F32)

    return (
        output[None],
        token_grad[None],
        gate_grad[None],
        d_gain_one,
        d_query_w,
        d_key_w,
        d_value_w,
        d_out_full,
        d_gain_two,
        d_expert[:, 0],
        d_expert[:, 1],
        d_expert[:, 2],
    )


def solution(mesh):
    rows = P("expert", "shard", None)
    split = P(("expert", "shard"), None)
    gain = P(("expert", "shard"))
    in_specs = (
        rows, P("expert", None), rows, rows, gain, split, split, split, split, gain, rows, rows, rows, rows,
    )
    out_specs = (rows, rows, rows, gain, split, split, split, split, gain, rows, rows, rows)
    return jax.shard_map(body, mesh=mesh, in_specs=in_specs, out_specs=out_specs, check_vma=False)
```

```python
import functools

import jax
import jax.numpy as jnp
from jax import lax
from jax.experimental import pallas as pl
from jax.experimental.pallas import tpu as pltpu
from jax.sharding import PartitionSpec as P

H = 16
KVH = 8
HD = 64
EXPERTS = 32
TOP = 8
CAP = 80
EPSILON = 1e-06
LANES = 128
PAIRS = KVH // 2
BLOCKS = 2
GATE_ROWS = 16

BF = jnp.bfloat16
F32 = jnp.float32
VMEM_BYTES = 56 * 1024 * 1024


def dot(left, right):
    return lax.dot_general(left, right, (((1,), (0,)), ((), ())), preferred_element_type=F32)


def dot_nt(left, right):
    return lax.dot_general(left, right, (((1,), (1,)), ((), ())), preferred_element_type=F32)


def dot_tn(left, right):
    return lax.dot_general(left, right, (((0,), (0,)), ((), ())), preferred_element_type=F32)


def call(kernel, grid, scalars, inputs, in_specs, out_shapes, out_specs, scratch=(), aliases=None):
    return pl.pallas_call(
        kernel,
        grid_spec=pltpu.PrefetchScalarGridSpec(
            num_scalar_prefetch=1,
            grid=grid,
            in_specs=in_specs,
            out_specs=out_specs,
            scratch_shapes=list(scratch),
        ),
        out_shape=out_shapes,
        input_output_aliases=aliases or {},
        compiler_params=pltpu.CompilerParams(vmem_limit_bytes=VMEM_BYTES),
        cost_estimate=pl.CostEstimate(flops=0, bytes_accessed=0, transcendentals=0),
    )(scalars, *inputs)


def whole_spec(shape):
    return pl.BlockSpec(tuple(shape), lambda *_: (0,) * len(shape))


def lane_ids(rows):
    return lax.broadcasted_iota(jnp.int32, (rows, LANES), 1)


def swap_halves(tile):
    first = lane_ids(tile.shape[0]) % HD < HD // 2
    return jnp.where(first, pltpu.roll(tile, LANES - HD // 2, 1), pltpu.roll(tile, HD // 2, 1))


def turn(value, cosine, signed_sine, direction):
    tiles = []
    for i in range(value.shape[1] // LANES):
        tile = value[:, i * LANES : (i + 1) * LANES]
        tiles.append(tile * cosine + direction * (swap_halves(tile) * signed_sine))
    return tiles[0] if len(tiles) == 1 else jnp.concatenate(tiles, axis=1)


def row_chunk(ids, r, count):
    return ids[0] ^ r if count > 1 else 0


def z_chunk(ids, r, count):
    return ids[1] ^ r if count > 1 else 0


def half_chunk(ids, h, count):
    return ids[2] ^ h if count > 1 else 0


def span(index, size):
    return pl.ds(pl.multiple_of(index * size, size), size)


def columns(nh, width):
    on, qn, kn = width // nh, H * HD // nh, KVH * HD // nh
    return on, on + qn, on + qn + kn, on + qn + 2 * kn


def qkv_kernel(nr, nh, ids, own_ref, other_ref, gain_ref, cos_ref, sin_ref, *rest):
    weights = rest[:nh]
    q_ref, k_ref, v_ref, normed_ref = rest[nh:]
    width = own_ref.shape[-1]
    chunk = width // nr
    qn, kn = H * HD // nh, KVH * HD // nh
    at_q, at_k, _, at_end = columns(nh, width)
    normalize(own_ref, other_ref, gain_ref, normed_ref)
    cosine, sine = cos_ref[...], sin_ref[...]
    for h in range(nh):
        total = None
        for r in range(nr):
            part = dot(
                normed_ref[:, span(row_chunk(ids, r, nr), chunk)],
                weights[h][r, :, at_k:at_end],
            )
            total = part if total is None else total + part
        here = span(half_chunk(ids, h, nh), kn)
        k_ref[:, here] = turn(total[:, :kn], cosine, sine, 1.0).astype(BF)
        v_ref[:, here] = total[:, kn:].astype(BF)

    rows = q_ref.shape[0]

    @pl.when(pl.program_id(0) == 0)
    def _():
        for h in range(nh):
            total = None
            for r in range(nr):
                part = dot(
                    normed_ref[:rows, span(row_chunk(ids, r, nr), chunk)], weights[h][r, :, at_q:at_k]
                )
                total = part if total is None else total + part
            turned = turn(total, cosine[:rows], sine[:rows], 1.0).astype(BF).astype(F32) * HD**-0.5
            q_ref[:, span(half_chunk(ids, h, nh), qn)] = turned.astype(BF)


def normalize(own_ref, other_ref, gain_ref, normed_ref):
    own = pl.program_id(0) < pl.num_programs(0) // 2
    rows = jnp.where(own, own_ref[...], other_ref[...])
    normed_ref[...] = (rows.astype(F32) * gain_ref[...]).astype(BF)


def rows_specs(steps, shape):
    half = steps // 2
    return [
        pl.BlockSpec(shape, lambda i, _: (jnp.minimum(i, half - 1), 0)),
        pl.BlockSpec(shape, lambda i, _: (jnp.maximum(i - half, 0), 0)),
    ]


def flat_rows(rows):
    return [part.reshape(-1, part.shape[-1]) for part in rows]


def project(ids, rows, gain, cosine, sine, weights):
    slots, (length, width) = 2 * rows[0].shape[0], rows[0].shape[1:]
    nr, nh = weights[0].shape[0], len(weights)
    tile, steps = BLOCKS * length, slots // BLOCKS
    return call(
        functools.partial(qkv_kernel, nr, nh),
        (steps,),
        ids,
        [*flat_rows(rows), gain, cosine, sine, *weights],
        [
            *rows_specs(steps, (tile, width)),
            whole_spec(gain.shape),
            pl.BlockSpec((tile, LANES), lambda i, _: (i, 0)),
            pl.BlockSpec((tile, LANES), lambda i, _: (i, 0)),
            *[whole_spec(w.shape) for w in weights],
        ],
        [
            jax.ShapeDtypeStruct((length, H * HD), BF),
            jax.ShapeDtypeStruct((slots * length, KVH * HD), BF),
            jax.ShapeDtypeStruct((slots * length, KVH * HD), BF),
        ],
        [
            whole_spec((length, H * HD)),
            pl.BlockSpec((tile, KVH * HD), lambda i, _: (i, 0)),
            pl.BlockSpec((tile, KVH * HD), lambda i, _: (i, 0)),
        ],
        [pltpu.VMEM((tile, width), BF)],
    )


def to_half(tile, which, wanted):
    if which != wanted:
        tile = pltpu.roll(tile, HD, 1)
    return jnp.where(lane_ids(tile.shape[0]) // HD == wanted, tile, 0.0)


def attend_kernel(ids, q_ref, k_ref, v_ref, kx_ref, qx_ref, o_ref, low_ref, lse_ref):
    keys = jnp.concatenate([k_ref[...], kx_ref[...]], axis=1)
    values = v_ref[...]
    extra = qx_ref[...]
    rows = q_ref.shape[0]
    lanes = lane_ids(rows)
    sums = jnp.zeros((rows, LANES), F32)
    for t in range(2):
        tile = q_ref[:, t * LANES : (t + 1) * LANES].astype(F32)
        mixed = jnp.zeros((rows, LANES), F32)
        for w in range(2):
            query = jnp.concatenate([to_half(tile, w, t).astype(BF), extra], axis=1)
            scores = dot_nt(query, keys)
            highest = jnp.max(scores, axis=1, keepdims=True)
            weights = jnp.exp(scores - highest)
            total = jnp.sum(weights, axis=1, keepdims=True)
            out = dot(weights.astype(BF), values) / total
            mixed = mixed + to_half(out, t, w)
            sums = jnp.where(lanes == 2 * t + w, highest + jnp.log(total), sums)
        o_ref[:, t * LANES : (t + 1) * LANES] = mixed
        low_ref[:, t * LANES : (t + 1) * LANES] = mixed.astype(BF)
    lse_ref[0] = sums


def attend(ids, q, k, v, key_extra, query_extra):
    length, keys = q.shape[0], k.shape[0]
    quad = pl.BlockSpec((length, 2 * LANES), lambda p, _: (0, p))
    pair = pl.BlockSpec((keys, LANES), lambda p, _: (0, p))
    return call(
        attend_kernel,
        (PAIRS,),
        ids,
        [q, k, v, key_extra, query_extra],
        [quad, pair, pair, whole_spec(key_extra.shape), whole_spec(query_extra.shape)],
        [
            jax.ShapeDtypeStruct((length, H * HD), F32),
            jax.ShapeDtypeStruct((length, H * HD), BF),
            jax.ShapeDtypeStruct((PAIRS, length, LANES), F32),
        ],
        [quad, quad, pl.BlockSpec((1, length, LANES), lambda p, _: (p, 0, 0))],
    )


def three_parts(value):
    high = value.astype(BF)
    rest = value - high.astype(F32)
    middle = rest.astype(BF)
    return high.astype(F32), middle.astype(F32), (rest - middle.astype(F32))


def with_parts(base, value, lanes):
    high, middle, low = three_parts(value)
    base = jnp.where(lanes == 16, high, base)
    base = jnp.where(lanes == 17, middle, base)
    return jnp.where(lanes == 18, low, base).astype(BF)


def attend_back_kernel(
    span_rows, ids, q_ref, do_ref, o_ref, lse_ref, k_ref, v_ref, kx_ref, qx_ref, cos_ref, sin_ref,
    dq_ref, own_ref, other_ref, sum_ref,
):
    rows = q_ref.shape[0]
    lanes = lane_ids(rows)
    extra = qx_ref[...].astype(F32)
    nothing = jnp.zeros((rows, LANES), F32)
    sums = lse_ref[0]
    queries, outs, pads_q, pads_o = [], [], [], []
    for t in range(2):
        at = slice(t * LANES, (t + 1) * LANES)
        tile, grad = q_ref[:, at].astype(F32), do_ref[:, at].astype(F32)
        product = grad * o_ref[:, at]
        for w in range(2):
            here = lanes // HD == w
            delta = jnp.sum(jnp.where(here, product, 0.0), axis=1, keepdims=True)
            log_sum = jnp.sum(jnp.where(lanes == 2 * t + w, sums, 0.0), axis=1, keepdims=True)
            q_pad = to_half(tile, w, t).astype(BF)
            o_pad = to_half(grad, w, t).astype(BF)
            queries.append(jnp.concatenate([q_pad, with_parts(extra, -log_sum, lanes)], axis=1))
            outs.append(jnp.concatenate([o_pad, with_parts(nothing, -delta, lanes)], axis=1))
            pads_q.append(q_pad)
            pads_o.append(o_pad)
    all_q = jnp.concatenate(pads_q, axis=0)
    every_q = jnp.concatenate(queries, axis=0)
    every_o = jnp.concatenate(outs, axis=0)
    all_o = jnp.concatenate(pads_o, axis=0)
    sum_ref[...] = jnp.zeros_like(sum_ref)

    spans = k_ref.shape[0] // 2 // span_rows

    def one_span(i, _, part, out_ref):
        put = pl.ds(pl.multiple_of(i * span_rows, span_rows), span_rows)
        first = part * spans * span_rows
        at = pl.ds(pl.multiple_of(first + i * span_rows, span_rows), span_rows)
        k_here, x_here = k_ref[at, :], kx_ref[at, :]
        keys = jnp.concatenate([k_here, x_here], axis=1)
        values = jnp.concatenate([v_ref[at, :], x_here], axis=1)
        probs = jnp.exp(dot_nt(keys, every_q))
        d_scores = (probs * dot_nt(values, every_o)).astype(BF)
        sum_ref[...] += dot_tn(k_here, d_scores)
        out_ref[1, put, :] = dot(probs.astype(BF), all_o).astype(BF)
        d_key = dot(d_scores, all_q)
        d_key = turn(d_key, cos_ref[at, :], sin_ref[at, :], -1.0)
        out_ref[0, put, :] = d_key.astype(BF)
        return 0

    for part, out_ref in enumerate((own_ref, other_ref)):
        lax.fori_loop(0, spans, functools.partial(one_span, part=part, out_ref=out_ref), 0)
    cosine, sine = cos_ref[:rows, :], sin_ref[:rows, :]
    for t in range(2):
        d_query = [sum_ref[:, n * rows : (n + 1) * rows].T for n in (2 * t, 2 * t + 1)]
        tile = to_half(d_query[0], t, 0) + to_half(d_query[1], t, 1)
        turned = turn(tile * HD**-0.5, cosine, sine, -1.0)
        dq_ref[:, t * LANES : (t + 1) * LANES] = turned.astype(BF)


def attend_back_part(*refs):
    attend_back_kernel(1024, *refs[:11], *refs[14:])


def attend_back(ids, q, d_out, out, lse, k, v, key_extra, query_extra, cosine, sine, half=None, done=None):
    length, keys = q.shape[0], k.shape[0]
    count = PAIRS if half is None else PAIRS // 2

    def at(p, ids):
        return p if half is None else (ids[2] ^ half) * count + p

    quad = pl.BlockSpec((length, 2 * LANES), lambda p, ids: (0, at(p, ids)))
    pair = pl.BlockSpec((keys, LANES), lambda p, ids: (0, at(p, ids)))
    ins = [q, d_out, out, lse, k, v, key_extra, query_extra, cosine, sine]
    specs = [
        quad,
        quad,
        quad,
        pl.BlockSpec((1, length, LANES), lambda p, ids: (at(p, ids), 0, 0)),
        pair,
        pair,
        whole_spec(key_extra.shape),
        whole_spec(query_extra.shape),
        whole_spec(cosine.shape),
        whole_spec(sine.shape),
    ]
    if done is not None:
        ins += done
        specs += [pl.BlockSpec(memory_space=pl.ANY)] * 3
    return call(
        attend_back_part if done is not None else functools.partial(attend_back_kernel, 1024),
        (count,),
        ids,
        ins,
        specs,
        [
            jax.ShapeDtypeStruct((length, H * HD), BF),
            jax.ShapeDtypeStruct((2, keys // 2, KVH * HD), BF),
            jax.ShapeDtypeStruct((2, keys // 2, KVH * HD), BF),
        ],
        [quad] + [pl.BlockSpec((2, keys // 2, LANES), lambda p, ids: (0, 0, at(p, ids)))] * 2,
        [pltpu.VMEM((LANES, 4 * length), F32)],
        aliases={11: 0, 12: 1, 13: 2} if done is not None else None,
    )


def out_kernel(nr, nh, ids, x_ref, o_ref, gain_ref, *rest):
    weights = rest[:nh]
    x2_ref, n2_ref = rest[nh:]
    width = x_ref.shape[1]
    chunk, cols = H * HD // nr, width // nh
    for h in range(nh):
        at = span(half_chunk(ids, h, nh), cols)
        total = x_ref[:, at]
        for r in range(nr):
            total = total + dot(
                o_ref[:, span(row_chunk(ids, r, nr), chunk)], weights[h][r]
            )
        x2_ref[:, at] = total
    middle = x2_ref[...]
    inverse = lax.rsqrt(jnp.mean(middle * middle, axis=1, keepdims=True) + EPSILON)
    n2_ref[...] = (middle * inverse * gain_ref[...]).astype(BF)


def out_spec(weight, cols):
    return pl.BlockSpec(weight.shape[:2] + (cols,), lambda *_: (0, 0, 0))


def project_out(ids, x, low, gain, weights):
    nr, nh = weights[0].shape[0], len(weights)
    ins = [x, low, gain, *weights]
    outs = [jax.ShapeDtypeStruct(x.shape, F32), jax.ShapeDtypeStruct(x.shape, BF)]
    return call(
        functools.partial(out_kernel, nr, nh),
        (1,),
        ids,
        ins,
        [whole_spec(i.shape) for i in ins[:3]] + [out_spec(w, x.shape[1] // nh) for w in weights],
        outs,
        [whole_spec(o.shape) for o in outs],
    )


def out_back_kernel(nr, nh, ids, c_ref, x2_ref, gain_ref, dn2_ref, low_ref, *rest):
    weights = rest[:nh]
    dx2_ref, do_ref = rest[nh : nh + 2]
    grads = rest[nh + 2 : 2 * nh + 2]
    dr_ref, term_ref = rest[2 * nh + 2 :]
    width = c_ref.shape[1]
    chunk, cols = H * HD // nr, width // nh
    middle, d_normed = x2_ref[...], dn2_ref[...]
    inverse = lax.rsqrt(jnp.mean(middle * middle, axis=1, keepdims=True) + EPSILON)
    scaled = d_normed * gain_ref[...]
    inner = jnp.mean(scaled * middle, axis=1, keepdims=True)
    d_middle = c_ref[...] + inverse * scaled - middle * (inverse * inverse * inverse * inner)
    dx2_ref[...] = d_middle
    dr_ref[...] = d_middle.astype(BF)
    term_ref[...] = d_normed * middle * inverse
    fold = width // cols
    rows = chunk // fold
    for r in range(nr):
        at = span(row_chunk(ids, r, nr), chunk)
        low = low_ref[:, at]
        gain_grad = jnp.sum(term_ref[:, at], axis=0, keepdims=True)
        gain_grad = jnp.concatenate([gain_grad] * (width // chunk), axis=1)
        total = None
        for h in range(nh):
            branch = dr_ref[:, span(half_chunk(ids, h, nh), cols)]
            part = dot_nt(branch, weights[h][r])
            total = part if total is None else total + part
            grad = dot_tn(low, branch).astype(BF)
            for f in range(fold):
                grads[h][r, :rows, f * cols : (f + 1) * cols] = grad[f * rows : (f + 1) * rows]
            grads[h][r, rows:] = jnp.broadcast_to(gain_grad, (GATE_ROWS, width)).astype(BF)
        do_ref[:, at] = total.astype(BF)


def project_out_back(ids, c, x2, gain, dn2, low, weights):
    nr, nh = weights[0].shape[0], len(weights)
    ins = [c, x2, gain, dn2, low, *weights]
    rows, cols = H * HD // nr, c.shape[1] // nh
    outs = [jax.ShapeDtypeStruct(c.shape, F32), jax.ShapeDtypeStruct((c.shape[0], H * HD), BF)]
    high = rows * cols // c.shape[1] + GATE_ROWS
    outs += [jax.ShapeDtypeStruct((nr, high, c.shape[1]), BF)] * nh
    got = call(
        functools.partial(out_back_kernel, nr, nh),
        (1,),
        ids,
        ins,
        [whole_spec(i.shape) for i in ins[:5]] + [out_spec(w, cols) for w in weights],
        outs,
        [whole_spec(o.shape) for o in outs],
        [pltpu.VMEM(c.shape, BF), pltpu.VMEM(c.shape, F32)],
    )
    return got[0], got[1], got[2:]


def picks(slot_ref, experts):
    tokens = slot_ref.shape[-1]
    places = lax.broadcasted_iota(jnp.int32, (CAP, tokens), 0).astype(F32)
    rows = [places == slot_ref[0, j : j + 1, :] for j in range(experts)]
    return rows[0] if experts == 1 else jnp.concatenate(rows, axis=0)


def gather_kernel(groups, per, experts, with_gates, ids, slot_ref, *rest):
    if with_gates:
        gate_ref, rest = rest[0], rest[1:]
    tokens, out_ref = rest[:groups], rest[groups]
    chosen = picks(slot_ref, experts)
    low = chosen.astype(F32).astype(BF)
    for g in range(groups):

        @pl.when(pl.program_id(0) // per == g)
        def _(g=g):
            rows = dot(low, tokens[g][0, : slot_ref.shape[-1]]).astype(BF)
            for j in range(experts):
                out_ref[j, 0] = rows[j * CAP : (j + 1) * CAP]

    if with_gates:
        for j in range(experts):
            mine = chosen[j * CAP : (j + 1) * CAP]
            gates = jnp.sum(jnp.where(mine, gate_ref[0, j : j + 1, :], 0.0), axis=1, keepdims=True)
            rest[groups + 1][j, 0] = jnp.broadcast_to(gates, (CAP, LANES))


def gather_rows(ids, slots, groups, gates=None):
    blocks, experts, length = slots.shape
    per, width = groups[0].shape[0], groups[0].shape[-1]
    ins, specs = [slots], [pl.BlockSpec((1, experts, length), lambda i, _: (i, 0, 0))]
    if gates is not None:
        ins.append(gates)
        specs.append(specs[0])
    for g, tokens in enumerate(groups):
        ins.append(tokens)
        specs.append(
            pl.BlockSpec(
                (1,) + tokens.shape[1:], lambda i, _, g=g: (jnp.clip(i - g * per, 0, per - 1), 0, 0)
            )
        )
    outs = [jax.ShapeDtypeStruct((experts, blocks, CAP, width), BF)]
    out_specs = [pl.BlockSpec((experts, 1, CAP, width), lambda i, _: (0, i, 0, 0))]
    if gates is not None:
        outs.append(jax.ShapeDtypeStruct((experts, blocks, CAP, LANES), F32))
        out_specs.append(pl.BlockSpec((experts, 1, CAP, LANES), lambda i, _: (0, i, 0, 0)))
    return call(
        functools.partial(gather_kernel, len(groups), per, experts, gates is not None),
        (blocks,),
        ids,
        ins,
        specs,
        outs,
        out_specs,
    )


def expert_kernel(nz, ids, x_ref, c_ref, gate_ref, *rest):
    weights, rest = rest[:nz], rest[nz:]
    y_ref, dx_ref, gg_ref = rest[:3]
    grads, acc_ref = rest[3 : 3 + nz], rest[3 + nz]
    chunk = x_ref.shape[-1] // nz
    step, last = pl.program_id(1), pl.num_programs(1) - 1
    a = b = ch = None
    for r in range(nz):
        at = span(z_chunk(ids, r, nz), chunk)
        x, c = x_ref[0, :, at], c_ref[0, :, at]
        parts = (
            dot(x, weights[r][0, 0]),
            dot(x, weights[r][0, 1]),
            dot(c, weights[r][0, 2]),
        )
        a, b, ch = parts if a is None else (a + parts[0], b + parts[1], ch + parts[2])
    gate = gate_ref[0][:, :1]
    sig = 1.0 / (1.0 + jnp.exp(-a))
    act = a * sig
    hidden = (act * b).astype(BF).astype(F32)
    gg_ref[0] = jnp.broadcast_to(jnp.sum(hidden * ch, axis=1, keepdims=True), gg_ref.shape[1:])
    hg = (hidden * gate).astype(BF)
    dh = ch * gate
    da = (dh * b * sig * (1.0 + a * (1.0 - sig))).astype(BF)
    db = (dh * act).astype(BF)

    @pl.when(step == 0)
    def _():
        acc_ref[...] = jnp.zeros_like(acc_ref)

    for r in range(nz):
        at = span(z_chunk(ids, r, nz), chunk)
        x, c = x_ref[0, :, at], c_ref[0, :, at]
        y_ref[0, :, at] = dot_nt(hg, weights[r][0, 2]).astype(BF)
        dx_ref[0, :, at] = (dot_nt(da, weights[r][0, 0]) + dot_nt(db, weights[r][0, 1])).astype(BF)
        acc_ref[r, 0] += dot_tn(x, da)
        acc_ref[r, 1] += dot_tn(x, db)
        acc_ref[r, 2] += dot_tn(c, hg)

    @pl.when(step == last)
    def _():
        for r in range(nz):
            grads[r][0] = acc_ref[r].astype(BF)


def run_experts(ids, x_rows, c_rows, gate_rows, weights):
    experts, rows, width = x_rows.shape
    nz = len(weights)
    hidden = weights[0].shape[-1]
    tile = 256
    block = pl.BlockSpec((1, tile, width), lambda j, i, _: (j, i, 0))
    narrow = pl.BlockSpec((1, tile, LANES), lambda j, i, _: (j, i, 0))
    matrix = pl.BlockSpec((1,) + weights[0].shape[1:], lambda j, i, _: (j, 0, 0, 0))
    got = call(
        functools.partial(expert_kernel, nz),
        (experts, rows // tile),
        ids,
        [x_rows, c_rows, gate_rows, *weights],
        [block, block, narrow] + [matrix] * nz,
        [
            jax.ShapeDtypeStruct(x_rows.shape, BF),
            jax.ShapeDtypeStruct(x_rows.shape, BF),
            jax.ShapeDtypeStruct((experts, rows, LANES), F32),
        ]
        + [jax.ShapeDtypeStruct(w.shape, BF) for w in weights],
        [block, block, narrow] + [matrix] * nz,
        [pltpu.VMEM((nz,) + weights[0].shape[1:], F32)],
    )
    return got[0], got[1], got[2], got[3:]


def spread_kernel(groups, per, experts, with_grads, ids, slot_ref, rows_ref, *rest):
    if with_grads:
        grad_ref, rest = rest[0], rest[1:]
    chosen = picks(slot_ref, experts)
    low = chosen.astype(F32).astype(BF)
    rows = [rows_ref[j, 0] for j in range(experts)]
    rows = rows[0] if experts == 1 else jnp.concatenate(rows, axis=0)
    total = dot_tn(low, rows).astype(BF)
    length, width = total.shape
    tail = None
    if with_grads:
        fit = width // length
        line = lax.broadcasted_iota(jnp.int32, (GATE_ROWS, width), 0)
        place = lax.broadcasted_iota(jnp.int32, (GATE_ROWS, width), 1) // length
        tail = jnp.zeros((GATE_ROWS, width), F32)
        for j in range(experts):
            mine = chosen[j * CAP : (j + 1) * CAP]
            sums = jnp.sum(jnp.where(mine, grad_ref[j, 0][:, :1], 0.0), axis=0, keepdims=True)
            wide = jnp.concatenate([sums] * fit, axis=1)
            number = ids[3] + j
            tail = tail + jnp.where((line == number // fit) & (place == number % fit), wide, 0.0)
    for g in range(groups):

        @pl.when(pl.program_id(0) // per == g)
        def _(g=g):
            rest[g][0, :length] = total
            if with_grads:
                rest[g][0, length:] = tail.astype(BF)


def spread_rows(ids, slots, rows, groups, grads=None):
    blocks, experts, length = slots.shape
    per, width = blocks // groups, rows.shape[-1]
    high = length + (GATE_ROWS if grads is not None else 0)
    ins = [slots, rows]
    specs = [
        pl.BlockSpec((1, experts, length), lambda i, _: (i, 0, 0)),
        pl.BlockSpec((experts, 1, CAP, width), lambda i, _: (0, i, 0, 0)),
    ]
    if grads is not None:
        ins.append(grads)
        specs.append(pl.BlockSpec((experts, 1, CAP, LANES), lambda i, _: (0, i, 0, 0)))
    return call(
        functools.partial(spread_kernel, groups, per, experts, grads is not None),
        (blocks,),
        ids,
        ins,
        specs,
        [jax.ShapeDtypeStruct((per, high, width), BF)] * groups,
        [
            pl.BlockSpec(
                (1, high, width), lambda i, _, g=g: (jnp.clip(i - g * per, 0, per - 1), 0, 0)
            )
            for g in range(groups)
        ],
    )


def mixture_kernel(nz, w_parts, groups, per, experts, tile, ids, slot_ref, gate_ref, *rest):
    n2_in, rest = rest[:groups], rest[groups:]
    c_in, rest = rest[:groups], rest[groups:]
    w_in, rest = rest[: len(w_parts)], rest[len(w_parts) :]
    dn2_out, rest = rest[:groups], rest[groups:]
    y_out, rest = rest[: groups // 2], rest[groups // 2 :]
    dw_out, rest = rest[:nz], rest[nz:]
    n2_ref, c_ref, w_ref, x_rows, c_rows, gate_rows, grad_rows, inner_ref, dw_ref = rest[:9]
    n2_sem, c_sem, w_sem, dn2_sem, y_sem, dw_sem = rest[9:]
    length = slot_ref.shape[-1]
    width = n2_ref.shape[-1]
    chunk = width // nz
    blocks = groups * per

    def n2_copy(g):
        return pltpu.make_async_copy(n2_in[g], n2_ref.at[pl.ds(g * per, per)], n2_sem.at[g])

    def c_copy(g):
        return pltpu.make_async_copy(c_in[g], c_ref.at[pl.ds(g * per, per)], c_sem.at[g])

    def w_copy(n):
        r, first, count = w_parts[n]
        to = w_ref.at[:, pl.ds(first, count), span(z_chunk(ids, r, nz), chunk)]
        return pltpu.make_async_copy(w_in[n], to, w_sem.at[n])

    for g in range(groups):
        c_copy(g).start()
        n2_copy(g).start()
    for n in range(len(w_parts)):
        w_copy(n).start()

    def chosen_rows(i):
        places = lax.broadcasted_iota(jnp.int32, (CAP, length), 0).astype(F32)
        return [places == slot_ref[i, j : j + 1, :] for j in range(experts)]

    def one_hot(chosen):
        chosen = [jnp.where(c, 1.0, 0.0).astype(BF) for c in chosen]
        return chosen[0] if experts == 1 else jnp.concatenate(chosen, axis=0)

    def gather(i, _):
        chosen = chosen_rows(i)
        low = one_hot(chosen)
        at = pl.ds(pl.multiple_of(i * CAP, CAP), CAP)
        got_x = dot(low, n2_ref[i]).astype(BF)
        got_c = dot(low, c_ref[i, :length]).astype(BF)
        for j in range(experts):
            x_rows[j, at] = got_x[j * CAP : (j + 1) * CAP]
            c_rows[j, at] = got_c[j * CAP : (j + 1) * CAP]
            gates = jnp.where(chosen[j], gate_ref[i, j : j + 1, :], 0.0)
            gate_rows[j, at] = jnp.broadcast_to(jnp.sum(gates, axis=1, keepdims=True), (CAP, LANES))
        return 0

    for g in range(groups):
        c_copy(g).wait()
        n2_copy(g).wait()
        lax.fori_loop(g * per, (g + 1) * per, gather, 0)
    for n in range(len(w_parts)):
        w_copy(n).wait()

    def dw_copy(j, r):
        rows = span(z_chunk(ids, r, nz), chunk)
        return pltpu.make_async_copy(dw_ref.at[j, :, rows], dw_out[r].at[j], dw_sem.at[j, r])

    for j in range(experts):

        def one_tile(i, _, j=j):
            at = pl.ds(pl.multiple_of(i * tile, tile), tile)
            x, c = x_rows[j, at], c_rows[j, at]
            a, b, ch = dot(x, w_ref[j, 0]), dot(x, w_ref[j, 1]), dot(c, w_ref[j, 2])
            gate = gate_rows[j, at][:, :1]
            sig = 1.0 / (1.0 + jnp.exp(-a))
            act = a * sig
            hidden = (act * b).astype(BF).astype(F32)
            grad = jnp.sum(hidden * ch, axis=1, keepdims=True)
            grad_rows[j, at] = jnp.broadcast_to(grad, (tile, LANES))
            hg = (hidden * gate).astype(BF)
            dh = ch * gate
            da = (dh * b * sig * (1.0 + a * (1.0 - sig))).astype(BF)
            db = (dh * act).astype(BF)
            inner_ref[0, at], inner_ref[1, at], inner_ref[2, at] = da, db, hg
            return 0

        lax.fori_loop(0, blocks * CAP // tile, one_tile, 0)
        for part in range(width // chunk):
            cols = slice(part * chunk, (part + 1) * chunk)
            for k in range(3):
                x = (c_rows if k == 2 else x_rows)[j, :, cols]
                dw_ref[j, k, cols] = dot_tn(x, inner_ref[k]).astype(BF)
        for r in range(nz):
            dw_copy(j, r).start()

        def back_tile(i, _, j=j):
            at = pl.ds(pl.multiple_of(i * tile, tile), tile)
            da, db, hg = inner_ref[0, at], inner_ref[1, at], inner_ref[2, at]
            c_rows[j, at] = dot_nt(hg, w_ref[j, 2]).astype(BF)
            x_rows[j, at] = (dot_nt(da, w_ref[j, 0]) + dot_nt(db, w_ref[j, 1])).astype(BF)
            return 0

        lax.fori_loop(0, blocks * CAP // tile, back_tile, 0)

    fit = width // length
    line = lax.broadcasted_iota(jnp.int32, (GATE_ROWS, width), 0)
    place = lax.broadcasted_iota(jnp.int32, (GATE_ROWS, width), 1) // length

    def spread(i, _):
        chosen = chosen_rows(i)
        low = one_hot(chosen)
        at = pl.ds(pl.multiple_of(i * CAP, CAP), CAP)
        both = []
        for rows_ref in (x_rows, c_rows):
            rows = [rows_ref[j, at] for j in range(experts)]
            both.append(rows[0] if experts == 1 else jnp.concatenate(rows, axis=0))
        n2_ref[i] = dot_tn(low, both[0]).astype(BF)
        c_ref[i, :length] = dot_tn(low, both[1]).astype(BF)
        tail = jnp.zeros((GATE_ROWS, width), F32)
        for j in range(experts):
            sums = jnp.where(chosen[j], grad_rows[j, at][:, :1], 0.0)
            wide = jnp.concatenate([jnp.sum(sums, axis=0, keepdims=True)] * fit, axis=1)
            number = ids[3] + j
            tail = tail + jnp.where((line == number // fit) & (place == number % fit), wide, 0.0)
        c_ref[i, length:] = tail.astype(BF)
        return 0

    def dn2_copy(g):
        return pltpu.make_async_copy(n2_ref.at[pl.ds(g * per, per)], dn2_out[g], dn2_sem.at[g])

    def y_copy(g):
        here = pl.ds((g % (groups // 2)) * per, per)
        return pltpu.make_async_copy(
            c_ref.at[pl.ds(g * per, per)], y_out[g // (groups // 2)].at[here], y_sem.at[g]
        )

    for g in range(groups):
        lax.fori_loop(g * per, (g + 1) * per, spread, 0)
        dn2_copy(g).start()
        y_copy(g).start()
    for g in range(groups):
        dn2_copy(g).wait()
        y_copy(g).wait()
    for j in range(experts):
        for r in range(nz):
            dw_copy(j, r).wait()


def mixture(ids, slots, gates, n2_groups, c_groups, weights):
    groups, nz = len(n2_groups), len(weights)
    per, length, width = n2_groups[0].shape
    blocks, experts, _ = slots.shape
    high, rows = c_groups[0].shape[1], blocks * CAP
    flat = [w for row in weights for w in row]
    w_parts = []
    for r, row in enumerate(weights):
        first = 0
        for w in row:
            w_parts.append((r, first, w.shape[1]))
            first += w.shape[1]
    part = flat[0].shape
    matrices = (part[0], 3) + part[2:]
    anywhere = pl.BlockSpec(memory_space=pl.ANY)
    outs = [jax.ShapeDtypeStruct((per, length, width), BF)] * groups
    outs += [jax.ShapeDtypeStruct((groups // 2 * per, high, width), BF)] * 2
    outs += [jax.ShapeDtypeStruct(matrices, BF)] * nz
    got = call(
        functools.partial(mixture_kernel, nz, tuple(w_parts), groups, per, experts, 256),
        (1,),
        ids,
        [slots, gates, *n2_groups, *c_groups, *flat],
        [whole_spec(slots.shape), whole_spec(gates.shape)] + [anywhere] * (2 * groups + len(flat)),
        outs,
        [anywhere] * len(outs),
        [
            pltpu.VMEM((blocks, length, width), BF),
            pltpu.VMEM((blocks, high, width), BF),
            pltpu.VMEM(matrices[:2] + (width,) + matrices[3:], BF),
            pltpu.VMEM((experts, rows, width), BF),
            pltpu.VMEM((experts, rows, width), BF),
            pltpu.VMEM((experts, rows, LANES), F32),
            pltpu.VMEM((experts, rows, LANES), F32),
            pltpu.VMEM((3, rows, part[-1]), BF),
            pltpu.VMEM(matrices[:2] + (width,) + matrices[3:], BF),
            pltpu.SemaphoreType.DMA((groups,)),
            pltpu.SemaphoreType.DMA((groups,)),
            pltpu.SemaphoreType.DMA((len(flat),)),
            pltpu.SemaphoreType.DMA((groups,)),
            pltpu.SemaphoreType.DMA((groups,)),
            pltpu.SemaphoreType.DMA((experts, nz)),
        ],
    )
    return got[:groups], got[groups : groups + 2], got[groups + 2 :]


def half_grads_kernel(nr, ids, own_rows, other_rows, gain_ref, dq_ref, own_ref, other_ref, grad_ref, normed_ref, acc_ref):
    chunk, qn, kn = grad_ref.shape[1], dq_ref.shape[1], own_ref.shape[2]
    step, count = pl.program_id(0), pl.num_programs(0)
    normalize(own_rows, other_rows, gain_ref, normed_ref)

    @pl.when(step == 0)
    def _():
        for r in range(nr):
            x = normed_ref[:, span(row_chunk(ids, r, nr), chunk)]
            grad_ref[r, :, :qn] = dot_tn(x[: dq_ref.shape[0]], dq_ref[...]).astype(BF)
        acc_ref[...] = jnp.zeros_like(acc_ref)

    def add(dkv_ref):
        grad = jnp.concatenate([dkv_ref[0], dkv_ref[1]], axis=1)
        for r in range(nr):
            acc_ref[r] += dot_tn(normed_ref[:, span(row_chunk(ids, r, nr), chunk)], grad)

    pl.when(step < count // 2)(lambda: add(own_ref))
    pl.when(step >= count // 2)(lambda: add(other_ref))

    @pl.when(step == count - 1)
    def _():
        for r in range(nr):
            grad_ref[r, :, qn:] = acc_ref[r].astype(BF)


def half_grads(ids, rows, gain, dq, dkv, half, nr, nh):
    slots, (length, width) = 2 * rows[0].shape[0], rows[0].shape[1:]
    qn, kn = H * HD // nh, KVH * HD // nh

    def body(ids, own_rows, other_rows, gain_ref, dq_ref, own_ref, other_ref, grad_ref, normed_ref, acc_ref):
        half_grads_kernel(
            nr, ids, own_rows, other_rows, gain_ref, dq_ref, own_ref, other_ref, grad_ref, normed_ref, acc_ref
        )

    def at(ids):
        return half_chunk(ids, half, nh)

    out = jax.ShapeDtypeStruct((nr, width // nr, qn + 2 * kn), BF)
    tile, steps = BLOCKS * length, slots // BLOCKS
    middle = steps // 2
    return call(
        body,
        (steps,),
        ids,
        [*flat_rows(rows), gain, dq, *dkv],
        [
            *rows_specs(steps, (tile, width)),
            whole_spec(gain.shape),
            pl.BlockSpec((length, qn), lambda i, ids: (0, at(ids))),
            pl.BlockSpec((2, tile, kn), lambda i, ids: (0, jnp.minimum(i, middle - 1), at(ids))),
            pl.BlockSpec((2, tile, kn), lambda i, ids: (0, jnp.maximum(i - middle, 0), at(ids))),
        ],
        out,
        whole_spec(out.shape),
        [pltpu.VMEM((tile, width), BF), pltpu.VMEM((nr, width // nr, 2 * kn), F32)],
    )


def rows_back_kernel(nr, nh, ids, dq_ref, dkv_ref, x_ref, dx2_ref, gain_ref, *rest):
    weights = rest[:nh]
    out_ref, grad_ref, low_ref = rest[nh:]
    width = x_ref.shape[1]
    chunk = width // nr
    qn, kn = H * HD // nh, KVH * HD // nh
    at_q, at_k, at_v, at_end = columns(nh, width)
    low_ref[...] = dkv_ref[...].astype(BF)
    for r in range(nr):
        total = None
        for h in range(nh):
            at = half_chunk(ids, h, nh)
            weight = weights[h]
            part = dot_nt(dq_ref[:, span(at, qn)], weight[r, :, at_q:at_k])
            part = part + dot_nt(low_ref[0, :, span(at, kn)], weight[r, :, at_k:at_v])
            part = part + dot_nt(low_ref[1, :, span(at, kn)], weight[r, :, at_v:at_end])
            total = part if total is None else total + part
        grad_ref[:, span(row_chunk(ids, r, nr), chunk)] = total
    x = x_ref[...]
    scaled = grad_ref[...] * gain_ref[...]
    inverse = lax.rsqrt(jnp.mean(x * x, axis=1, keepdims=True) + EPSILON)
    inner = jnp.mean(scaled * x, axis=1, keepdims=True)
    out_ref[...] = dx2_ref[...] + inverse * scaled - x * (inverse * inverse * inverse * inner)


def rows_back(ids, dq, dkv, x, dx2, gain, weights):
    nr, nh = weights[0].shape[0], len(weights)
    ins = [dq, dkv, x, dx2, gain, *weights]
    return call(
        functools.partial(rows_back_kernel, nr, nh),
        (1,),
        ids,
        ins,
        [whole_spec(i.shape) for i in ins],
        jax.ShapeDtypeStruct(x.shape, F32),
        whole_spec(x.shape),
        [pltpu.VMEM(x.shape, F32), pltpu.VMEM(dkv.shape, BF)],
    )


def swap(value, axis, distance):
    count = lax.axis_size(axis)
    return lax.ppermute(value, axis, [(i, i ^ distance) for i in range(count)])


def after(value, *done):
    return lax.optimization_barrier((value,) + done)[0]


def together(*values):
    return lax.optimization_barrier(values)


def pick(array, index):
    return lax.dynamic_index_in_dim(array, index, 0, keepdims=False)


def gather_z(value):
    chips = lax.axis_size("shard") // 2
    if chips != 4:
        return [value] + [swap(value, "shard", 2 * r) for r in range(1, chips)]
    near, far = swap(value, "shard", 2), swap(value, "shard", 4)
    return [value, near, far, swap(far, "shard", 2)]


def scatter_z(parts):
    total = parts[0].astype(F32)
    for r in range(1, len(parts)):
        total = total + swap(parts[r], "shard", 2 * r).astype(F32)
    return total


def in_order(mine, other, core, axis):
    return jnp.where(
        core == 0,
        jnp.concatenate([mine, other], axis=axis),
        jnp.concatenate([other, mine], axis=axis),
    )


def add_low(*values):
    total = values[0].astype(F32)
    for value in values[1:]:
        total = total + value.astype(F32)
    return total.astype(BF)


def body(
    tokens,
    block_ids,
    routes,
    gates,
    attn_gain,
    w_query,
    w_key,
    w_value,
    w_out,
    moe_gain,
    w_gate,
    w_up,
    w_down,
    cotangent,
):
    length, width = tokens.shape[1], tokens.shape[2]
    n_expert, n_shard = lax.axis_size("expert"), lax.axis_size("shard")
    chips = n_shard // 2
    local = w_gate.shape[0]
    fast = n_expert == 4 and n_shard == 8 and local % 4 == 0
    sides = 2 if fast else 1
    experts = local // (2 * sides)
    e, s = lax.axis_index("expert"), lax.axis_index("shard")
    z, core = s // 2, s % 2
    side = z // 2 if fast else 0
    first_expert = e * local + core * (local // 2) + side * experts
    ids = jnp.stack([e, z, core, first_expert]).astype(jnp.int32)
    nh = 2 if fast else 1

    x = tokens[0]
    c = cotangent[0]

    inverse_one = lax.rsqrt(jnp.mean(x * x, axis=-1, keepdims=True) + EPSILON)
    scaled_rows = (x * inverse_one).astype(BF)

    def halves(matrix):
        low = matrix.astype(BF)
        return low.reshape(low.shape[0], nh, low.shape[1] // nh).transpose(1, 0, 2)

    def column(gain):
        return jnp.broadcast_to(gain.astype(BF)[None, :, None], (nh, gain.shape[0], LANES // 2))

    packed = jnp.concatenate(
        [halves(w_out), halves(w_query), halves(w_key), halves(w_value), column(attn_gain), column(moe_gain)],
        axis=2,
    )
    at_q, at_k, at_v, at_end = columns(nh, width)

    numbers = jnp.arange(EXPERTS, dtype=jnp.int32)
    lines = EXPERTS * length // width

    def positions(start):
        s_late = after(s, start)
        owners = jnp.stack([s_late ^ (2 * r + k) for k in range(2) for r in range(chips)])
        places = (owners[:, None] * length + jnp.arange(length)[None, :]).reshape(n_shard * length)
        freqs = 10000.0 ** (-(jnp.arange(HD // 2, dtype=F32) * 2.0 / HD))
        angles = places.astype(F32)[:, None] * freqs[None, :]
        cosine, sine = jnp.cos(angles), jnp.sin(angles)
        cosine = jnp.concatenate([cosine] * 4, axis=1)
        sine = jnp.concatenate([-sine, sine] * 2, axis=1)
        every = block_ids[0].reshape(n_shard, length)
        key_blocks = jnp.concatenate(
            [pick(every, s_late ^ (2 * r + k)) for k in range(2) for r in range(chips)]
        )
        own_blocks = pick(every, s_late)
        lanes = jnp.arange(LANES, dtype=jnp.int32)[None, :]
        key_extra = ((lanes == key_blocks[:, None]) | ((lanes >= 16) & (lanes < 19))).astype(BF)
        query_extra = jnp.where((lanes < 16) & (lanes > own_blocks[:, None]), -1e30, 0.0).astype(BF)
        return cosine, sine, key_extra, query_extra

    def named_experts(routed):
        return routed[0][None, :, :] == numbers[:, None, None]

    def cotangent_rows(start):
        value, routed, gated = after((c, routes, gates), start)
        dense = jnp.sum(jnp.where(named_experts(routed), gated[0][None, :, :], 0.0), axis=-1)
        dense = dense.reshape(lines, width)
        high = dense.astype(BF)
        low = (dense - high.astype(F32)).astype(BF)
        return jnp.concatenate([value.astype(BF), high, low], axis=0)

    def own_experts(start):
        low = jnp.stack([m.astype(BF) for m in after((w_gate, w_up, w_down), start)], axis=1)
        low = low.reshape((2, local // 2) + low.shape[1:])
        return pick(low, core), swap(pick(low, 1 - core), "shard", 1)

    def over_columns(value):
        return [swap(value, "expert", r) for r in range(1, n_expert)]

    if fast:
        mine, other = pick(packed, core), pick(packed, 1 - core)
        chip = in_order(mine, swap(other, "shard", 1), core, 0)

    if fast:
        w_near, w_far = swap(chip, "shard", 2), swap(chip, "shard", 4)
        x_near = swap(scaled_rows, "shard", 2)
        x_far = swap(after(scaled_rows, w_far), "shard", 4)
        stacked = jnp.stack([chip, w_near, w_far, swap(w_far, "shard", 2)])
        block = jnp.concatenate([pick(stacked, z ^ i) for i in range(chips)], axis=0)
        c_pack = cotangent_rows(chip)
        w_mine, w_other = own_experts(chip)
        cosine, sine, key_extra, query_extra = positions(chip)
        w_got = over_columns(after(block, x_near, w_other))
        x_cross = swap(x_far, "shard", 2)
        c_far = swap(after(c_pack, x_far), "shard", 4)
        chip_w = in_order(after(w_mine, x_cross), w_other, core, 2)
        chip_w = chip_w.reshape((2, experts, 3, 2 * w_gate.shape[1], w_gate.shape[2]))
        here, there = pick(chip_w, side), pick(chip_w, 1 - side)
        there = [there[:, k : k + 1] for k in range(3)]
        own_core = jnp.stack([scaled_rows, x_near, x_far, x_cross])
        x_other = swap(own_core, "shard", 1)
        rows = [own_core, x_other]
        early = (own_core, c_far, cosine, sine, key_extra, query_extra)
        w_got = [after(got, *early) for got in w_got]
        blocks = jnp.stack([block] + w_got)
        attn_w = [blocks, swap(blocks, "shard", 1)]
        gain_cols = blocks[:, :, at_end:]
        gain_cols = jnp.concatenate([pick(gain_cols, e ^ i) for i in range(n_expert)], axis=0)
        near_a = swap(after(here[:, :1], blocks), "shard", 2)
        far_a = swap(after(there[0], blocks), "shard", 4)
        c_own_got = over_columns(after(c_pack, attn_w[1]))
    else:
        c_pack = cotangent_rows(packed)
        own_core = jnp.stack(gather_z(scaled_rows))
        rows = [own_core, swap(own_core, "shard", 1)]
        cosine, sine, key_extra, query_extra = positions(packed)
        blocks = lax.all_gather(packed[0], ("expert", "shard"), axis=0, tiled=True)
        attn_w = [blocks[None]]
        gain_cols = blocks[:, at_end:]
        expert_w = gather_z(in_order(*own_experts(packed), core, 2))
    gain_one = gain_cols[:, 0].astype(F32)[None]
    gain_two = gain_cols[:, LANES // 2].astype(F32)[None]
    nr = attn_w[0].shape[0]

    q, k, v = project(ids, rows, gain_one, cosine, sine, attn_w)
    if fast:
        c_far_got = over_columns(after(c_far, q))
        q, near_a, far_a, *c_own_got = together(q, near_a, far_a, *c_own_got)
        near_b = swap(after(here[:, 1:], q), "shard", 2)
        far_b = swap(after(there[1], q), "shard", 4)
        c_own = jnp.stack([c_pack] + c_own_got)
    mixed, mixed_low, lse = attend(ids, q, k, v, key_extra, query_extra)
    x2, n2 = project_out(ids, x, mixed_low, gain_two, attn_w)

    def places_of(groups):
        tails = jnp.concatenate([group[:, length:] for group in groups], axis=0).astype(F32)
        dense = (tails[:, :lines] + tails[:, lines:]).reshape(-1, EXPERTS, length)
        gate_here = lax.dynamic_slice_in_dim(dense, first_expert, experts, 1)
        chosen = gate_here > 0.0
        before = jnp.triu(jnp.ones((length, length), BF), 1)
        ranks = jnp.einsum("net,tu->neu", chosen.astype(BF), before, preferred_element_type=F32)
        return gate_here, jnp.where(chosen, ranks, -1.0)

    if fast:
        n2, near_b, far_b, *c_far_got = together(n2, near_b, far_b, *c_far_got)
        n2_far = swap(n2, "shard", 4)
        n2_own_got = over_columns(n2)
        cross_a = swap(after(far_a, n2), "shard", 2)
        n2_far, cross_a, *n2_own_got = together(n2_far, cross_a, *n2_own_got)
        cross_b = swap(after(far_b, n2_far), "shard", 2)
        n2_far_got = over_columns(n2_far)
        far_c = swap(after(there[2], n2_far), "shard", 4)
        n2_own = jnp.stack([n2] + n2_own_got)
        c_across = jnp.stack([after(piece, n2_far) for piece in [c_far, *c_far_got]])
        far_c, cross_b, n2_own, c_across, *n2_far_got = together(
            far_c, cross_b, n2_own, c_across, *n2_far_got
        )
        n2_across = jnp.stack([n2_far] + n2_far_got)
        cross_c = swap(far_c, "shard", 2)
        n2_groups = [n2_own, n2_across, swap(n2_own, "shard", 1), swap(n2_across, "shard", 1)]
        c_groups = [c_own, c_across] + [swap(after(g, far_c), "shard", 1) for g in (c_own, c_across)]
        gate_here, slots = places_of(c_groups)
        expert_w = [[here], [near_a, near_b], [far_a, far_b, far_c], [cross_a, cross_b, cross_c]]
        dn2_parts, y_parts, d_experts = mixture(
            ids, slots, gate_here, n2_groups, c_groups, expert_w
        )
        step = swap(d_experts[3], "shard", 2)
        dn2_other = [swap(dn2_parts[3], "shard", 1), swap(dn2_parts[2], "shard", 1)][::-1]
        far_sums = add_low(dn2_parts[1], dn2_other[1])
        own_sums = add_low(dn2_parts[0], dn2_other[0])
        far_got = [swap(far_sums[r], "expert", r) for r in range(1, n_expert)]
        dn2_far = add_low(far_sums[0], *[after(got, own_sums, step) for got in far_got])
        dn2_got = swap(dn2_far, "shard", 4)
        own_got = [swap(after(own_sums[r], dn2_far), "expert", r) for r in range(1, n_expert)]
        d_far = add_low(d_experts[2], after(step, dn2_far))
        y_sum = add_low(y_parts[0], swap(after(y_parts[1], dn2_far), "shard", 1))
        y_sum = y_sum.reshape((2, n_expert) + y_sum.shape[1:])
        far_early, near_early = after((d_far[:, :1], d_experts[1][:, :1]), dn2_got)
        own_got = [after(got, far_early, near_early, y_sum) for got in own_got]
        dn2 = sum([g.astype(F32) for g in own_got + [dn2_got]], own_sums[0].astype(F32))
    else:
        c_own = jnp.stack([c_pack] + over_columns(c_pack))
        c_groups = [c_own, swap(c_own, "shard", 1)]
        gate_here, slots = places_of(c_groups)
        n2_own = jnp.stack([n2] + over_columns(n2))
        n2_groups = [n2_own, swap(n2_own, "shard", 1)]
        c_rows, gate_rows = gather_rows(ids, slots, c_groups, gate_here)
        (x_rows,) = gather_rows(ids, slots, n2_groups)
        flat = (experts, slots.shape[0] * CAP)
        y_rows, dx_rows, grad_rows, d_experts = run_experts(
            ids,
            x_rows.reshape(flat + (width,)),
            c_rows.reshape(flat + (width,)),
            gate_rows.reshape(flat + (LANES,)),
            expert_w,
        )
        split = (experts, slots.shape[0], CAP)
        dn2_parts = spread_rows(ids, slots, dx_rows.reshape(split + (width,)), 2)
        y_parts = spread_rows(
            ids, slots, y_rows.reshape(split + (width,)), 2, grad_rows.reshape(split + (LANES,))
        )
        own_sums = add_low(dn2_parts[0], swap(dn2_parts[1], "shard", 1))
        own_got = [swap(own_sums[r], "expert", r) for r in range(1, n_expert)]
        dn2 = sum([g.astype(F32) for g in own_got], own_sums[0].astype(F32))
        y_sum = add_low(y_parts[0], swap(y_parts[1], "shard", 1))[None]

    dx2, d_mixed, d_out_w = project_out_back(ids, c, x2, gain_two, dn2, mixed_low, attn_w)
    args = (mixed, lse, k, v, key_extra, query_extra, cosine, sine)
    if fast:
        d_out_sums = add_low(d_out_w[0], swap(d_out_w[1], "shard", 1))
        far_a, near_a = swap(far_early, "shard", 4), swap(near_early, "shard", 2)
        y_got = [swap(after(y_sum[1, r], dn2), "expert", r) for r in range(1, n_expert)]
        done = attend_back(ids, q, after(d_mixed, d_out_sums), *args, 1)
        y_across = add_low(y_sum[1, 0], *[after(g, done[0]) for g in y_got])
        dq = after(done[0], y_across, far_a, near_a)
        far_b = swap(after(d_far[:, 1:], dq), "shard", 4)
        near_b = swap(after(d_experts[1][:, 1:], dq), "shard", 2)
        both = jnp.concatenate([y_sum[0], after(d_out_sums, dq)], axis=1)
        both_got = [swap(both[r], "expert", r) for r in range(1, n_expert)]
        d_other = half_grads(ids, rows, gain_one, dq, done[1:], 1, nr, nh)
        dq, *dkv = attend_back(ids, q, after(d_mixed, d_other), *args, 0, done)
        dq, far_b, near_b, *parts = together(dq, far_b, near_b, *dkv, *both_got)
        dkv, both_got = parts[:2], parts[2:]
        d_other = swap(after(d_other, dq), "shard", 1)
        y_far = swap(after(y_across, dq), "shard", 4)
    else:
        dq, *dkv = attend_back(ids, q, d_mixed, *args)
        y_got = [swap(y_sum[0, r], "expert", r) for r in range(1, n_expert)]
    dkv_core = swap(dkv[1], "shard", 1)
    d_own = half_grads(ids, rows, gain_one, dq, dkv, 0, nr, nh)
    if fast:
        d_own, d_other, dkv_core = together(d_own, d_other, dkv_core)
    dkv_sums = add_low(dkv[0], dkv_core)
    dkv_parts = [dkv_sums[:, r * length : (r + 1) * length] for r in range(chips)]
    if fast:
        sums = add_low(d_own, d_other)
        dkv_step = swap(dkv_parts[3], "shard", 2)
        dkv_far = add_low(dkv_parts[2], dkv_step)
        sums, y_far, dkv_far = together(sums, y_far, dkv_far)
        got = [swap(sums[r], "expert", r) for r in range(1, n_expert)]
        dkv_far = swap(dkv_far, "shard", 4)
        dkv_near = swap(after(dkv_parts[1], dkv_step), "shard", 2)
        dkv_near, dkv_far, *got = together(dkv_near, dkv_far, *got)
        both = sum([g.astype(F32) for g in both_got], both[0].astype(F32))
        y_out, d_out_total = both[: y_sum.shape[2]], both[y_sum.shape[2] :].astype(BF)
        cols = width // nh
        high = d_out_total.shape[0] - GATE_ROWS
        gain_grad = d_out_total[high, : width // n_expert]
        d_out_total = jnp.concatenate(
            [d_out_total[:high, f * cols : (f + 1) * cols] for f in range(nh)], axis=0
        )
        gain_grad = jnp.broadcast_to(gain_grad[:, None], (gain_grad.shape[0], LANES))
        d_out_total = jnp.concatenate([d_out_total, gain_grad], axis=1)
        dkv_own = sum([g.astype(F32) for g in (dkv_near, dkv_far)], dkv_parts[0].astype(F32))
        d_total = add_low(sums[0], *got)
        total = jnp.concatenate([d_out_total, d_total], axis=1)
        total = total.reshape(chips, total.shape[0] // chips, total.shape[1])
        total = [pick(total, z ^ r) for r in range(chips)]
        step, near = swap(total[3], "shard", 2), swap(total[1], "shard", 2)
        far = swap(add_low(total[2], step), "shard", 4)
        token_grad = rows_back(ids, dq, dkv_own, x, dx2, gain_one, attn_w)
        summed = total[0].astype(F32) + near.astype(F32) + after(far, token_grad).astype(F32)
        summed = summed.reshape(2, summed.shape[0] // 2, summed.shape[1])
        mine = pick(summed, core)
        other = swap(pick(summed, 1 - core).astype(BF), "shard", 1).astype(F32)
        parts = (jnp.where(core == 0, mine, other), jnp.where(core == 0, other, mine))
        out_sum = y_out + after(y_far, far).astype(F32)
    else:
        out_sum = sum([g.astype(F32) for g in y_got], y_sum[0, 0].astype(F32))
        dkv_own = scatter_z(dkv_parts)
        token_grad = rows_back(ids, dq, dkv_own, x, dx2, gain_one, attn_w)
        gain_grad = jnp.broadcast_to(d_out_w[0][0, width][:, None], (width, LANES))
        joined = jnp.concatenate([d_out_w[0][0, :width], gain_grad, d_own[0]], axis=1)
        joined = lax.psum_scatter(joined, ("expert", "shard"), scatter_dimension=0, tiled=True)
        parts = [joined.astype(F32)]

    on, qn, kn = width // nh, H * HD // nh, KVH * HD // nh
    start = on + LANES
    d_out_full = jnp.concatenate([p[:, :on] for p in parts], axis=1)
    d_gain_two = parts[0][:, on]
    d_query_w = jnp.concatenate([p[:, start : start + qn] for p in parts], axis=1)
    d_key_w = jnp.concatenate([p[:, start + qn : start + qn + kn] for p in parts], axis=1)
    d_value_w = jnp.concatenate([p[:, start + qn + kn :] for p in parts], axis=1)
    row_sums = (
        jnp.sum(w_query.astype(BF).astype(F32) * d_query_w, axis=1)
        + jnp.sum(w_key.astype(BF).astype(F32) * d_key_w, axis=1)
        + jnp.sum(w_value.astype(BF).astype(F32) * d_value_w, axis=1)
    )
    d_gain_one = row_sums / attn_gain.astype(BF).astype(F32)

    output = x2 + out_sum[:length]
    gate_sums = out_sum[length : length + lines].reshape(EXPERTS, length)
    gate_grad = jnp.sum(jnp.where(named_experts(routes), gate_sums[:, :, None], 0.0), axis=0)

    if fast:
        there_sum = jnp.concatenate([far_a, far_b], axis=1).astype(F32)
        here_sum = d_experts[0].astype(F32)
        here_sum = here_sum + jnp.concatenate([near_a, near_b], axis=1).astype(F32)
        d_chip = jnp.where(
            side == 0,
            jnp.concatenate([here_sum, there_sum], axis=0),
            jnp.concatenate([there_sum, here_sum], axis=0),
        )
    else:
        d_chip = scatter_z(d_experts)
    half = d_chip.shape[2] // 2
    d_chip = d_chip.astype(BF)
    if fast:
        d_chip = after(d_chip, *got)
    mine = lax.dynamic_slice_in_dim(d_chip, core * half, half, 2)
    other = swap(lax.dynamic_slice_in_dim(d_chip, (1 - core) * half, half, 2), "shard", 1)
    if fast:
        other = after(other, dkv_own)
    d_expert = in_order(mine, other, core, 0).astype(F32)

    return (
        output[None],
        token_grad[None],
        gate_grad[None],
        d_gain_one,
        d_query_w,
        d_key_w,
        d_value_w,
        d_out_full,
        d_gain_two,
        d_expert[:, 0],
        d_expert[:, 1],
        d_expert[:, 2],
    )


def solution(mesh):
    rows = P("expert", "shard", None)
    split = P(("expert", "shard"), None)
    gain = P(("expert", "shard"))
    in_specs = (
        rows, P("expert", None), rows, rows, gain, split, split, split, split, gain, rows, rows, rows, rows,
    )
    out_specs = (rows, rows, rows, gain, split, split, split, split, gain, rows, rows, rows)
    return jax.shard_map(body, mesh=mesh, in_specs=in_specs, out_specs=out_specs, check_vma=False)
```

```python
import functools

import jax
import jax.numpy as jnp
import numpy as np
from jax import lax
from jax.experimental import pallas as pl
from jax.experimental.pallas import tpu as pltpu
from jax.sharding import PartitionSpec as P

H = 16
KVH = 8
HD = 64
EXPERTS = 32
TOP = 8
CAP = 80
EPSILON = 1e-06
LANES = 128
PAIRS = KVH // 2
BLOCKS = 2
GATE_ROWS = 16

BF = jnp.bfloat16
F32 = jnp.float32
VMEM_BYTES = 56 * 1024 * 1024


def dot(left, right):
    return lax.dot_general(left, right, (((1,), (0,)), ((), ())), preferred_element_type=F32)


def dot_nt(left, right):
    return lax.dot_general(left, right, (((1,), (1,)), ((), ())), preferred_element_type=F32)


def dot_tn(left, right):
    return lax.dot_general(left, right, (((0,), (0,)), ((), ())), preferred_element_type=F32)


def call(kernel, grid, scalars, inputs, in_specs, out_shapes, out_specs, scratch=(), aliases=None):
    return pl.pallas_call(
        kernel,
        grid_spec=pltpu.PrefetchScalarGridSpec(
            num_scalar_prefetch=1,
            grid=grid,
            in_specs=in_specs,
            out_specs=out_specs,
            scratch_shapes=list(scratch),
        ),
        out_shape=out_shapes,
        input_output_aliases=aliases or {},
        compiler_params=pltpu.CompilerParams(vmem_limit_bytes=VMEM_BYTES),
        cost_estimate=pl.CostEstimate(flops=0, bytes_accessed=0, transcendentals=0),
    )(scalars, *inputs)


def whole_spec(shape):
    return pl.BlockSpec(tuple(shape), lambda *_: (0,) * len(shape))


def lane_ids(rows):
    return lax.broadcasted_iota(jnp.int32, (rows, LANES), 1)


def swap_halves(tile):
    first = lane_ids(tile.shape[0]) % HD < HD // 2
    return jnp.where(first, pltpu.roll(tile, LANES - HD // 2, 1), pltpu.roll(tile, HD // 2, 1))


def turn(value, cosine, signed_sine, direction):
    tiles = []
    for i in range(value.shape[1] // LANES):
        tile = value[:, i * LANES : (i + 1) * LANES]
        tiles.append(tile * cosine + direction * (swap_halves(tile) * signed_sine))
    return tiles[0] if len(tiles) == 1 else jnp.concatenate(tiles, axis=1)


def row_chunk(ids, r, count):
    return ids[0] ^ r if count > 1 else 0


def z_chunk(ids, r, count):
    return ids[1] ^ r if count > 1 else 0


def half_chunk(ids, h, count):
    return ids[2] ^ h if count > 1 else 0


def span(index, size):
    return pl.ds(pl.multiple_of(index * size, size), size)


def columns(nh, width):
    on, qn, kn = width // nh, H * HD // nh, KVH * HD // nh
    return on, on + qn, on + qn + kn, on + qn + 2 * kn


def frequencies():
    return np.tile(10000.0 ** (-np.arange(HD // 2) * 2.0 / HD), 2 * LANES // HD)


def place_tables(length):
    angles = np.arange(length)[:, None] * frequencies()[None, :]
    return np.cos(angles).astype(np.float32), np.sin(angles).astype(np.float32)


def qkv_kernel(nr, nh, ids, own_ref, other_ref, gain_ref, cos_ref, sin_ref, slot_cos, slot_sin, *rest):
    weights = rest[:nh]
    q_ref, k_ref, v_ref, cos_out, sin_out, normed_ref = rest[nh:]
    width = own_ref.shape[-1]
    chunk = width // nr
    qn, kn = H * HD // nh, KVH * HD // nh
    at_q, at_k, _, at_end = columns(nh, width)
    normalize(own_ref, other_ref, gain_ref, normed_ref)
    length = cos_ref.shape[0]
    sign = jnp.where(lane_ids(length) % HD < HD // 2, -1.0, 1.0)
    for b in range(cos_out.shape[0] // length):
        slot = pl.ds(pl.program_id(0) * (cos_out.shape[0] // length) + b, 1)
        c, s = slot_cos[slot], slot_sin[slot]
        at = slice(b * length, (b + 1) * length)
        cos_out[at] = cos_ref[...] * c - sin_ref[...] * s
        sin_out[at] = sign * (sin_ref[...] * c + cos_ref[...] * s)
    cosine, sine = cos_out[...], sin_out[...]
    for h in range(nh):
        total = None
        for r in range(nr):
            part = dot(
                normed_ref[:, span(row_chunk(ids, r, nr), chunk)],
                weights[h][r, :, at_k:at_end],
            )
            total = part if total is None else total + part
        here = span(half_chunk(ids, h, nh), kn)
        k_ref[:, here] = turn(total[:, :kn], cosine, sine, 1.0).astype(BF)
        v_ref[:, here] = total[:, kn:].astype(BF)

    rows = q_ref.shape[0]

    @pl.when(pl.program_id(0) == 0)
    def _():
        for h in range(nh):
            total = None
            for r in range(nr):
                part = dot(
                    normed_ref[:rows, span(row_chunk(ids, r, nr), chunk)], weights[h][r, :, at_q:at_k]
                )
                total = part if total is None else total + part
            turned = turn(total, cosine[:rows], sine[:rows], 1.0).astype(BF).astype(F32) * HD**-0.5
            q_ref[:, span(half_chunk(ids, h, nh), qn)] = turned.astype(BF)


def normalize(own_ref, other_ref, gain_ref, normed_ref):
    own = pl.program_id(0) < pl.num_programs(0) // 2
    rows = jnp.where(own, own_ref[...], other_ref[...])
    normed_ref[...] = (rows.astype(F32) * gain_ref[...]).astype(BF)


def rows_specs(steps, shape):
    half = steps // 2
    return [
        pl.BlockSpec(shape, lambda i, _: (jnp.minimum(i, half - 1), 0)),
        pl.BlockSpec(shape, lambda i, _: (jnp.maximum(i - half, 0), 0)),
    ]


def flat_rows(rows):
    return [part.reshape(-1, part.shape[-1]) for part in rows]


def project(ids, rows, gain, cosine, sine, weights):
    slots, (length, width) = 2 * rows[0].shape[0], rows[0].shape[1:]
    nr, nh = weights[0].shape[0], len(weights)
    tile, steps = BLOCKS * length, slots // BLOCKS
    tables = [jnp.asarray(t) for t in place_tables(length)]
    return call(
        functools.partial(qkv_kernel, nr, nh),
        (steps,),
        ids,
        [*flat_rows(rows), gain, *tables, cosine, sine, *weights],
        [
            *rows_specs(steps, (tile, width)),
            whole_spec(gain.shape),
            *[whole_spec(t.shape) for t in tables],
            whole_spec(cosine.shape),
            whole_spec(sine.shape),
            *[whole_spec(w.shape) for w in weights],
        ],
        [
            jax.ShapeDtypeStruct((length, H * HD), BF),
            jax.ShapeDtypeStruct((slots * length, KVH * HD), BF),
            jax.ShapeDtypeStruct((slots * length, KVH * HD), BF),
            jax.ShapeDtypeStruct((slots * length, LANES), F32),
            jax.ShapeDtypeStruct((slots * length, LANES), F32),
        ],
        [
            whole_spec((length, H * HD)),
            pl.BlockSpec((tile, KVH * HD), lambda i, _: (i, 0)),
            pl.BlockSpec((tile, KVH * HD), lambda i, _: (i, 0)),
            pl.BlockSpec((tile, LANES), lambda i, _: (i, 0)),
            pl.BlockSpec((tile, LANES), lambda i, _: (i, 0)),
        ],
        [pltpu.VMEM((tile, width), BF)],
    )


def to_half(tile, which, wanted):
    if which != wanted:
        tile = pltpu.roll(tile, HD, 1)
    return jnp.where(lane_ids(tile.shape[0]) // HD == wanted, tile, 0.0)


def attend_kernel(ids, q_ref, k_ref, v_ref, kx_ref, qx_ref, o_ref, low_ref, lse_ref):
    keys = jnp.concatenate([k_ref[...], kx_ref[...]], axis=1)
    values = v_ref[...]
    extra = qx_ref[...]
    rows = q_ref.shape[0]
    lanes = lane_ids(rows)
    sums = jnp.zeros((rows, LANES), F32)
    for t in range(2):
        tile = q_ref[:, t * LANES : (t + 1) * LANES].astype(F32)
        mixed = jnp.zeros((rows, LANES), F32)
        for w in range(2):
            query = jnp.concatenate([to_half(tile, w, t).astype(BF), extra], axis=1)
            scores = dot_nt(query, keys)
            highest = jnp.max(scores, axis=1, keepdims=True)
            weights = jnp.exp(scores - highest)
            total = jnp.sum(weights, axis=1, keepdims=True)
            out = dot(weights.astype(BF), values) / total
            mixed = mixed + to_half(out, t, w)
            sums = jnp.where(lanes == 2 * t + w, highest + jnp.log(total), sums)
        o_ref[:, t * LANES : (t + 1) * LANES] = mixed
        low_ref[:, t * LANES : (t + 1) * LANES] = mixed.astype(BF)
    lse_ref[0] = sums


def attend(ids, q, k, v, key_extra, query_extra):
    length, keys = q.shape[0], k.shape[0]
    quad = pl.BlockSpec((length, 2 * LANES), lambda p, _: (0, p))
    pair = pl.BlockSpec((keys, LANES), lambda p, _: (0, p))
    return call(
        attend_kernel,
        (PAIRS,),
        ids,
        [q, k, v, key_extra, query_extra],
        [quad, pair, pair, whole_spec(key_extra.shape), whole_spec(query_extra.shape)],
        [
            jax.ShapeDtypeStruct((length, H * HD), F32),
            jax.ShapeDtypeStruct((length, H * HD), BF),
            jax.ShapeDtypeStruct((PAIRS, length, LANES), F32),
        ],
        [quad, quad, pl.BlockSpec((1, length, LANES), lambda p, _: (p, 0, 0))],
    )


def three_parts(value):
    high = value.astype(BF)
    rest = value - high.astype(F32)
    middle = rest.astype(BF)
    return high.astype(F32), middle.astype(F32), (rest - middle.astype(F32))


def with_parts(base, value, lanes):
    high, middle, low = three_parts(value)
    base = jnp.where(lanes == 16, high, base)
    base = jnp.where(lanes == 17, middle, base)
    return jnp.where(lanes == 18, low, base).astype(BF)


def attend_back_kernel(
    span_rows, ids, q_ref, do_ref, o_ref, lse_ref, k_ref, v_ref, kx_ref, qx_ref, cos_ref, sin_ref,
    dq_ref, own_ref, other_ref, sum_ref,
):
    rows = q_ref.shape[0]
    lanes = lane_ids(rows)
    extra = qx_ref[...].astype(F32)
    nothing = jnp.zeros((rows, LANES), F32)
    sums = lse_ref[0]
    queries, outs, pads_q, pads_o = [], [], [], []
    for t in range(2):
        at = slice(t * LANES, (t + 1) * LANES)
        tile, grad = q_ref[:, at].astype(F32), do_ref[:, at].astype(F32)
        product = grad * o_ref[:, at]
        for w in range(2):
            here = lanes // HD == w
            delta = jnp.sum(jnp.where(here, product, 0.0), axis=1, keepdims=True)
            log_sum = jnp.sum(jnp.where(lanes == 2 * t + w, sums, 0.0), axis=1, keepdims=True)
            q_pad = to_half(tile, w, t).astype(BF)
            o_pad = to_half(grad, w, t).astype(BF)
            queries.append(jnp.concatenate([q_pad, with_parts(extra, -log_sum, lanes)], axis=1))
            outs.append(jnp.concatenate([o_pad, with_parts(nothing, -delta, lanes)], axis=1))
            pads_q.append(q_pad)
            pads_o.append(o_pad)
    all_q = jnp.concatenate(pads_q, axis=0)
    every_q = jnp.concatenate(queries, axis=0)
    every_o = jnp.concatenate(outs, axis=0)
    all_o = jnp.concatenate(pads_o, axis=0)
    sum_ref[...] = jnp.zeros_like(sum_ref)

    spans = k_ref.shape[0] // 2 // span_rows

    def one_span(i, _, part, out_ref):
        put = pl.ds(pl.multiple_of(i * span_rows, span_rows), span_rows)
        first = part * spans * span_rows
        at = pl.ds(pl.multiple_of(first + i * span_rows, span_rows), span_rows)
        k_here, x_here = k_ref[at, :], kx_ref[at, :]
        keys = jnp.concatenate([k_here, x_here], axis=1)
        values = jnp.concatenate([v_ref[at, :], x_here], axis=1)
        probs = jnp.exp(dot_nt(keys, every_q))
        d_scores = (probs * dot_nt(values, every_o)).astype(BF)
        sum_ref[...] += dot_tn(k_here, d_scores)
        out_ref[1, put, :] = dot(probs.astype(BF), all_o).astype(BF)
        d_key = dot(d_scores, all_q)
        d_key = turn(d_key, cos_ref[at, :], sin_ref[at, :], -1.0)
        out_ref[0, put, :] = d_key.astype(BF)
        return 0

    for part, out_ref in enumerate((own_ref, other_ref)):
        lax.fori_loop(0, spans, functools.partial(one_span, part=part, out_ref=out_ref), 0)
    cosine, sine = cos_ref[:rows, :], sin_ref[:rows, :]
    for t in range(2):
        d_query = [sum_ref[:, n * rows : (n + 1) * rows].T for n in (2 * t, 2 * t + 1)]
        tile = to_half(d_query[0], t, 0) + to_half(d_query[1], t, 1)
        turned = turn(tile * HD**-0.5, cosine, sine, -1.0)
        dq_ref[:, t * LANES : (t + 1) * LANES] = turned.astype(BF)


def attend_back_part(*refs):
    attend_back_kernel(1024, *refs[:11], *refs[14:])


def attend_back(ids, q, d_out, out, lse, k, v, key_extra, query_extra, cosine, sine, half=None, done=None):
    length, keys = q.shape[0], k.shape[0]
    count = PAIRS if half is None else PAIRS // 2

    def at(p, ids):
        return p if half is None else (ids[2] ^ half) * count + p

    quad = pl.BlockSpec((length, 2 * LANES), lambda p, ids: (0, at(p, ids)))
    pair = pl.BlockSpec((keys, LANES), lambda p, ids: (0, at(p, ids)))
    ins = [q, d_out, out, lse, k, v, key_extra, query_extra, cosine, sine]
    specs = [
        quad,
        quad,
        quad,
        pl.BlockSpec((1, length, LANES), lambda p, ids: (at(p, ids), 0, 0)),
        pair,
        pair,
        whole_spec(key_extra.shape),
        whole_spec(query_extra.shape),
        whole_spec(cosine.shape),
        whole_spec(sine.shape),
    ]
    if done is not None:
        ins += done
        specs += [pl.BlockSpec(memory_space=pl.ANY)] * 3
    return call(
        attend_back_part if done is not None else functools.partial(attend_back_kernel, 1024),
        (count,),
        ids,
        ins,
        specs,
        [
            jax.ShapeDtypeStruct((length, H * HD), BF),
            jax.ShapeDtypeStruct((2, keys // 2, KVH * HD), BF),
            jax.ShapeDtypeStruct((2, keys // 2, KVH * HD), BF),
        ],
        [quad] + [pl.BlockSpec((2, keys // 2, LANES), lambda p, ids: (0, 0, at(p, ids)))] * 2,
        [pltpu.VMEM((LANES, 4 * length), F32)],
        aliases={11: 0, 12: 1, 13: 2} if done is not None else None,
    )


def out_kernel(nr, nh, ids, x_ref, o_ref, gain_ref, *rest):
    weights = rest[:nh]
    x2_ref, n2_ref = rest[nh:]
    width = x_ref.shape[1]
    chunk, cols = H * HD // nr, width // nh
    for h in range(nh):
        at = span(half_chunk(ids, h, nh), cols)
        total = x_ref[:, at]
        for r in range(nr):
            total = total + dot(
                o_ref[:, span(row_chunk(ids, r, nr), chunk)], weights[h][r]
            )
        x2_ref[:, at] = total
    middle = x2_ref[...]
    inverse = lax.rsqrt(jnp.mean(middle * middle, axis=1, keepdims=True) + EPSILON)
    n2_ref[...] = (middle * inverse * gain_ref[...]).astype(BF)


def out_spec(weight, cols):
    return pl.BlockSpec(weight.shape[:2] + (cols,), lambda *_: (0, 0, 0))


def project_out(ids, x, low, gain, weights):
    nr, nh = weights[0].shape[0], len(weights)
    ins = [x, low, gain, *weights]
    outs = [jax.ShapeDtypeStruct(x.shape, F32), jax.ShapeDtypeStruct(x.shape, BF)]
    return call(
        functools.partial(out_kernel, nr, nh),
        (1,),
        ids,
        ins,
        [whole_spec(i.shape) for i in ins[:3]] + [out_spec(w, x.shape[1] // nh) for w in weights],
        outs,
        [whole_spec(o.shape) for o in outs],
    )


def out_back_kernel(nr, nh, ids, c_ref, x2_ref, gain_ref, dn2_ref, low_ref, *rest):
    weights = rest[:nh]
    dx2_ref, do_ref = rest[nh : nh + 2]
    grads = rest[nh + 2 : 2 * nh + 2]
    dr_ref, term_ref = rest[2 * nh + 2 :]
    width = c_ref.shape[1]
    chunk, cols = H * HD // nr, width // nh
    middle, d_normed = x2_ref[...], dn2_ref[...]
    inverse = lax.rsqrt(jnp.mean(middle * middle, axis=1, keepdims=True) + EPSILON)
    scaled = d_normed * gain_ref[...]
    inner = jnp.mean(scaled * middle, axis=1, keepdims=True)
    d_middle = c_ref[...] + inverse * scaled - middle * (inverse * inverse * inverse * inner)
    dx2_ref[...] = d_middle
    dr_ref[...] = d_middle.astype(BF)
    term_ref[...] = d_normed * middle * inverse
    fold = width // cols
    rows = chunk // fold
    for r in range(nr):
        at = span(row_chunk(ids, r, nr), chunk)
        low = low_ref[:, at]
        gain_grad = jnp.sum(term_ref[:, at], axis=0, keepdims=True)
        gain_grad = jnp.concatenate([gain_grad] * (width // chunk), axis=1)
        total = None
        for h in range(nh):
            branch = dr_ref[:, span(half_chunk(ids, h, nh), cols)]
            part = dot_nt(branch, weights[h][r])
            total = part if total is None else total + part
            grad = dot_tn(low, branch).astype(BF)
            for f in range(fold):
                grads[h][r, :rows, f * cols : (f + 1) * cols] = grad[f * rows : (f + 1) * rows]
            grads[h][r, rows:] = jnp.broadcast_to(gain_grad, (GATE_ROWS, width)).astype(BF)
        do_ref[:, at] = total.astype(BF)


def project_out_back(ids, c, x2, gain, dn2, low, weights):
    nr, nh = weights[0].shape[0], len(weights)
    ins = [c, x2, gain, dn2, low, *weights]
    rows, cols = H * HD // nr, c.shape[1] // nh
    outs = [jax.ShapeDtypeStruct(c.shape, F32), jax.ShapeDtypeStruct((c.shape[0], H * HD), BF)]
    high = rows * cols // c.shape[1] + GATE_ROWS
    outs += [jax.ShapeDtypeStruct((nr, high, c.shape[1]), BF)] * nh
    got = call(
        functools.partial(out_back_kernel, nr, nh),
        (1,),
        ids,
        ins,
        [whole_spec(i.shape) for i in ins[:5]] + [out_spec(w, cols) for w in weights],
        outs,
        [whole_spec(o.shape) for o in outs],
        [pltpu.VMEM(c.shape, BF), pltpu.VMEM(c.shape, F32)],
    )
    return got[0], got[1], got[2:]


def picks(slot_ref, experts):
    tokens = slot_ref.shape[-1]
    places = lax.broadcasted_iota(jnp.int32, (CAP, tokens), 0).astype(F32)
    rows = [places == slot_ref[0, j : j + 1, :] for j in range(experts)]
    return rows[0] if experts == 1 else jnp.concatenate(rows, axis=0)


def gather_kernel(groups, per, experts, with_gates, ids, slot_ref, *rest):
    if with_gates:
        gate_ref, rest = rest[0], rest[1:]
    tokens, out_ref = rest[:groups], rest[groups]
    chosen = picks(slot_ref, experts)
    low = chosen.astype(F32).astype(BF)
    for g in range(groups):

        @pl.when(pl.program_id(0) // per == g)
        def _(g=g):
            rows = dot(low, tokens[g][0, : slot_ref.shape[-1]]).astype(BF)
            for j in range(experts):
                out_ref[j, 0] = rows[j * CAP : (j + 1) * CAP]

    if with_gates:
        for j in range(experts):
            mine = chosen[j * CAP : (j + 1) * CAP]
            gates = jnp.sum(jnp.where(mine, gate_ref[0, j : j + 1, :], 0.0), axis=1, keepdims=True)
            rest[groups + 1][j, 0] = jnp.broadcast_to(gates, (CAP, LANES))


def gather_rows(ids, slots, groups, gates=None):
    blocks, experts, length = slots.shape
    per, width = groups[0].shape[0], groups[0].shape[-1]
    ins, specs = [slots], [pl.BlockSpec((1, experts, length), lambda i, _: (i, 0, 0))]
    if gates is not None:
        ins.append(gates)
        specs.append(specs[0])
    for g, tokens in enumerate(groups):
        ins.append(tokens)
        specs.append(
            pl.BlockSpec(
                (1,) + tokens.shape[1:], lambda i, _, g=g: (jnp.clip(i - g * per, 0, per - 1), 0, 0)
            )
        )
    outs = [jax.ShapeDtypeStruct((experts, blocks, CAP, width), BF)]
    out_specs = [pl.BlockSpec((experts, 1, CAP, width), lambda i, _: (0, i, 0, 0))]
    if gates is not None:
        outs.append(jax.ShapeDtypeStruct((experts, blocks, CAP, LANES), F32))
        out_specs.append(pl.BlockSpec((experts, 1, CAP, LANES), lambda i, _: (0, i, 0, 0)))
    return call(
        functools.partial(gather_kernel, len(groups), per, experts, gates is not None),
        (blocks,),
        ids,
        ins,
        specs,
        outs,
        out_specs,
    )


def expert_kernel(nz, ids, x_ref, c_ref, gate_ref, *rest):
    weights, rest = rest[:nz], rest[nz:]
    y_ref, dx_ref, gg_ref = rest[:3]
    grads, acc_ref = rest[3 : 3 + nz], rest[3 + nz]
    chunk = x_ref.shape[-1] // nz
    step, last = pl.program_id(1), pl.num_programs(1) - 1
    a = b = ch = None
    for r in range(nz):
        at = span(z_chunk(ids, r, nz), chunk)
        x, c = x_ref[0, :, at], c_ref[0, :, at]
        parts = (
            dot(x, weights[r][0, 0]),
            dot(x, weights[r][0, 1]),
            dot(c, weights[r][0, 2]),
        )
        a, b, ch = parts if a is None else (a + parts[0], b + parts[1], ch + parts[2])
    gate = gate_ref[0][:, :1]
    sig = 1.0 / (1.0 + jnp.exp(-a))
    act = a * sig
    hidden = (act * b).astype(BF).astype(F32)
    gg_ref[0] = jnp.broadcast_to(jnp.sum(hidden * ch, axis=1, keepdims=True), gg_ref.shape[1:])
    hg = (hidden * gate).astype(BF)
    dh = ch * gate
    da = (dh * b * sig * (1.0 + a * (1.0 - sig))).astype(BF)
    db = (dh * act).astype(BF)

    @pl.when(step == 0)
    def _():
        acc_ref[...] = jnp.zeros_like(acc_ref)

    for r in range(nz):
        at = span(z_chunk(ids, r, nz), chunk)
        x, c = x_ref[0, :, at], c_ref[0, :, at]
        y_ref[0, :, at] = dot_nt(hg, weights[r][0, 2]).astype(BF)
        dx_ref[0, :, at] = (dot_nt(da, weights[r][0, 0]) + dot_nt(db, weights[r][0, 1])).astype(BF)
        acc_ref[r, 0] += dot_tn(x, da)
        acc_ref[r, 1] += dot_tn(x, db)
        acc_ref[r, 2] += dot_tn(c, hg)

    @pl.when(step == last)
    def _():
        for r in range(nz):
            grads[r][0] = acc_ref[r].astype(BF)


def run_experts(ids, x_rows, c_rows, gate_rows, weights):
    experts, rows, width = x_rows.shape
    nz = len(weights)
    hidden = weights[0].shape[-1]
    tile = 256
    block = pl.BlockSpec((1, tile, width), lambda j, i, _: (j, i, 0))
    narrow = pl.BlockSpec((1, tile, LANES), lambda j, i, _: (j, i, 0))
    matrix = pl.BlockSpec((1,) + weights[0].shape[1:], lambda j, i, _: (j, 0, 0, 0))
    got = call(
        functools.partial(expert_kernel, nz),
        (experts, rows // tile),
        ids,
        [x_rows, c_rows, gate_rows, *weights],
        [block, block, narrow] + [matrix] * nz,
        [
            jax.ShapeDtypeStruct(x_rows.shape, BF),
            jax.ShapeDtypeStruct(x_rows.shape, BF),
            jax.ShapeDtypeStruct((experts, rows, LANES), F32),
        ]
        + [jax.ShapeDtypeStruct(w.shape, BF) for w in weights],
        [block, block, narrow] + [matrix] * nz,
        [pltpu.VMEM((nz,) + weights[0].shape[1:], F32)],
    )
    return got[0], got[1], got[2], got[3:]


def spread_kernel(groups, per, experts, with_grads, ids, slot_ref, rows_ref, *rest):
    if with_grads:
        grad_ref, rest = rest[0], rest[1:]
    chosen = picks(slot_ref, experts)
    low = chosen.astype(F32).astype(BF)
    rows = [rows_ref[j, 0] for j in range(experts)]
    rows = rows[0] if experts == 1 else jnp.concatenate(rows, axis=0)
    total = dot_tn(low, rows).astype(BF)
    length, width = total.shape
    tail = None
    if with_grads:
        fit = width // length
        line = lax.broadcasted_iota(jnp.int32, (GATE_ROWS, width), 0)
        place = lax.broadcasted_iota(jnp.int32, (GATE_ROWS, width), 1) // length
        tail = jnp.zeros((GATE_ROWS, width), F32)
        for j in range(experts):
            mine = chosen[j * CAP : (j + 1) * CAP]
            sums = jnp.sum(jnp.where(mine, grad_ref[j, 0][:, :1], 0.0), axis=0, keepdims=True)
            wide = jnp.concatenate([sums] * fit, axis=1)
            number = ids[3] + j
            tail = tail + jnp.where((line == number // fit) & (place == number % fit), wide, 0.0)
    for g in range(groups):

        @pl.when(pl.program_id(0) // per == g)
        def _(g=g):
            rest[g][0, :length] = total
            if with_grads:
                rest[g][0, length:] = tail.astype(BF)


def spread_rows(ids, slots, rows, groups, grads=None):
    blocks, experts, length = slots.shape
    per, width = blocks // groups, rows.shape[-1]
    high = length + (GATE_ROWS if grads is not None else 0)
    ins = [slots, rows]
    specs = [
        pl.BlockSpec((1, experts, length), lambda i, _: (i, 0, 0)),
        pl.BlockSpec((experts, 1, CAP, width), lambda i, _: (0, i, 0, 0)),
    ]
    if grads is not None:
        ins.append(grads)
        specs.append(pl.BlockSpec((experts, 1, CAP, LANES), lambda i, _: (0, i, 0, 0)))
    return call(
        functools.partial(spread_kernel, groups, per, experts, grads is not None),
        (blocks,),
        ids,
        ins,
        specs,
        [jax.ShapeDtypeStruct((per, high, width), BF)] * groups,
        [
            pl.BlockSpec(
                (1, high, width), lambda i, _, g=g: (jnp.clip(i - g * per, 0, per - 1), 0, 0)
            )
            for g in range(groups)
        ],
    )


def mixture_kernel(nz, w_parts, groups, per, experts, tile, ids, slot_ref, gate_ref, *rest):
    n2_in, rest = rest[:groups], rest[groups:]
    c_in, rest = rest[:groups], rest[groups:]
    w_in, rest = rest[: len(w_parts)], rest[len(w_parts) :]
    dn2_out, rest = rest[:groups], rest[groups:]
    y_out, rest = rest[: groups // 2], rest[groups // 2 :]
    dw_out, rest = rest[:nz], rest[nz:]
    n2_ref, c_ref, w_ref, x_rows, c_rows, gate_rows, grad_rows, inner_ref, dw_ref = rest[:9]
    n2_sem, c_sem, w_sem, dn2_sem, y_sem, dw_sem = rest[9:]
    length = slot_ref.shape[-1]
    width = n2_ref.shape[-1]
    chunk = width // nz
    blocks = groups * per

    def n2_copy(g):
        return pltpu.make_async_copy(n2_in[g], n2_ref.at[pl.ds(g * per, per)], n2_sem.at[g])

    def c_copy(g):
        return pltpu.make_async_copy(c_in[g], c_ref.at[pl.ds(g * per, per)], c_sem.at[g])

    def w_copy(n):
        r, first, count = w_parts[n]
        to = w_ref.at[:, pl.ds(first, count), span(z_chunk(ids, r, nz), chunk)]
        return pltpu.make_async_copy(w_in[n], to, w_sem.at[n])

    for g in range(groups):
        c_copy(g).start()
        n2_copy(g).start()
    for n in range(len(w_parts)):
        w_copy(n).start()

    def chosen_rows(i):
        places = lax.broadcasted_iota(jnp.int32, (CAP, length), 0).astype(F32)
        return [places == slot_ref[i, j : j + 1, :] for j in range(experts)]

    def one_hot(chosen):
        chosen = [jnp.where(c, 1.0, 0.0).astype(BF) for c in chosen]
        return chosen[0] if experts == 1 else jnp.concatenate(chosen, axis=0)

    def gather(i, _):
        chosen = chosen_rows(i)
        low = one_hot(chosen)
        at = pl.ds(pl.multiple_of(i * CAP, CAP), CAP)
        got_x = dot(low, n2_ref[i]).astype(BF)
        got_c = dot(low, c_ref[i, :length]).astype(BF)
        for j in range(experts):
            x_rows[j, at] = got_x[j * CAP : (j + 1) * CAP]
            c_rows[j, at] = got_c[j * CAP : (j + 1) * CAP]
            gates = jnp.where(chosen[j], gate_ref[i, j : j + 1, :], 0.0)
            gate_rows[j, at] = jnp.broadcast_to(jnp.sum(gates, axis=1, keepdims=True), (CAP, LANES))
        return 0

    for g in range(groups):
        c_copy(g).wait()
        n2_copy(g).wait()
        lax.fori_loop(g * per, (g + 1) * per, gather, 0, unroll=True)
    for n in range(len(w_parts)):
        w_copy(n).wait()

    def dw_copy(j, r):
        rows = span(z_chunk(ids, r, nz), chunk)
        return pltpu.make_async_copy(dw_ref.at[j, :, rows], dw_out[r].at[j], dw_sem.at[j, r])

    for j in range(experts):

        def one_tile(i, _, j=j):
            at = pl.ds(pl.multiple_of(i * tile, tile), tile)
            x, c = x_rows[j, at], c_rows[j, at]
            a, b, ch = dot(x, w_ref[j, 0]), dot(x, w_ref[j, 1]), dot(c, w_ref[j, 2])
            gate = gate_rows[j, at][:, :1]
            sig = 1.0 / (1.0 + jnp.exp(-a))
            act = a * sig
            hidden = (act * b).astype(BF).astype(F32)
            grad = jnp.sum(hidden * ch, axis=1, keepdims=True)
            grad_rows[j, at] = jnp.broadcast_to(grad, (tile, LANES))
            hg = (hidden * gate).astype(BF)
            dh = ch * gate
            da = (dh * b * sig * (1.0 + a * (1.0 - sig))).astype(BF)
            db = (dh * act).astype(BF)
            inner_ref[0, at], inner_ref[1, at], inner_ref[2, at] = da, db, hg
            return 0

        lax.fori_loop(0, blocks * CAP // tile, one_tile, 0)
        for part in range(width // chunk):
            cols = slice(part * chunk, (part + 1) * chunk)
            for k in range(3):
                x = (c_rows if k == 2 else x_rows)[j, :, cols]
                dw_ref[j, k, cols] = dot_tn(x, inner_ref[k]).astype(BF)
        for r in range(nz):
            dw_copy(j, r).start()

        def back_tile(i, _, j=j):
            at = pl.ds(pl.multiple_of(i * tile, tile), tile)
            da, db, hg = inner_ref[0, at], inner_ref[1, at], inner_ref[2, at]
            c_rows[j, at] = dot_nt(hg, w_ref[j, 2]).astype(BF)
            x_rows[j, at] = (dot_nt(da, w_ref[j, 0]) + dot_nt(db, w_ref[j, 1])).astype(BF)
            return 0

        lax.fori_loop(0, blocks * CAP // tile, back_tile, 0)

    fit = width // length
    line = lax.broadcasted_iota(jnp.int32, (GATE_ROWS, width), 0)
    place = lax.broadcasted_iota(jnp.int32, (GATE_ROWS, width), 1) // length

    def spread(i, _):
        chosen = chosen_rows(i)
        low = one_hot(chosen)
        at = pl.ds(pl.multiple_of(i * CAP, CAP), CAP)
        both = []
        for rows_ref in (x_rows, c_rows):
            rows = [rows_ref[j, at] for j in range(experts)]
            both.append(rows[0] if experts == 1 else jnp.concatenate(rows, axis=0))
        n2_ref[i] = dot_tn(low, both[0]).astype(BF)
        c_ref[i, :length] = dot_tn(low, both[1]).astype(BF)
        tail = jnp.zeros((GATE_ROWS, width), F32)
        for j in range(experts):
            sums = jnp.where(chosen[j], grad_rows[j, at][:, :1], 0.0)
            wide = jnp.concatenate([jnp.sum(sums, axis=0, keepdims=True)] * fit, axis=1)
            number = ids[3] + j
            tail = tail + jnp.where((line == number // fit) & (place == number % fit), wide, 0.0)
        c_ref[i, length:] = tail.astype(BF)
        return 0

    def dn2_copy(g):
        return pltpu.make_async_copy(n2_ref.at[pl.ds(g * per, per)], dn2_out[g], dn2_sem.at[g])

    def y_copy(g):
        here = pl.ds((g % (groups // 2)) * per, per)
        return pltpu.make_async_copy(
            c_ref.at[pl.ds(g * per, per)], y_out[g // (groups // 2)].at[here], y_sem.at[g]
        )

    for g in range(groups):
        lax.fori_loop(g * per, (g + 1) * per, spread, 0, unroll=True)
        dn2_copy(g).start()
        y_copy(g).start()
    for g in range(groups):
        dn2_copy(g).wait()
        y_copy(g).wait()
    for j in range(experts):
        for r in range(nz):
            dw_copy(j, r).wait()


def mixture(ids, slots, gates, n2_groups, c_groups, weights):
    groups, nz = len(n2_groups), len(weights)
    per, length, width = n2_groups[0].shape
    blocks, experts, _ = slots.shape
    high, rows = c_groups[0].shape[1], blocks * CAP
    flat = [w for row in weights for w in row]
    w_parts = []
    for r, row in enumerate(weights):
        first = 0
        for w in row:
            w_parts.append((r, first, w.shape[1]))
            first += w.shape[1]
    part = flat[0].shape
    matrices = (part[0], 3) + part[2:]
    anywhere = pl.BlockSpec(memory_space=pl.ANY)
    outs = [jax.ShapeDtypeStruct((per, length, width), BF)] * groups
    outs += [jax.ShapeDtypeStruct((groups // 2 * per, high, width), BF)] * 2
    outs += [jax.ShapeDtypeStruct(matrices, BF)] * nz
    got = call(
        functools.partial(mixture_kernel, nz, tuple(w_parts), groups, per, experts, 640),
        (1,),
        ids,
        [slots, gates, *n2_groups, *c_groups, *flat],
        [whole_spec(slots.shape), whole_spec(gates.shape)] + [anywhere] * (2 * groups + len(flat)),
        outs,
        [anywhere] * len(outs),
        [
            pltpu.VMEM((blocks, length, width), BF),
            pltpu.VMEM((blocks, high, width), BF),
            pltpu.VMEM(matrices[:2] + (width,) + matrices[3:], BF),
            pltpu.VMEM((experts, rows, width), BF),
            pltpu.VMEM((experts, rows, width), BF),
            pltpu.VMEM((experts, rows, LANES), F32),
            pltpu.VMEM((experts, rows, LANES), F32),
            pltpu.VMEM((3, rows, part[-1]), BF),
            pltpu.VMEM(matrices[:2] + (width,) + matrices[3:], BF),
            pltpu.SemaphoreType.DMA((groups,)),
            pltpu.SemaphoreType.DMA((groups,)),
            pltpu.SemaphoreType.DMA((len(flat),)),
            pltpu.SemaphoreType.DMA((groups,)),
            pltpu.SemaphoreType.DMA((groups,)),
            pltpu.SemaphoreType.DMA((experts, nz)),
        ],
    )
    return got[:groups], got[groups : groups + 2], got[groups + 2 :]


def half_grads_kernel(nr, ids, own_rows, other_rows, gain_ref, dq_ref, own_ref, other_ref, grad_ref, normed_ref, acc_ref):
    chunk, qn, kn = grad_ref.shape[1], dq_ref.shape[1], own_ref.shape[2]
    step, count = pl.program_id(0), pl.num_programs(0)
    normalize(own_rows, other_rows, gain_ref, normed_ref)

    @pl.when(step == 0)
    def _():
        for r in range(nr):
            x = normed_ref[:, span(row_chunk(ids, r, nr), chunk)]
            grad_ref[r, :, :qn] = dot_tn(x[: dq_ref.shape[0]], dq_ref[...]).astype(BF)
        acc_ref[...] = jnp.zeros_like(acc_ref)

    def add(dkv_ref):
        grad = jnp.concatenate([dkv_ref[0], dkv_ref[1]], axis=1)
        for r in range(nr):
            acc_ref[r] += dot_tn(normed_ref[:, span(row_chunk(ids, r, nr), chunk)], grad)

    pl.when(step < count // 2)(lambda: add(own_ref))
    pl.when(step >= count // 2)(lambda: add(other_ref))

    @pl.when(step == count - 1)
    def _():
        for r in range(nr):
            grad_ref[r, :, qn:] = acc_ref[r].astype(BF)


def half_grads(ids, rows, gain, dq, dkv, half, nr, nh):
    slots, (length, width) = 2 * rows[0].shape[0], rows[0].shape[1:]
    qn, kn = H * HD // nh, KVH * HD // nh

    def body(ids, own_rows, other_rows, gain_ref, dq_ref, own_ref, other_ref, grad_ref, normed_ref, acc_ref):
        half_grads_kernel(
            nr, ids, own_rows, other_rows, gain_ref, dq_ref, own_ref, other_ref, grad_ref, normed_ref, acc_ref
        )

    def at(ids):
        return half_chunk(ids, half, nh)

    out = jax.ShapeDtypeStruct((nr, width // nr, qn + 2 * kn), BF)
    tile, steps = BLOCKS * length, slots // BLOCKS
    middle = steps // 2
    return call(
        body,
        (steps,),
        ids,
        [*flat_rows(rows), gain, dq, *dkv],
        [
            *rows_specs(steps, (tile, width)),
            whole_spec(gain.shape),
            pl.BlockSpec((length, qn), lambda i, ids: (0, at(ids))),
            pl.BlockSpec((2, tile, kn), lambda i, ids: (0, jnp.minimum(i, middle - 1), at(ids))),
            pl.BlockSpec((2, tile, kn), lambda i, ids: (0, jnp.maximum(i - middle, 0), at(ids))),
        ],
        out,
        whole_spec(out.shape),
        [pltpu.VMEM((tile, width), BF), pltpu.VMEM((nr, width // nr, 2 * kn), F32)],
    )


def rows_back_kernel(nr, nh, ids, dq_ref, dkv_ref, x_ref, dx2_ref, gain_ref, *rest):
    weights = rest[:nh]
    out_ref, grad_ref, low_ref = rest[nh:]
    width = x_ref.shape[1]
    chunk = width // nr
    qn, kn = H * HD // nh, KVH * HD // nh
    at_q, at_k, at_v, at_end = columns(nh, width)
    low_ref[...] = dkv_ref[...].astype(BF)
    for r in range(nr):
        total = None
        for h in range(nh):
            at = half_chunk(ids, h, nh)
            weight = weights[h]
            part = dot_nt(dq_ref[:, span(at, qn)], weight[r, :, at_q:at_k])
            part = part + dot_nt(low_ref[0, :, span(at, kn)], weight[r, :, at_k:at_v])
            part = part + dot_nt(low_ref[1, :, span(at, kn)], weight[r, :, at_v:at_end])
            total = part if total is None else total + part
        grad_ref[:, span(row_chunk(ids, r, nr), chunk)] = total
    x = x_ref[...]
    scaled = grad_ref[...] * gain_ref[...]
    inverse = lax.rsqrt(jnp.mean(x * x, axis=1, keepdims=True) + EPSILON)
    inner = jnp.mean(scaled * x, axis=1, keepdims=True)
    out_ref[...] = dx2_ref[...] + inverse * scaled - x * (inverse * inverse * inverse * inner)


def rows_back(ids, dq, dkv, x, dx2, gain, weights):
    nr, nh = weights[0].shape[0], len(weights)
    ins = [dq, dkv, x, dx2, gain, *weights]
    return call(
        functools.partial(rows_back_kernel, nr, nh),
        (1,),
        ids,
        ins,
        [whole_spec(i.shape) for i in ins],
        jax.ShapeDtypeStruct(x.shape, F32),
        whole_spec(x.shape),
        [pltpu.VMEM(x.shape, F32), pltpu.VMEM(dkv.shape, BF)],
    )


def swap(value, axis, distance):
    count = lax.axis_size(axis)
    return lax.ppermute(value, axis, [(i, i ^ distance) for i in range(count)])


def after(value, *done):
    return lax.optimization_barrier((value,) + done)[0]


def together(*values):
    return lax.optimization_barrier(values)


def pick(array, index):
    return lax.dynamic_index_in_dim(array, index, 0, keepdims=False)


def gather_z(value):
    chips = lax.axis_size("shard") // 2
    if chips != 4:
        return [value] + [swap(value, "shard", 2 * r) for r in range(1, chips)]
    near, far = swap(value, "shard", 2), swap(value, "shard", 4)
    return [value, near, far, swap(far, "shard", 2)]


def scatter_z(parts):
    total = parts[0].astype(F32)
    for r in range(1, len(parts)):
        total = total + swap(parts[r], "shard", 2 * r).astype(F32)
    return total


def in_order(mine, other, core, axis):
    return jnp.where(
        core == 0,
        jnp.concatenate([mine, other], axis=axis),
        jnp.concatenate([other, mine], axis=axis),
    )


def add_low(*values):
    total = values[0].astype(F32)
    for value in values[1:]:
        total = total + value.astype(F32)
    return total.astype(BF)


def body(
    tokens,
    block_ids,
    routes,
    gates,
    attn_gain,
    w_query,
    w_key,
    w_value,
    w_out,
    moe_gain,
    w_gate,
    w_up,
    w_down,
    cotangent,
):
    length, width = tokens.shape[1], tokens.shape[2]
    n_expert, n_shard = lax.axis_size("expert"), lax.axis_size("shard")
    chips = n_shard // 2
    local = w_gate.shape[0]
    fast = n_expert == 4 and n_shard == 8 and local % 4 == 0
    sides = 2 if fast else 1
    experts = local // (2 * sides)
    e, s = lax.axis_index("expert"), lax.axis_index("shard")
    z, core = s // 2, s % 2
    side = z // 2 if fast else 0
    first_expert = e * local + core * (local // 2) + side * experts
    ids = jnp.stack([e, z, core, first_expert]).astype(jnp.int32)
    nh = 2 if fast else 1

    x = tokens[0]
    c = cotangent[0]

    inverse_one = lax.rsqrt(jnp.mean(x * x, axis=-1, keepdims=True) + EPSILON)
    scaled_rows = (x * inverse_one).astype(BF)

    def halves(matrix):
        low = matrix.astype(BF)
        return low.reshape(low.shape[0], nh, low.shape[1] // nh).transpose(1, 0, 2)

    def column(gain):
        return jnp.broadcast_to(gain.astype(BF)[None, :, None], (nh, gain.shape[0], LANES // 2))

    packed = jnp.concatenate(
        [halves(w_out), halves(w_query), halves(w_key), halves(w_value), column(attn_gain), column(moe_gain)],
        axis=2,
    )
    at_q, at_k, at_v, at_end = columns(nh, width)

    numbers = jnp.arange(EXPERTS, dtype=jnp.int32)
    lines = EXPERTS * length // width

    def positions(start):
        s_late = after(s, start)
        owners = jnp.stack([s_late ^ (2 * r + k) for k in range(2) for r in range(chips)])
        angles = (owners * length).astype(F32)[:, None] * jnp.asarray(frequencies(), F32)[None, :]
        cosine, sine = jnp.cos(angles), jnp.sin(angles)
        every = block_ids[0].reshape(n_shard, length)
        key_blocks = jnp.concatenate(
            [pick(every, s_late ^ (2 * r + k)) for k in range(2) for r in range(chips)]
        )
        own_blocks = pick(every, s_late)
        lanes = jnp.arange(LANES, dtype=jnp.int32)[None, :]
        key_extra = ((lanes == key_blocks[:, None]) | ((lanes >= 16) & (lanes < 19))).astype(BF)
        query_extra = jnp.where((lanes < 16) & (lanes > own_blocks[:, None]), -1e30, 0.0).astype(BF)
        return cosine, sine, key_extra, query_extra

    def named_experts(routed):
        return routed[0][None, :, :] == numbers[:, None, None]

    def cotangent_rows(start):
        value, routed, gated = after((c, routes, gates), start)
        dense = jnp.sum(jnp.where(named_experts(routed), gated[0][None, :, :], 0.0), axis=-1)
        dense = dense.reshape(lines, width)
        high = dense.astype(BF)
        low = (dense - high.astype(F32)).astype(BF)
        return jnp.concatenate([value.astype(BF), high, low], axis=0)

    def own_experts(start):
        low = jnp.stack([m.astype(BF) for m in after((w_gate, w_up, w_down), start)], axis=1)
        low = low.reshape((2, local // 2) + low.shape[1:])
        return pick(low, core), swap(pick(low, 1 - core), "shard", 1)

    def over_columns(value):
        return [swap(value, "expert", r) for r in range(1, n_expert)]

    if fast:
        mine, other = pick(packed, core), pick(packed, 1 - core)
        chip = in_order(mine, swap(other, "shard", 1), core, 0)

    if fast:
        w_near, w_far = swap(chip, "shard", 2), swap(chip, "shard", 4)
        stacked = jnp.stack([chip, w_near, w_far, swap(w_far, "shard", 2)])
        block = jnp.concatenate([pick(stacked, z ^ i) for i in range(chips)], axis=0)
        c_pack = cotangent_rows(chip)
        w_mine, w_other = own_experts(chip)
        cosine, sine, key_extra, query_extra = positions(chip)
        w_got = over_columns(after(block, w_other))
        x_late = after(scaled_rows, block)
        x_near, x_far = swap(x_late, "shard", 2), swap(x_late, "shard", 4)
        x_cross = swap(x_far, "shard", 2)
        c_far = swap(after(c_pack, x_far), "shard", 4)
        chip_w = in_order(after(w_mine, x_cross), w_other, core, 2)
        chip_w = chip_w.reshape((2, experts, 3, 2 * w_gate.shape[1], w_gate.shape[2]))
        here, there = pick(chip_w, side), pick(chip_w, 1 - side)
        there = [there[:, k : k + 1] for k in range(3)]
        own_core = jnp.stack([scaled_rows, x_near, x_far, x_cross])
        x_other = swap(own_core, "shard", 1)
        rows = [own_core, x_other]
        early = (own_core, c_far, cosine, sine, key_extra, query_extra)
        w_got = [after(got, *early) for got in w_got]
        blocks = jnp.stack([block] + w_got)
        gain_cols = blocks[:, :, at_end:]
        gain_cols = jnp.concatenate([pick(gain_cols, e ^ i) for i in range(n_expert)], axis=0)
        attn_other, near_a, far_a, gain_one, gain_two, ids = together(
            swap(blocks, "shard", 1),
            here[:, :1],
            there[0],
            gain_cols[:, 0].astype(F32)[None],
            gain_cols[:, LANES // 2].astype(F32)[None],
            ids,
        )
        attn_w = [blocks, attn_other]
        near_a, far_a = swap(near_a, "shard", 2), swap(far_a, "shard", 4)
        c_own_got = over_columns(after(c_pack, attn_w[1]))
    else:
        c_pack = cotangent_rows(packed)
        own_core = jnp.stack(gather_z(scaled_rows))
        rows = [own_core, swap(own_core, "shard", 1)]
        cosine, sine, key_extra, query_extra = positions(packed)
        blocks = lax.all_gather(packed[0], ("expert", "shard"), axis=0, tiled=True)
        attn_w = [blocks[None]]
        gain_cols = blocks[:, at_end:]
        expert_w = gather_z(in_order(*own_experts(packed), core, 2))
        gain_one = gain_cols[:, 0].astype(F32)[None]
        gain_two = gain_cols[:, LANES // 2].astype(F32)[None]
    nr = attn_w[0].shape[0]

    q, k, v, cosine, sine = project(ids, rows, gain_one, cosine, sine, attn_w)
    if fast:
        c_far_got = over_columns(after(c_far, q))
        q, near_a, far_a, *c_own_got = together(q, near_a, far_a, *c_own_got)
        near_b = swap(after(here[:, 1:], q), "shard", 2)
        far_b = swap(after(there[1], q), "shard", 4)
        c_own = jnp.stack([c_pack] + c_own_got)
    mixed, mixed_low, lse = attend(ids, q, k, v, key_extra, query_extra)
    x2, n2 = project_out(ids, x, mixed_low, gain_two, attn_w)

    def places_of(groups):
        tails = jnp.concatenate([group[:, length:] for group in groups], axis=0).astype(F32)
        dense = (tails[:, :lines] + tails[:, lines:]).reshape(-1, EXPERTS, length)
        gate_here = lax.dynamic_slice_in_dim(dense, first_expert, experts, 1)
        chosen = gate_here > 0.0
        before = jnp.triu(jnp.ones((length, length), BF), 1)
        ranks = jnp.einsum("net,tu->neu", chosen.astype(BF), before, preferred_element_type=F32)
        return gate_here, jnp.where(chosen, ranks, -1.0)

    if fast:
        n2, near_b, far_b, *c_far_got = together(n2, near_b, far_b, *c_far_got)
        n2_far = swap(n2, "shard", 4)
        n2_own_got = over_columns(n2)
        cross_a = swap(after(far_a, n2), "shard", 2)
        n2_far, cross_a, *n2_own_got = together(n2_far, cross_a, *n2_own_got)
        cross_b = swap(after(far_b, n2_far), "shard", 2)
        n2_far_got = over_columns(n2_far)
        far_c = swap(after(there[2], n2_far), "shard", 4)
        n2_own = jnp.stack([n2] + n2_own_got)
        c_across = jnp.stack([after(piece, n2_far) for piece in [c_far, *c_far_got]])
        far_c, cross_b, n2_own, c_across, *n2_far_got = together(
            far_c, cross_b, n2_own, c_across, *n2_far_got
        )
        n2_across = jnp.stack([n2_far] + n2_far_got)
        cross_c = swap(far_c, "shard", 2)
        n2_groups = [n2_own, n2_across, swap(n2_own, "shard", 1), swap(n2_across, "shard", 1)]
        c_groups = [c_own, c_across] + [swap(after(g, far_c), "shard", 1) for g in (c_own, c_across)]
        gate_here, slots = places_of(c_groups)
        expert_w = [[here], [near_a, near_b], [far_a, far_b, far_c], [cross_a, cross_b, cross_c]]
        dn2_parts, y_parts, d_experts = mixture(
            ids, slots, gate_here, n2_groups, c_groups, expert_w
        )
        step = swap(d_experts[3], "shard", 2)
        dn2_other = [swap(dn2_parts[3], "shard", 1), swap(dn2_parts[2], "shard", 1)][::-1]
        far_sums = add_low(dn2_parts[1], dn2_other[1])
        own_sums = add_low(dn2_parts[0], dn2_other[0])
        far_got = [swap(far_sums[r], "expert", r) for r in range(1, n_expert)]
        dn2_far = add_low(far_sums[0], *[after(got, own_sums, step) for got in far_got])
        dn2_got = swap(dn2_far, "shard", 4)
        own_got = [swap(after(own_sums[r], dn2_far), "expert", r) for r in range(1, n_expert)]
        d_far = add_low(d_experts[2], after(step, dn2_far))
        y_sum = add_low(y_parts[0], swap(after(y_parts[1], dn2_far), "shard", 1))
        y_sum = y_sum.reshape((2, n_expert) + y_sum.shape[1:])
        far_early, near_early = after((d_far[:, :1], d_experts[1][:, :1]), dn2_got)
        own_got = [after(got, far_early, near_early, y_sum) for got in own_got]
        dn2 = sum([g.astype(F32) for g in own_got + [dn2_got]], own_sums[0].astype(F32))
    else:
        c_own = jnp.stack([c_pack] + over_columns(c_pack))
        c_groups = [c_own, swap(c_own, "shard", 1)]
        gate_here, slots = places_of(c_groups)
        n2_own = jnp.stack([n2] + over_columns(n2))
        n2_groups = [n2_own, swap(n2_own, "shard", 1)]
        c_rows, gate_rows = gather_rows(ids, slots, c_groups, gate_here)
        (x_rows,) = gather_rows(ids, slots, n2_groups)
        flat = (experts, slots.shape[0] * CAP)
        y_rows, dx_rows, grad_rows, d_experts = run_experts(
            ids,
            x_rows.reshape(flat + (width,)),
            c_rows.reshape(flat + (width,)),
            gate_rows.reshape(flat + (LANES,)),
            expert_w,
        )
        split = (experts, slots.shape[0], CAP)
        dn2_parts = spread_rows(ids, slots, dx_rows.reshape(split + (width,)), 2)
        y_parts = spread_rows(
            ids, slots, y_rows.reshape(split + (width,)), 2, grad_rows.reshape(split + (LANES,))
        )
        own_sums = add_low(dn2_parts[0], swap(dn2_parts[1], "shard", 1))
        own_got = [swap(own_sums[r], "expert", r) for r in range(1, n_expert)]
        dn2 = sum([g.astype(F32) for g in own_got], own_sums[0].astype(F32))
        y_sum = add_low(y_parts[0], swap(y_parts[1], "shard", 1))[None]

    dx2, d_mixed, d_out_w = project_out_back(ids, c, x2, gain_two, dn2, mixed_low, attn_w)
    args = (mixed, lse, k, v, key_extra, query_extra, cosine, sine)
    if fast:
        d_out_sums = add_low(d_out_w[0], swap(d_out_w[1], "shard", 1))
        far_a, near_a = swap(far_early, "shard", 4), swap(near_early, "shard", 2)
        y_got = [swap(after(y_sum[1, r], dn2), "expert", r) for r in range(1, n_expert)]
        done = attend_back(ids, q, after(d_mixed, d_out_sums), *args, 1)
        y_across = add_low(y_sum[1, 0], *[after(g, done[0]) for g in y_got])
        dq = after(done[0], y_across, far_a, near_a)
        far_b = swap(after(d_far[:, 1:], dq), "shard", 4)
        near_b = swap(after(d_experts[1][:, 1:], dq), "shard", 2)
        both = jnp.concatenate([y_sum[0], after(d_out_sums, dq)], axis=1)
        both_got = [swap(both[r], "expert", r) for r in range(1, n_expert)]
        d_other = half_grads(ids, rows, gain_one, dq, done[1:], 1, nr, nh)
        dq, *dkv = attend_back(ids, q, after(d_mixed, d_other), *args, 0, done)
        dq, far_b, near_b, *parts = together(dq, far_b, near_b, *dkv, *both_got)
        dkv, both_got = parts[:2], parts[2:]
        d_other = swap(after(d_other, dq), "shard", 1)
        y_far = swap(after(y_across, dq), "shard", 4)
    else:
        dq, *dkv = attend_back(ids, q, d_mixed, *args)
        y_got = [swap(y_sum[0, r], "expert", r) for r in range(1, n_expert)]
    dkv_core = swap(dkv[1], "shard", 1)
    d_own = half_grads(ids, rows, gain_one, dq, dkv, 0, nr, nh)
    if fast:
        d_own, d_other, dkv_core = together(d_own, d_other, dkv_core)
    dkv_sums = add_low(dkv[0], dkv_core)
    dkv_parts = [dkv_sums[:, r * length : (r + 1) * length] for r in range(chips)]
    if fast:
        sums = add_low(d_own, d_other)
        dkv_step = swap(dkv_parts[3], "shard", 2)
        dkv_far = add_low(dkv_parts[2], dkv_step)
        sums, y_far, dkv_far = together(sums, y_far, dkv_far)
        got = [swap(sums[r], "expert", r) for r in range(1, n_expert)]
        dkv_far = swap(dkv_far, "shard", 4)
        dkv_near = swap(after(dkv_parts[1], dkv_step), "shard", 2)
        dkv_near, dkv_far, *got = together(dkv_near, dkv_far, *got)
        both = sum([g.astype(F32) for g in both_got], both[0].astype(F32))
        y_out, d_out_total = both[: y_sum.shape[2]], both[y_sum.shape[2] :].astype(BF)
        cols = width // nh
        high = d_out_total.shape[0] - GATE_ROWS
        gain_grad = d_out_total[high, : width // n_expert]
        d_out_total = jnp.concatenate(
            [d_out_total[:high, f * cols : (f + 1) * cols] for f in range(nh)], axis=0
        )
        gain_grad = jnp.broadcast_to(gain_grad[:, None], (gain_grad.shape[0], LANES))
        d_out_total = jnp.concatenate([d_out_total, gain_grad], axis=1)
        dkv_own = sum([g.astype(F32) for g in (dkv_near, dkv_far)], dkv_parts[0].astype(F32))
        d_total = add_low(sums[0], *got)
        total = jnp.concatenate([d_out_total, d_total], axis=1)
        total = total.reshape(chips, total.shape[0] // chips, total.shape[1])
        total = [pick(total, z ^ r) for r in range(chips)]
        step, near = swap(total[3], "shard", 2), swap(total[1], "shard", 2)
        far = swap(add_low(total[2], step), "shard", 4)
        token_grad = rows_back(ids, dq, dkv_own, x, dx2, gain_one, attn_w)
        summed = total[0].astype(F32) + near.astype(F32) + after(far, token_grad).astype(F32)
        summed = summed.reshape(2, summed.shape[0] // 2, summed.shape[1])
        mine = pick(summed, core)
        other = swap(pick(summed, 1 - core).astype(BF), "shard", 1).astype(F32)
        parts = (jnp.where(core == 0, mine, other), jnp.where(core == 0, other, mine))
        out_sum = y_out + after(y_far, far).astype(F32)
    else:
        out_sum = sum([g.astype(F32) for g in y_got], y_sum[0, 0].astype(F32))
        dkv_own = scatter_z(dkv_parts)
        token_grad = rows_back(ids, dq, dkv_own, x, dx2, gain_one, attn_w)
        gain_grad = jnp.broadcast_to(d_out_w[0][0, width][:, None], (width, LANES))
        joined = jnp.concatenate([d_out_w[0][0, :width], gain_grad, d_own[0]], axis=1)
        joined = lax.psum_scatter(joined, ("expert", "shard"), scatter_dimension=0, tiled=True)
        parts = [joined.astype(F32)]

    on, qn, kn = width // nh, H * HD // nh, KVH * HD // nh
    start = on + LANES
    d_out_full = jnp.concatenate([p[:, :on] for p in parts], axis=1)
    d_gain_two = parts[0][:, on]
    d_query_w = jnp.concatenate([p[:, start : start + qn] for p in parts], axis=1)
    d_key_w = jnp.concatenate([p[:, start + qn : start + qn + kn] for p in parts], axis=1)
    d_value_w = jnp.concatenate([p[:, start + qn + kn :] for p in parts], axis=1)
    row_sums = (
        jnp.sum(w_query.astype(BF).astype(F32) * d_query_w, axis=1)
        + jnp.sum(w_key.astype(BF).astype(F32) * d_key_w, axis=1)
        + jnp.sum(w_value.astype(BF).astype(F32) * d_value_w, axis=1)
    )
    d_gain_one = row_sums / attn_gain.astype(BF).astype(F32)

    output = x2 + out_sum[:length]
    gate_sums = out_sum[length : length + lines].reshape(EXPERTS, length)
    gate_grad = jnp.sum(jnp.where(named_experts(routes), gate_sums[:, :, None], 0.0), axis=0)

    if fast:
        there_sum = jnp.concatenate([far_a, far_b], axis=1).astype(F32)
        here_sum = d_experts[0].astype(F32)
        here_sum = here_sum + jnp.concatenate([near_a, near_b], axis=1).astype(F32)
        d_chip = jnp.where(
            side == 0,
            jnp.concatenate([here_sum, there_sum], axis=0),
            jnp.concatenate([there_sum, here_sum], axis=0),
        )
    else:
        d_chip = scatter_z(d_experts)
    half = d_chip.shape[2] // 2
    d_chip = d_chip.astype(BF)
    if fast:
        d_chip = after(d_chip, *got)
    mine = lax.dynamic_slice_in_dim(d_chip, core * half, half, 2)
    other = swap(lax.dynamic_slice_in_dim(d_chip, (1 - core) * half, half, 2), "shard", 1)
    if fast:
        other = after(other, dkv_own)
    d_expert = in_order(mine, other, core, 0).astype(F32)

    return (
        output[None],
        token_grad[None],
        gate_grad[None],
        d_gain_one,
        d_query_w,
        d_key_w,
        d_value_w,
        d_out_full,
        d_gain_two,
        d_expert[:, 0],
        d_expert[:, 1],
        d_expert[:, 2],
    )


def solution(mesh):
    rows = P("expert", "shard", None)
    split = P(("expert", "shard"), None)
    gain = P(("expert", "shard"))
    in_specs = (
        rows, P("expert", None), rows, rows, gain, split, split, split, split, gain, rows, rows, rows, rows,
    )
    out_specs = (rows, rows, rows, gain, split, split, split, split, gain, rows, rows, rows)
    return jax.shard_map(body, mesh=mesh, in_specs=in_specs, out_specs=out_specs, check_vma=False)
```

```python
import functools

import jax
import jax.numpy as jnp
import numpy as np
from jax import lax
from jax.experimental import pallas as pl
from jax.experimental.pallas import tpu as pltpu
from jax.sharding import PartitionSpec as P

H = 16
KVH = 8
HD = 64
EXPERTS = 32
TOP = 8
CAP = 80
EPSILON = 1e-06
LANES = 128
PAIRS = KVH // 2
BLOCKS = 2
GATE_ROWS = 16

BF = jnp.bfloat16
F32 = jnp.float32
VMEM_BYTES = 56 * 1024 * 1024


def dot(left, right):
    return lax.dot_general(left, right, (((1,), (0,)), ((), ())), preferred_element_type=F32)


def dot_nt(left, right):
    return lax.dot_general(left, right, (((1,), (1,)), ((), ())), preferred_element_type=F32)


def dot_tn(left, right):
    return lax.dot_general(left, right, (((0,), (0,)), ((), ())), preferred_element_type=F32)


def call(kernel, grid, scalars, inputs, in_specs, out_shapes, out_specs, scratch=(), aliases=None):
    return pl.pallas_call(
        kernel,
        grid_spec=pltpu.PrefetchScalarGridSpec(
            num_scalar_prefetch=1,
            grid=grid,
            in_specs=in_specs,
            out_specs=out_specs,
            scratch_shapes=list(scratch),
        ),
        out_shape=out_shapes,
        input_output_aliases=aliases or {},
        compiler_params=pltpu.CompilerParams(vmem_limit_bytes=VMEM_BYTES),
        cost_estimate=pl.CostEstimate(flops=0, bytes_accessed=0, transcendentals=0),
    )(scalars, *inputs)


def whole_spec(shape):
    return pl.BlockSpec(tuple(shape), lambda *_: (0,) * len(shape))


def lane_ids(rows):
    return lax.broadcasted_iota(jnp.int32, (rows, LANES), 1)


def swap_halves(tile):
    first = lane_ids(tile.shape[0]) % HD < HD // 2
    return jnp.where(first, pltpu.roll(tile, LANES - HD // 2, 1), pltpu.roll(tile, HD // 2, 1))


def turn(value, cosine, signed_sine, direction):
    tiles = []
    for i in range(value.shape[1] // LANES):
        tile = value[:, i * LANES : (i + 1) * LANES]
        tiles.append(tile * cosine + direction * (swap_halves(tile) * signed_sine))
    return tiles[0] if len(tiles) == 1 else jnp.concatenate(tiles, axis=1)


def row_chunk(ids, r, count):
    return ids[0] ^ r if count > 1 else 0


def z_chunk(ids, r, count):
    return ids[1] ^ r if count > 1 else 0


def half_chunk(ids, h, count):
    return ids[2] ^ h if count > 1 else 0


def span(index, size):
    return pl.ds(pl.multiple_of(index * size, size), size)


def columns(nh, width):
    on, qn, kn = width // nh, H * HD // nh, KVH * HD // nh
    return on, on + qn, on + qn + kn, on + qn + 2 * kn


def frequencies():
    return np.tile(10000.0 ** (-np.arange(HD // 2) * 2.0 / HD), 2 * LANES // HD)


def place_tables(length):
    angles = np.arange(length)[:, None] * frequencies()[None, :]
    return np.cos(angles).astype(np.float32), np.sin(angles).astype(np.float32)


def qkv_kernel(nr, nh, ids, own_ref, other_ref, gain_ref, cos_ref, sin_ref, slot_cos, slot_sin, *rest):
    weights = rest[:nh]
    q_ref, k_ref, v_ref, cos_out, sin_out, normed_ref = rest[nh:]
    width = own_ref.shape[-1]
    chunk = width // nr
    qn, kn = H * HD // nh, KVH * HD // nh
    at_q, at_k, _, at_end = columns(nh, width)
    normalize(own_ref, other_ref, gain_ref, normed_ref)
    length = cos_ref.shape[0]
    sign = jnp.where(lane_ids(length) % HD < HD // 2, -1.0, 1.0)
    for b in range(cos_out.shape[0] // length):
        slot = pl.ds(pl.program_id(0) * (cos_out.shape[0] // length) + b, 1)
        c, s = slot_cos[slot], slot_sin[slot]
        at = slice(b * length, (b + 1) * length)
        cos_out[at] = cos_ref[...] * c - sin_ref[...] * s
        sin_out[at] = sign * (sin_ref[...] * c + cos_ref[...] * s)
    cosine, sine = cos_out[...], sin_out[...]
    for h in range(nh):
        total = None
        for r in range(nr):
            part = dot(
                normed_ref[:, span(row_chunk(ids, r, nr), chunk)],
                weights[h][r, :, at_k:at_end],
            )
            total = part if total is None else total + part
        here = span(half_chunk(ids, h, nh), kn)
        k_ref[:, here] = turn(total[:, :kn], cosine, sine, 1.0).astype(BF)
        v_ref[:, here] = total[:, kn:].astype(BF)

    rows = q_ref.shape[0]

    @pl.when(pl.program_id(0) == 0)
    def _():
        for h in range(nh):
            total = None
            for r in range(nr):
                part = dot(
                    normed_ref[:rows, span(row_chunk(ids, r, nr), chunk)], weights[h][r, :, at_q:at_k]
                )
                total = part if total is None else total + part
            turned = turn(total, cosine[:rows], sine[:rows], 1.0).astype(BF).astype(F32) * HD**-0.5
            q_ref[:, span(half_chunk(ids, h, nh), qn)] = turned.astype(BF)


def normalize(own_ref, other_ref, gain_ref, normed_ref):
    own = pl.program_id(0) < pl.num_programs(0) // 2
    rows = jnp.where(own, own_ref[...], other_ref[...])
    normed_ref[...] = (rows.astype(F32) * gain_ref[...]).astype(BF)


def rows_specs(steps, shape):
    half = steps // 2
    return [
        pl.BlockSpec(shape, lambda i, _: (jnp.minimum(i, half - 1), 0)),
        pl.BlockSpec(shape, lambda i, _: (jnp.maximum(i - half, 0), 0)),
    ]


def flat_rows(rows):
    return [part.reshape(-1, part.shape[-1]) for part in rows]


def project(ids, rows, gain, cosine, sine, weights):
    slots, (length, width) = 2 * rows[0].shape[0], rows[0].shape[1:]
    nr, nh = weights[0].shape[0], len(weights)
    tile, steps = BLOCKS * length, slots // BLOCKS
    tables = [jnp.asarray(t) for t in place_tables(length)]
    return call(
        functools.partial(qkv_kernel, nr, nh),
        (steps,),
        ids,
        [*flat_rows(rows), gain, *tables, cosine, sine, *weights],
        [
            *rows_specs(steps, (tile, width)),
            whole_spec(gain.shape),
            *[whole_spec(t.shape) for t in tables],
            whole_spec(cosine.shape),
            whole_spec(sine.shape),
            *[whole_spec(w.shape) for w in weights],
        ],
        [
            jax.ShapeDtypeStruct((length, H * HD), BF),
            jax.ShapeDtypeStruct((slots * length, KVH * HD), BF),
            jax.ShapeDtypeStruct((slots * length, KVH * HD), BF),
            jax.ShapeDtypeStruct((slots * length, LANES), F32),
            jax.ShapeDtypeStruct((slots * length, LANES), F32),
        ],
        [
            whole_spec((length, H * HD)),
            pl.BlockSpec((tile, KVH * HD), lambda i, _: (i, 0)),
            pl.BlockSpec((tile, KVH * HD), lambda i, _: (i, 0)),
            pl.BlockSpec((tile, LANES), lambda i, _: (i, 0)),
            pl.BlockSpec((tile, LANES), lambda i, _: (i, 0)),
        ],
        [pltpu.VMEM((tile, width), BF)],
    )


def to_half(tile, which, wanted):
    if which != wanted:
        tile = pltpu.roll(tile, HD, 1)
    return jnp.where(lane_ids(tile.shape[0]) // HD == wanted, tile, 0.0)


def attend_kernel(ids, q_ref, k_ref, v_ref, kx_ref, qx_ref, o_ref, low_ref, lse_ref):
    keys = jnp.concatenate([k_ref[...], kx_ref[...]], axis=1)
    values = v_ref[...]
    extra = qx_ref[...]
    rows = q_ref.shape[0]
    lanes = lane_ids(rows)
    sums = jnp.zeros((rows, LANES), F32)
    for t in range(2):
        tile = q_ref[:, t * LANES : (t + 1) * LANES].astype(F32)
        mixed = jnp.zeros((rows, LANES), F32)
        for w in range(2):
            query = jnp.concatenate([to_half(tile, w, t).astype(BF), extra], axis=1)
            scores = dot_nt(query, keys)
            highest = jnp.max(scores, axis=1, keepdims=True)
            weights = jnp.exp(scores - highest)
            total = jnp.sum(weights, axis=1, keepdims=True)
            out = dot(weights.astype(BF), values) / total
            mixed = mixed + to_half(out, t, w)
            sums = jnp.where(lanes == 2 * t + w, highest + jnp.log(total), sums)
        o_ref[:, t * LANES : (t + 1) * LANES] = mixed
        low_ref[:, t * LANES : (t + 1) * LANES] = mixed.astype(BF)
    lse_ref[0] = sums


def attend(ids, q, k, v, key_extra, query_extra):
    length, keys = q.shape[0], k.shape[0]
    quad = pl.BlockSpec((length, 2 * LANES), lambda p, _: (0, p))
    pair = pl.BlockSpec((keys, LANES), lambda p, _: (0, p))
    return call(
        attend_kernel,
        (PAIRS,),
        ids,
        [q, k, v, key_extra, query_extra],
        [quad, pair, pair, whole_spec(key_extra.shape), whole_spec(query_extra.shape)],
        [
            jax.ShapeDtypeStruct((length, H * HD), F32),
            jax.ShapeDtypeStruct((length, H * HD), BF),
            jax.ShapeDtypeStruct((PAIRS, length, LANES), F32),
        ],
        [quad, quad, pl.BlockSpec((1, length, LANES), lambda p, _: (p, 0, 0))],
    )


def three_parts(value):
    high = value.astype(BF)
    rest = value - high.astype(F32)
    middle = rest.astype(BF)
    return high.astype(F32), middle.astype(F32), (rest - middle.astype(F32))


def with_parts(base, value, lanes):
    high, middle, low = three_parts(value)
    base = jnp.where(lanes == 16, high, base)
    base = jnp.where(lanes == 17, middle, base)
    return jnp.where(lanes == 18, low, base).astype(BF)


def attend_back_kernel(
    span_rows, ids, q_ref, do_ref, o_ref, lse_ref, k_ref, v_ref, kx_ref, qx_ref, cos_ref, sin_ref,
    dq_ref, own_ref, other_ref, sum_ref,
):
    rows = q_ref.shape[0]
    lanes = lane_ids(rows)
    extra = qx_ref[...].astype(F32)
    nothing = jnp.zeros((rows, LANES), F32)
    sums = lse_ref[0]
    queries, outs, pads_q, pads_o = [], [], [], []
    for t in range(2):
        at = slice(t * LANES, (t + 1) * LANES)
        tile, grad = q_ref[:, at].astype(F32), do_ref[:, at].astype(F32)
        product = grad * o_ref[:, at]
        for w in range(2):
            here = lanes // HD == w
            delta = jnp.sum(jnp.where(here, product, 0.0), axis=1, keepdims=True)
            log_sum = jnp.sum(jnp.where(lanes == 2 * t + w, sums, 0.0), axis=1, keepdims=True)
            q_pad = to_half(tile, w, t).astype(BF)
            o_pad = to_half(grad, w, t).astype(BF)
            queries.append(jnp.concatenate([q_pad, with_parts(extra, -log_sum, lanes)], axis=1))
            outs.append(jnp.concatenate([o_pad, with_parts(nothing, -delta, lanes)], axis=1))
            pads_q.append(q_pad)
            pads_o.append(o_pad)
    all_q = jnp.concatenate(pads_q, axis=0)
    every_q = jnp.concatenate(queries, axis=0)
    every_o = jnp.concatenate(outs, axis=0)
    all_o = jnp.concatenate(pads_o, axis=0)
    sum_ref[...] = jnp.zeros_like(sum_ref)

    spans = k_ref.shape[0] // 2 // span_rows

    def one_span(i, _, part, out_ref):
        put = pl.ds(pl.multiple_of(i * span_rows, span_rows), span_rows)
        first = part * spans * span_rows
        at = pl.ds(pl.multiple_of(first + i * span_rows, span_rows), span_rows)
        k_here, x_here = k_ref[at, :], kx_ref[at, :]
        keys = jnp.concatenate([k_here, x_here], axis=1)
        values = jnp.concatenate([v_ref[at, :], x_here], axis=1)
        probs = jnp.exp(dot_nt(keys, every_q))
        d_scores = (probs * dot_nt(values, every_o)).astype(BF)
        sum_ref[...] += dot_tn(k_here, d_scores)
        out_ref[1, put, :] = dot(probs.astype(BF), all_o).astype(BF)
        d_key = dot(d_scores, all_q)
        d_key = turn(d_key, cos_ref[at, :], sin_ref[at, :], -1.0)
        out_ref[0, put, :] = d_key.astype(BF)
        return 0

    for part, out_ref in enumerate((own_ref, other_ref)):
        lax.fori_loop(0, spans, functools.partial(one_span, part=part, out_ref=out_ref), 0)
    cosine, sine = cos_ref[:rows, :], sin_ref[:rows, :]
    for t in range(2):
        d_query = [sum_ref[:, n * rows : (n + 1) * rows].T for n in (2 * t, 2 * t + 1)]
        tile = to_half(d_query[0], t, 0) + to_half(d_query[1], t, 1)
        turned = turn(tile * HD**-0.5, cosine, sine, -1.0)
        dq_ref[:, t * LANES : (t + 1) * LANES] = turned.astype(BF)


def attend_back_part(*refs):
    attend_back_kernel(1024, *refs[:11], *refs[14:])


def attend_back(ids, q, d_out, out, lse, k, v, key_extra, query_extra, cosine, sine, half=None, done=None):
    length, keys = q.shape[0], k.shape[0]
    count = PAIRS if half is None else PAIRS // 2

    def at(p, ids):
        return p if half is None else (ids[2] ^ half) * count + p

    quad = pl.BlockSpec((length, 2 * LANES), lambda p, ids: (0, at(p, ids)))
    pair = pl.BlockSpec((keys, LANES), lambda p, ids: (0, at(p, ids)))
    ins = [q, d_out, out, lse, k, v, key_extra, query_extra, cosine, sine]
    specs = [
        quad,
        quad,
        quad,
        pl.BlockSpec((1, length, LANES), lambda p, ids: (at(p, ids), 0, 0)),
        pair,
        pair,
        whole_spec(key_extra.shape),
        whole_spec(query_extra.shape),
        whole_spec(cosine.shape),
        whole_spec(sine.shape),
    ]
    if done is not None:
        ins += done
        specs += [pl.BlockSpec(memory_space=pl.ANY)] * 3
    return call(
        attend_back_part if done is not None else functools.partial(attend_back_kernel, 1024),
        (count,),
        ids,
        ins,
        specs,
        [
            jax.ShapeDtypeStruct((length, H * HD), BF),
            jax.ShapeDtypeStruct((2, keys // 2, KVH * HD), BF),
            jax.ShapeDtypeStruct((2, keys // 2, KVH * HD), BF),
        ],
        [quad] + [pl.BlockSpec((2, keys // 2, LANES), lambda p, ids: (0, 0, at(p, ids)))] * 2,
        [pltpu.VMEM((LANES, 4 * length), F32)],
        aliases={11: 0, 12: 1, 13: 2} if done is not None else None,
    )


def out_kernel(nr, nh, ids, x_ref, o_ref, gain_ref, *rest):
    weights = rest[:nh]
    x2_ref, n2_ref = rest[nh:]
    width = x_ref.shape[1]
    chunk, cols = H * HD // nr, width // nh
    for h in range(nh):
        at = span(half_chunk(ids, h, nh), cols)
        total = x_ref[:, at]
        for r in range(nr):
            total = total + dot(
                o_ref[:, span(row_chunk(ids, r, nr), chunk)], weights[h][r]
            )
        x2_ref[:, at] = total
    middle = x2_ref[...]
    inverse = lax.rsqrt(jnp.mean(middle * middle, axis=1, keepdims=True) + EPSILON)
    n2_ref[...] = (middle * inverse * gain_ref[...]).astype(BF)


def out_spec(weight, cols):
    return pl.BlockSpec(weight.shape[:2] + (cols,), lambda *_: (0, 0, 0))


def project_out(ids, x, low, gain, weights):
    nr, nh = weights[0].shape[0], len(weights)
    ins = [x, low, gain, *weights]
    outs = [jax.ShapeDtypeStruct(x.shape, F32), jax.ShapeDtypeStruct(x.shape, BF)]
    return call(
        functools.partial(out_kernel, nr, nh),
        (1,),
        ids,
        ins,
        [whole_spec(i.shape) for i in ins[:3]] + [out_spec(w, x.shape[1] // nh) for w in weights],
        outs,
        [whole_spec(o.shape) for o in outs],
    )


def out_back_kernel(nr, nh, ids, c_ref, x2_ref, gain_ref, dn2_ref, low_ref, *rest):
    weights = rest[:nh]
    dx2_ref, do_ref = rest[nh : nh + 2]
    grads = rest[nh + 2 : 2 * nh + 2]
    dr_ref, term_ref = rest[2 * nh + 2 :]
    width = c_ref.shape[1]
    chunk, cols = H * HD // nr, width // nh
    middle, d_normed = x2_ref[...], dn2_ref[...]
    inverse = lax.rsqrt(jnp.mean(middle * middle, axis=1, keepdims=True) + EPSILON)
    scaled = d_normed * gain_ref[...]
    inner = jnp.mean(scaled * middle, axis=1, keepdims=True)
    d_middle = c_ref[...] + inverse * scaled - middle * (inverse * inverse * inverse * inner)
    dx2_ref[...] = d_middle
    dr_ref[...] = d_middle.astype(BF)
    term_ref[...] = d_normed * middle * inverse
    fold = width // cols
    rows = chunk // fold
    for r in range(nr):
        at = span(row_chunk(ids, r, nr), chunk)
        low = low_ref[:, at]
        gain_grad = jnp.sum(term_ref[:, at], axis=0, keepdims=True)
        gain_grad = jnp.concatenate([gain_grad] * (width // chunk), axis=1)
        total = None
        for h in range(nh):
            branch = dr_ref[:, span(half_chunk(ids, h, nh), cols)]
            part = dot_nt(branch, weights[h][r])
            total = part if total is None else total + part
            grad = dot_tn(low, branch).astype(BF)
            for f in range(fold):
                grads[h][r, :rows, f * cols : (f + 1) * cols] = grad[f * rows : (f + 1) * rows]
            grads[h][r, rows:] = jnp.broadcast_to(gain_grad, (GATE_ROWS, width)).astype(BF)
        do_ref[:, at] = total.astype(BF)


def project_out_back(ids, c, x2, gain, dn2, low, weights):
    nr, nh = weights[0].shape[0], len(weights)
    ins = [c, x2, gain, dn2, low, *weights]
    rows, cols = H * HD // nr, c.shape[1] // nh
    outs = [jax.ShapeDtypeStruct(c.shape, F32), jax.ShapeDtypeStruct((c.shape[0], H * HD), BF)]
    high = rows * cols // c.shape[1] + GATE_ROWS
    outs += [jax.ShapeDtypeStruct((nr, high, c.shape[1]), BF)] * nh
    got = call(
        functools.partial(out_back_kernel, nr, nh),
        (1,),
        ids,
        ins,
        [whole_spec(i.shape) for i in ins[:5]] + [out_spec(w, cols) for w in weights],
        outs,
        [whole_spec(o.shape) for o in outs],
        [pltpu.VMEM(c.shape, BF), pltpu.VMEM(c.shape, F32)],
    )
    return got[0], got[1], got[2:]


def picks(slot_ref, experts):
    tokens = slot_ref.shape[-1]
    places = lax.broadcasted_iota(jnp.int32, (CAP, tokens), 0).astype(F32)
    rows = [places == slot_ref[0, j : j + 1, :] for j in range(experts)]
    return rows[0] if experts == 1 else jnp.concatenate(rows, axis=0)


def gather_kernel(groups, per, experts, with_gates, ids, slot_ref, *rest):
    if with_gates:
        gate_ref, rest = rest[0], rest[1:]
    tokens, out_ref = rest[:groups], rest[groups]
    chosen = picks(slot_ref, experts)
    low = chosen.astype(F32).astype(BF)
    for g in range(groups):

        @pl.when(pl.program_id(0) // per == g)
        def _(g=g):
            rows = dot(low, tokens[g][0, : slot_ref.shape[-1]]).astype(BF)
            for j in range(experts):
                out_ref[j, 0] = rows[j * CAP : (j + 1) * CAP]

    if with_gates:
        for j in range(experts):
            mine = chosen[j * CAP : (j + 1) * CAP]
            gates = jnp.sum(jnp.where(mine, gate_ref[0, j : j + 1, :], 0.0), axis=1, keepdims=True)
            rest[groups + 1][j, 0] = jnp.broadcast_to(gates, (CAP, LANES))


def gather_rows(ids, slots, groups, gates=None):
    blocks, experts, length = slots.shape
    per, width = groups[0].shape[0], groups[0].shape[-1]
    ins, specs = [slots], [pl.BlockSpec((1, experts, length), lambda i, _: (i, 0, 0))]
    if gates is not None:
        ins.append(gates)
        specs.append(specs[0])
    for g, tokens in enumerate(groups):
        ins.append(tokens)
        specs.append(
            pl.BlockSpec(
                (1,) + tokens.shape[1:], lambda i, _, g=g: (jnp.clip(i - g * per, 0, per - 1), 0, 0)
            )
        )
    outs = [jax.ShapeDtypeStruct((experts, blocks, CAP, width), BF)]
    out_specs = [pl.BlockSpec((experts, 1, CAP, width), lambda i, _: (0, i, 0, 0))]
    if gates is not None:
        outs.append(jax.ShapeDtypeStruct((experts, blocks, CAP, LANES), F32))
        out_specs.append(pl.BlockSpec((experts, 1, CAP, LANES), lambda i, _: (0, i, 0, 0)))
    return call(
        functools.partial(gather_kernel, len(groups), per, experts, gates is not None),
        (blocks,),
        ids,
        ins,
        specs,
        outs,
        out_specs,
    )


def expert_kernel(nz, ids, x_ref, c_ref, gate_ref, *rest):
    weights, rest = rest[:nz], rest[nz:]
    y_ref, dx_ref, gg_ref = rest[:3]
    grads, acc_ref = rest[3 : 3 + nz], rest[3 + nz]
    chunk = x_ref.shape[-1] // nz
    step, last = pl.program_id(1), pl.num_programs(1) - 1
    a = b = ch = None
    for r in range(nz):
        at = span(z_chunk(ids, r, nz), chunk)
        x, c = x_ref[0, :, at], c_ref[0, :, at]
        parts = (
            dot(x, weights[r][0, 0]),
            dot(x, weights[r][0, 1]),
            dot(c, weights[r][0, 2]),
        )
        a, b, ch = parts if a is None else (a + parts[0], b + parts[1], ch + parts[2])
    gate = gate_ref[0][:, :1]
    sig = 1.0 / (1.0 + jnp.exp(-a))
    act = a * sig
    hidden = (act * b).astype(BF).astype(F32)
    gg_ref[0] = jnp.broadcast_to(jnp.sum(hidden * ch, axis=1, keepdims=True), gg_ref.shape[1:])
    hg = (hidden * gate).astype(BF)
    dh = ch * gate
    da = (dh * b * sig * (1.0 + a * (1.0 - sig))).astype(BF)
    db = (dh * act).astype(BF)

    @pl.when(step == 0)
    def _():
        acc_ref[...] = jnp.zeros_like(acc_ref)

    for r in range(nz):
        at = span(z_chunk(ids, r, nz), chunk)
        x, c = x_ref[0, :, at], c_ref[0, :, at]
        y_ref[0, :, at] = dot_nt(hg, weights[r][0, 2]).astype(BF)
        dx_ref[0, :, at] = (dot_nt(da, weights[r][0, 0]) + dot_nt(db, weights[r][0, 1])).astype(BF)
        acc_ref[r, 0] += dot_tn(x, da)
        acc_ref[r, 1] += dot_tn(x, db)
        acc_ref[r, 2] += dot_tn(c, hg)

    @pl.when(step == last)
    def _():
        for r in range(nz):
            grads[r][0] = acc_ref[r].astype(BF)


def run_experts(ids, x_rows, c_rows, gate_rows, weights):
    experts, rows, width = x_rows.shape
    nz = len(weights)
    hidden = weights[0].shape[-1]
    tile = 256
    block = pl.BlockSpec((1, tile, width), lambda j, i, _: (j, i, 0))
    narrow = pl.BlockSpec((1, tile, LANES), lambda j, i, _: (j, i, 0))
    matrix = pl.BlockSpec((1,) + weights[0].shape[1:], lambda j, i, _: (j, 0, 0, 0))
    got = call(
        functools.partial(expert_kernel, nz),
        (experts, rows // tile),
        ids,
        [x_rows, c_rows, gate_rows, *weights],
        [block, block, narrow] + [matrix] * nz,
        [
            jax.ShapeDtypeStruct(x_rows.shape, BF),
            jax.ShapeDtypeStruct(x_rows.shape, BF),
            jax.ShapeDtypeStruct((experts, rows, LANES), F32),
        ]
        + [jax.ShapeDtypeStruct(w.shape, BF) for w in weights],
        [block, block, narrow] + [matrix] * nz,
        [pltpu.VMEM((nz,) + weights[0].shape[1:], F32)],
    )
    return got[0], got[1], got[2], got[3:]


def spread_kernel(groups, per, experts, with_grads, ids, slot_ref, rows_ref, *rest):
    if with_grads:
        grad_ref, rest = rest[0], rest[1:]
    chosen = picks(slot_ref, experts)
    low = chosen.astype(F32).astype(BF)
    rows = [rows_ref[j, 0] for j in range(experts)]
    rows = rows[0] if experts == 1 else jnp.concatenate(rows, axis=0)
    total = dot_tn(low, rows).astype(BF)
    length, width = total.shape
    tail = None
    if with_grads:
        fit = width // length
        line = lax.broadcasted_iota(jnp.int32, (GATE_ROWS, width), 0)
        place = lax.broadcasted_iota(jnp.int32, (GATE_ROWS, width), 1) // length
        tail = jnp.zeros((GATE_ROWS, width), F32)
        for j in range(experts):
            mine = chosen[j * CAP : (j + 1) * CAP]
            sums = jnp.sum(jnp.where(mine, grad_ref[j, 0][:, :1], 0.0), axis=0, keepdims=True)
            wide = jnp.concatenate([sums] * fit, axis=1)
            number = ids[3] + j
            tail = tail + jnp.where((line == number // fit) & (place == number % fit), wide, 0.0)
    for g in range(groups):

        @pl.when(pl.program_id(0) // per == g)
        def _(g=g):
            rest[g][0, :length] = total
            if with_grads:
                rest[g][0, length:] = tail.astype(BF)


def spread_rows(ids, slots, rows, groups, grads=None):
    blocks, experts, length = slots.shape
    per, width = blocks // groups, rows.shape[-1]
    high = length + (GATE_ROWS if grads is not None else 0)
    ins = [slots, rows]
    specs = [
        pl.BlockSpec((1, experts, length), lambda i, _: (i, 0, 0)),
        pl.BlockSpec((experts, 1, CAP, width), lambda i, _: (0, i, 0, 0)),
    ]
    if grads is not None:
        ins.append(grads)
        specs.append(pl.BlockSpec((experts, 1, CAP, LANES), lambda i, _: (0, i, 0, 0)))
    return call(
        functools.partial(spread_kernel, groups, per, experts, grads is not None),
        (blocks,),
        ids,
        ins,
        specs,
        [jax.ShapeDtypeStruct((per, high, width), BF)] * groups,
        [
            pl.BlockSpec(
                (1, high, width), lambda i, _, g=g: (jnp.clip(i - g * per, 0, per - 1), 0, 0)
            )
            for g in range(groups)
        ],
    )


def mixture_kernel(nz, w_parts, groups, per, experts, tile, ids, slot_ref, gate_ref, *rest):
    n2_in, rest = rest[:groups], rest[groups:]
    c_in, rest = rest[:groups], rest[groups:]
    w_in, rest = rest[: len(w_parts)], rest[len(w_parts) :]
    dn2_out, rest = rest[:groups], rest[groups:]
    y_out, rest = rest[: groups // 2], rest[groups // 2 :]
    dw_out, rest = rest[:nz], rest[nz:]
    n2_ref, c_ref, w_ref, x_rows, c_rows, gate_rows, grad_rows, inner_ref, dw_ref = rest[:9]
    n2_sem, c_sem, w_sem, dn2_sem, y_sem, dw_sem = rest[9:]
    length = slot_ref.shape[-1]
    width = n2_ref.shape[-1]
    chunk = width // nz
    blocks = groups * per

    def n2_copy(g):
        return pltpu.make_async_copy(n2_in[g], n2_ref.at[pl.ds(g * per, per)], n2_sem.at[g])

    def c_copy(g):
        return pltpu.make_async_copy(c_in[g], c_ref.at[pl.ds(g * per, per)], c_sem.at[g])

    def w_copy(n):
        r, first, count = w_parts[n]
        to = w_ref.at[:, pl.ds(first, count), span(z_chunk(ids, r, nz), chunk)]
        return pltpu.make_async_copy(w_in[n], to, w_sem.at[n])

    for g in range(groups):
        c_copy(g).start()
        n2_copy(g).start()
    for n in range(len(w_parts)):
        w_copy(n).start()

    def chosen_rows(i):
        places = lax.broadcasted_iota(jnp.int32, (CAP, length), 0).astype(F32)
        return [places == slot_ref[i, j : j + 1, :] for j in range(experts)]

    def one_hot(chosen):
        chosen = [jnp.where(c, 1.0, 0.0).astype(BF) for c in chosen]
        return chosen[0] if experts == 1 else jnp.concatenate(chosen, axis=0)

    def gather(i, _):
        chosen = chosen_rows(i)
        low = one_hot(chosen)
        at = pl.ds(pl.multiple_of(i * CAP, CAP), CAP)
        got_x = dot(low, n2_ref[i]).astype(BF)
        got_c = dot(low, c_ref[i, :length]).astype(BF)
        for j in range(experts):
            x_rows[j, at] = got_x[j * CAP : (j + 1) * CAP]
            c_rows[j, at] = got_c[j * CAP : (j + 1) * CAP]
            gates = jnp.where(chosen[j], gate_ref[i, j : j + 1, :], 0.0)
            gate_rows[j, at] = jnp.broadcast_to(jnp.sum(gates, axis=1, keepdims=True), (CAP, LANES))
        return 0

    for g in range(groups):
        c_copy(g).wait()
        n2_copy(g).wait()
        lax.fori_loop(g * per, (g + 1) * per, gather, 0, unroll=True)
    for n in range(len(w_parts)):
        w_copy(n).wait()

    def dw_copy(j, r):
        rows = span(z_chunk(ids, r, nz), chunk)
        return pltpu.make_async_copy(dw_ref.at[j, :, rows], dw_out[r].at[j], dw_sem.at[j, r])

    for j in range(experts):

        def one_tile(i, _, j=j):
            at = pl.ds(pl.multiple_of(i * tile, tile), tile)
            x, c = x_rows[j, at], c_rows[j, at]
            a, b, ch = dot(x, w_ref[j, 0]), dot(x, w_ref[j, 1]), dot(c, w_ref[j, 2])
            gate = gate_rows[j, at][:, :1]
            sig = 1.0 / (1.0 + jnp.exp(-a))
            act = a * sig
            hidden = (act * b).astype(BF).astype(F32)
            grad = jnp.sum(hidden * ch, axis=1, keepdims=True)
            grad_rows[j, at] = jnp.broadcast_to(grad, (tile, LANES))
            hg = (hidden * gate).astype(BF)
            dh = ch * gate
            da = (dh * b * sig * (1.0 + a * (1.0 - sig))).astype(BF)
            db = (dh * act).astype(BF)
            inner_ref[0, at], inner_ref[1, at], inner_ref[2, at] = da, db, hg
            return 0

        lax.fori_loop(0, blocks * CAP // tile, one_tile, 0)
        for part in range(width // chunk):
            cols = slice(part * chunk, (part + 1) * chunk)
            for k in range(3):
                x = (c_rows if k == 2 else x_rows)[j, :, cols]
                dw_ref[j, k, cols] = dot_tn(x, inner_ref[k]).astype(BF)
        for r in range(nz):
            dw_copy(j, r).start()

        def back_tile(i, _, j=j):
            at = pl.ds(pl.multiple_of(i * tile, tile), tile)
            da, db, hg = inner_ref[0, at], inner_ref[1, at], inner_ref[2, at]
            c_rows[j, at] = dot_nt(hg, w_ref[j, 2]).astype(BF)
            x_rows[j, at] = (dot_nt(da, w_ref[j, 0]) + dot_nt(db, w_ref[j, 1])).astype(BF)
            return 0

        lax.fori_loop(0, blocks * CAP // tile, back_tile, 0)

    fit = width // length
    line = lax.broadcasted_iota(jnp.int32, (GATE_ROWS, width), 0)
    place = lax.broadcasted_iota(jnp.int32, (GATE_ROWS, width), 1) // length

    def spread(i, _):
        chosen = chosen_rows(i)
        low = one_hot(chosen)
        at = pl.ds(pl.multiple_of(i * CAP, CAP), CAP)
        both = []
        for rows_ref in (x_rows, c_rows):
            rows = [rows_ref[j, at] for j in range(experts)]
            both.append(rows[0] if experts == 1 else jnp.concatenate(rows, axis=0))
        n2_ref[i] = dot_tn(low, both[0]).astype(BF)
        c_ref[i, :length] = dot_tn(low, both[1]).astype(BF)
        tail = jnp.zeros((GATE_ROWS, width), F32)
        for j in range(experts):
            sums = jnp.where(chosen[j], grad_rows[j, at][:, :1], 0.0)
            wide = jnp.concatenate([jnp.sum(sums, axis=0, keepdims=True)] * fit, axis=1)
            number = ids[3] + j
            tail = tail + jnp.where((line == number // fit) & (place == number % fit), wide, 0.0)
        c_ref[i, length:] = tail.astype(BF)
        return 0

    def dn2_copy(g):
        return pltpu.make_async_copy(n2_ref.at[pl.ds(g * per, per)], dn2_out[g], dn2_sem.at[g])

    def y_copy(g):
        here = pl.ds((g % (groups // 2)) * per, per)
        return pltpu.make_async_copy(
            c_ref.at[pl.ds(g * per, per)], y_out[g // (groups // 2)].at[here], y_sem.at[g]
        )

    for g in range(groups):
        lax.fori_loop(g * per, (g + 1) * per, spread, 0, unroll=True)
        dn2_copy(g).start()
        y_copy(g).start()
    for g in range(groups):
        dn2_copy(g).wait()
        y_copy(g).wait()
    for j in range(experts):
        for r in range(nz):
            dw_copy(j, r).wait()


def mixture(ids, slots, gates, n2_groups, c_groups, weights):
    groups, nz = len(n2_groups), len(weights)
    per, length, width = n2_groups[0].shape
    blocks, experts, _ = slots.shape
    high, rows = c_groups[0].shape[1], blocks * CAP
    flat = [w for row in weights for w in row]
    w_parts = []
    for r, row in enumerate(weights):
        first = 0
        for w in row:
            w_parts.append((r, first, w.shape[1]))
            first += w.shape[1]
    part = flat[0].shape
    matrices = (part[0], 3) + part[2:]
    anywhere = pl.BlockSpec(memory_space=pl.ANY)
    outs = [jax.ShapeDtypeStruct((per, length, width), BF)] * groups
    outs += [jax.ShapeDtypeStruct((groups // 2 * per, high, width), BF)] * 2
    outs += [jax.ShapeDtypeStruct(matrices, BF)] * nz
    got = call(
        functools.partial(mixture_kernel, nz, tuple(w_parts), groups, per, experts, 640),
        (1,),
        ids,
        [slots, gates, *n2_groups, *c_groups, *flat],
        [whole_spec(slots.shape), whole_spec(gates.shape)] + [anywhere] * (2 * groups + len(flat)),
        outs,
        [anywhere] * len(outs),
        [
            pltpu.VMEM((blocks, length, width), BF),
            pltpu.VMEM((blocks, high, width), BF),
            pltpu.VMEM(matrices[:2] + (width,) + matrices[3:], BF),
            pltpu.VMEM((experts, rows, width), BF),
            pltpu.VMEM((experts, rows, width), BF),
            pltpu.VMEM((experts, rows, LANES), F32),
            pltpu.VMEM((experts, rows, LANES), F32),
            pltpu.VMEM((3, rows, part[-1]), BF),
            pltpu.VMEM(matrices[:2] + (width,) + matrices[3:], BF),
            pltpu.SemaphoreType.DMA((groups,)),
            pltpu.SemaphoreType.DMA((groups,)),
            pltpu.SemaphoreType.DMA((len(flat),)),
            pltpu.SemaphoreType.DMA((groups,)),
            pltpu.SemaphoreType.DMA((groups,)),
            pltpu.SemaphoreType.DMA((experts, nz)),
        ],
    )
    return got[:groups], got[groups : groups + 2], got[groups + 2 :]


def half_grads_kernel(nr, ids, own_rows, other_rows, gain_ref, dq_ref, own_ref, other_ref, grad_ref, normed_ref, acc_ref):
    chunk, qn, kn = grad_ref.shape[1], dq_ref.shape[1], own_ref.shape[2]
    step, count = pl.program_id(0), pl.num_programs(0)
    normalize(own_rows, other_rows, gain_ref, normed_ref)

    @pl.when(step == 0)
    def _():
        for r in range(nr):
            x = normed_ref[:, span(row_chunk(ids, r, nr), chunk)]
            grad_ref[r, :, :qn] = dot_tn(x[: dq_ref.shape[0]], dq_ref[...]).astype(BF)
        acc_ref[...] = jnp.zeros_like(acc_ref)

    def add(dkv_ref):
        grad = jnp.concatenate([dkv_ref[0], dkv_ref[1]], axis=1)
        for r in range(nr):
            acc_ref[r] += dot_tn(normed_ref[:, span(row_chunk(ids, r, nr), chunk)], grad)

    pl.when(step < count // 2)(lambda: add(own_ref))
    pl.when(step >= count // 2)(lambda: add(other_ref))

    @pl.when(step == count - 1)
    def _():
        for r in range(nr):
            grad_ref[r, :, qn:] = acc_ref[r].astype(BF)


def half_grads(ids, rows, gain, dq, dkv, half, nr, nh):
    slots, (length, width) = 2 * rows[0].shape[0], rows[0].shape[1:]
    qn, kn = H * HD // nh, KVH * HD // nh

    def body(ids, own_rows, other_rows, gain_ref, dq_ref, own_ref, other_ref, grad_ref, normed_ref, acc_ref):
        half_grads_kernel(
            nr, ids, own_rows, other_rows, gain_ref, dq_ref, own_ref, other_ref, grad_ref, normed_ref, acc_ref
        )

    def at(ids):
        return half_chunk(ids, half, nh)

    out = jax.ShapeDtypeStruct((nr, width // nr, qn + 2 * kn), BF)
    tile, steps = BLOCKS * length, slots // BLOCKS
    middle = steps // 2
    return call(
        body,
        (steps,),
        ids,
        [*flat_rows(rows), gain, dq, *dkv],
        [
            *rows_specs(steps, (tile, width)),
            whole_spec(gain.shape),
            pl.BlockSpec((length, qn), lambda i, ids: (0, at(ids))),
            pl.BlockSpec((2, tile, kn), lambda i, ids: (0, jnp.minimum(i, middle - 1), at(ids))),
            pl.BlockSpec((2, tile, kn), lambda i, ids: (0, jnp.maximum(i - middle, 0), at(ids))),
        ],
        out,
        whole_spec(out.shape),
        [pltpu.VMEM((tile, width), BF), pltpu.VMEM((nr, width // nr, 2 * kn), F32)],
    )


def rows_back_kernel(nr, nh, ids, dq_ref, dkv_ref, x_ref, dx2_ref, gain_ref, *rest):
    weights = rest[:nh]
    out_ref, grad_ref, low_ref = rest[nh:]
    width = x_ref.shape[1]
    chunk = width // nr
    qn, kn = H * HD // nh, KVH * HD // nh
    at_q, at_k, at_v, at_end = columns(nh, width)
    low_ref[...] = dkv_ref[...].astype(BF)
    for r in range(nr):
        total = None
        for h in range(nh):
            at = half_chunk(ids, h, nh)
            weight = weights[h]
            part = dot_nt(dq_ref[:, span(at, qn)], weight[r, :, at_q:at_k])
            part = part + dot_nt(low_ref[0, :, span(at, kn)], weight[r, :, at_k:at_v])
            part = part + dot_nt(low_ref[1, :, span(at, kn)], weight[r, :, at_v:at_end])
            total = part if total is None else total + part
        grad_ref[:, span(row_chunk(ids, r, nr), chunk)] = total
    x = x_ref[...]
    scaled = grad_ref[...] * gain_ref[...]
    inverse = lax.rsqrt(jnp.mean(x * x, axis=1, keepdims=True) + EPSILON)
    inner = jnp.mean(scaled * x, axis=1, keepdims=True)
    out_ref[...] = dx2_ref[...] + inverse * scaled - x * (inverse * inverse * inverse * inner)


def rows_back(ids, dq, dkv, x, dx2, gain, weights):
    nr, nh = weights[0].shape[0], len(weights)
    ins = [dq, dkv, x, dx2, gain, *weights]
    return call(
        functools.partial(rows_back_kernel, nr, nh),
        (1,),
        ids,
        ins,
        [whole_spec(i.shape) for i in ins],
        jax.ShapeDtypeStruct(x.shape, F32),
        whole_spec(x.shape),
        [pltpu.VMEM(x.shape, F32), pltpu.VMEM(dkv.shape, BF)],
    )


def swap(value, axis, distance):
    count = lax.axis_size(axis)
    return lax.ppermute(value, axis, [(i, i ^ distance) for i in range(count)])


def after(value, *done):
    return lax.optimization_barrier((value,) + done)[0]


def together(*values):
    return lax.optimization_barrier(values)


def pick(array, index):
    return lax.dynamic_index_in_dim(array, index, 0, keepdims=False)


def gather_z(value):
    chips = lax.axis_size("shard") // 2
    if chips != 4:
        return [value] + [swap(value, "shard", 2 * r) for r in range(1, chips)]
    near, far = swap(value, "shard", 2), swap(value, "shard", 4)
    return [value, near, far, swap(far, "shard", 2)]


def scatter_z(parts):
    total = parts[0].astype(F32)
    for r in range(1, len(parts)):
        total = total + swap(parts[r], "shard", 2 * r).astype(F32)
    return total


def in_order(mine, other, core, axis):
    return jnp.where(
        core == 0,
        jnp.concatenate([mine, other], axis=axis),
        jnp.concatenate([other, mine], axis=axis),
    )


def add_low(*values):
    total = values[0].astype(F32)
    for value in values[1:]:
        total = total + value.astype(F32)
    return total.astype(BF)


def sum_start(blocks, first):
    return swap(jnp.stack([blocks[first], blocks[3]]), "expert", first)


def sum_next(blocks, got, first):
    mine = blocks[0].astype(F32) + got[0].astype(F32)
    return mine, swap(add_low(blocks[3 - first], got[1]), "expert", 3 - first)


def body(
    tokens,
    block_ids,
    routes,
    gates,
    attn_gain,
    w_query,
    w_key,
    w_value,
    w_out,
    moe_gain,
    w_gate,
    w_up,
    w_down,
    cotangent,
):
    length, width = tokens.shape[1], tokens.shape[2]
    n_expert, n_shard = lax.axis_size("expert"), lax.axis_size("shard")
    chips = n_shard // 2
    local = w_gate.shape[0]
    fast = n_expert == 4 and n_shard == 8 and local % 4 == 0
    sides = 2 if fast else 1
    experts = local // (2 * sides)
    e, s = lax.axis_index("expert"), lax.axis_index("shard")
    z, core = s // 2, s % 2
    side = z // 2 if fast else 0
    first_expert = e * local + core * (local // 2) + side * experts
    ids = jnp.stack([e, z, core, first_expert]).astype(jnp.int32)
    nh = 2 if fast else 1

    x = tokens[0]
    c = cotangent[0]

    inverse_one = lax.rsqrt(jnp.mean(x * x, axis=-1, keepdims=True) + EPSILON)
    scaled_rows = (x * inverse_one).astype(BF)

    def halves(matrix):
        low = matrix.astype(BF)
        return low.reshape(low.shape[0], nh, low.shape[1] // nh).transpose(1, 0, 2)

    def column(gain):
        return jnp.broadcast_to(gain.astype(BF)[None, :, None], (nh, gain.shape[0], LANES // 2))

    packed = jnp.concatenate(
        [halves(w_out), halves(w_query), halves(w_key), halves(w_value), column(attn_gain), column(moe_gain)],
        axis=2,
    )
    at_q, at_k, at_v, at_end = columns(nh, width)

    numbers = jnp.arange(EXPERTS, dtype=jnp.int32)
    lines = EXPERTS * length // width

    def positions(start):
        s_late = after(s, start)
        owners = jnp.stack([s_late ^ (2 * r + k) for k in range(2) for r in range(chips)])
        angles = (owners * length).astype(F32)[:, None] * jnp.asarray(frequencies(), F32)[None, :]
        cosine, sine = jnp.cos(angles), jnp.sin(angles)
        every = block_ids[0].reshape(n_shard, length)
        key_blocks = jnp.concatenate(
            [pick(every, s_late ^ (2 * r + k)) for k in range(2) for r in range(chips)]
        )
        own_blocks = pick(every, s_late)
        lanes = jnp.arange(LANES, dtype=jnp.int32)[None, :]
        key_extra = ((lanes == key_blocks[:, None]) | ((lanes >= 16) & (lanes < 19))).astype(BF)
        query_extra = jnp.where((lanes < 16) & (lanes > own_blocks[:, None]), -1e30, 0.0).astype(BF)
        return cosine, sine, key_extra, query_extra

    def named_experts(routed):
        return routed[0][None, :, :] == numbers[:, None, None]

    def cotangent_rows(start):
        value, routed, gated = after((c, routes, gates), start)
        dense = jnp.sum(jnp.where(named_experts(routed), gated[0][None, :, :], 0.0), axis=-1)
        dense = dense.reshape(lines, width)
        high = dense.astype(BF)
        low = (dense - high.astype(F32)).astype(BF)
        return jnp.concatenate([value.astype(BF), high, low], axis=0)

    def own_experts(start):
        low = jnp.stack([m.astype(BF) for m in after((w_gate, w_up, w_down), start)], axis=1)
        low = low.reshape((2, local // 2) + low.shape[1:])
        return pick(low, core), swap(pick(low, 1 - core), "shard", 1)

    def over_columns(value):
        return [swap(value, "expert", r) for r in range(1, n_expert)]

    if fast:
        mine, other = pick(packed, core), pick(packed, 1 - core)
        chip = in_order(mine, swap(other, "shard", 1), core, 0)

    if fast:
        w_near, w_far = swap(chip, "shard", 2), swap(chip, "shard", 4)
        stacked = jnp.stack([chip, w_near, w_far, swap(w_far, "shard", 2)])
        block = jnp.concatenate([pick(stacked, z ^ i) for i in range(chips)], axis=0)
        c_pack = cotangent_rows(chip)
        w_mine, w_other = own_experts(chip)
        cosine, sine, key_extra, query_extra = positions(chip)
        w_got = over_columns(after(block, w_other))
        x_late = after(scaled_rows, block)
        x_near, x_far = swap(x_late, "shard", 2), swap(x_late, "shard", 4)
        x_cross = swap(x_far, "shard", 2)
        c_far = swap(after(c_pack, x_far), "shard", 4)
        chip_w = in_order(after(w_mine, x_cross), w_other, core, 2)
        chip_w = chip_w.reshape((2, experts, 3, 2 * w_gate.shape[1], w_gate.shape[2]))
        here, there = pick(chip_w, side), pick(chip_w, 1 - side)
        there = [there[:, k : k + 1] for k in range(3)]
        own_core = jnp.stack([scaled_rows, x_near, x_far, x_cross])
        x_other = swap(own_core, "shard", 1)
        rows = [own_core, x_other]
        early = (own_core, c_far, cosine, sine, key_extra, query_extra)
        w_got = [after(got, *early) for got in w_got]
        blocks = jnp.stack([block] + w_got)
        gain_cols = blocks[:, :, at_end:]
        gain_cols = jnp.concatenate([pick(gain_cols, e ^ i) for i in range(n_expert)], axis=0)
        attn_other, near_a, far_a, gain_one, gain_two, ids = together(
            swap(blocks, "shard", 1),
            here[:, :1],
            there[0],
            gain_cols[:, 0].astype(F32)[None],
            gain_cols[:, LANES // 2].astype(F32)[None],
            ids,
        )
        attn_w = [blocks, attn_other]
        near_a, far_a = swap(near_a, "shard", 2), swap(far_a, "shard", 4)
        c_own_got = over_columns(after(c_pack, attn_w[1]))
    else:
        c_pack = cotangent_rows(packed)
        own_core = jnp.stack(gather_z(scaled_rows))
        rows = [own_core, swap(own_core, "shard", 1)]
        cosine, sine, key_extra, query_extra = positions(packed)
        blocks = lax.all_gather(packed[0], ("expert", "shard"), axis=0, tiled=True)
        attn_w = [blocks[None]]
        gain_cols = blocks[:, at_end:]
        expert_w = gather_z(in_order(*own_experts(packed), core, 2))
        gain_one = gain_cols[:, 0].astype(F32)[None]
        gain_two = gain_cols[:, LANES // 2].astype(F32)[None]
    nr = attn_w[0].shape[0]

    q, k, v, cosine, sine = project(ids, rows, gain_one, cosine, sine, attn_w)
    if fast:
        c_far_got = over_columns(after(c_far, q))
        q, near_a, far_a, *c_own_got = together(q, near_a, far_a, *c_own_got)
        near_b = swap(after(here[:, 1:], q), "shard", 2)
        far_b = swap(after(there[1], q), "shard", 4)
        c_own = jnp.stack([c_pack] + c_own_got)
    mixed, mixed_low, lse = attend(ids, q, k, v, key_extra, query_extra)
    x2, n2 = project_out(ids, x, mixed_low, gain_two, attn_w)

    def places_of(groups):
        tails = jnp.concatenate([group[:, length:] for group in groups], axis=0).astype(F32)
        dense = (tails[:, :lines] + tails[:, lines:]).reshape(-1, EXPERTS, length)
        gate_here = lax.dynamic_slice_in_dim(dense, first_expert, experts, 1)
        chosen = gate_here > 0.0
        before = jnp.triu(jnp.ones((length, length), BF), 1)
        ranks = jnp.einsum("net,tu->neu", chosen.astype(BF), before, preferred_element_type=F32)
        return gate_here, jnp.where(chosen, ranks, -1.0)

    if fast:
        n2, near_b, far_b, *c_far_got = together(n2, near_b, far_b, *c_far_got)
        n2_far = swap(n2, "shard", 4)
        n2_own_got = over_columns(n2)
        cross_a = swap(after(far_a, n2), "shard", 2)
        n2_far, cross_a, *n2_own_got = together(n2_far, cross_a, *n2_own_got)
        cross_b = swap(after(far_b, n2_far), "shard", 2)
        n2_far_got = over_columns(n2_far)
        far_c = swap(after(there[2], n2_far), "shard", 4)
        n2_own = jnp.stack([n2] + n2_own_got)
        c_across = jnp.stack([after(piece, n2_far) for piece in [c_far, *c_far_got]])
        far_c, cross_b, n2_own, c_across, *n2_far_got = together(
            far_c, cross_b, n2_own, c_across, *n2_far_got
        )
        n2_across = jnp.stack([n2_far] + n2_far_got)
        cross_c = swap(far_c, "shard", 2)
        n2_groups = [n2_own, n2_across, swap(n2_own, "shard", 1), swap(n2_across, "shard", 1)]
        c_groups = [c_own, c_across] + [swap(after(g, far_c), "shard", 1) for g in (c_own, c_across)]
        gate_here, slots = places_of(c_groups)
        expert_w = [[here], [near_a, near_b], [far_a, far_b, far_c], [cross_a, cross_b, cross_c]]
        dn2_parts, y_parts, d_experts = mixture(
            ids, slots, gate_here, n2_groups, c_groups, expert_w
        )
        step = swap(d_experts[3], "shard", 2)
        dn2_other = [swap(dn2_parts[3], "shard", 1), swap(dn2_parts[2], "shard", 1)][::-1]
        far_sums = add_low(dn2_parts[1], dn2_other[1])
        own_sums = add_low(dn2_parts[0], dn2_other[0])
        far_got = [swap(far_sums[r], "expert", r) for r in range(1, n_expert)]
        dn2_far = add_low(far_sums[0], *[after(got, own_sums, step) for got in far_got])
        dn2_got = swap(dn2_far, "shard", 4)
        own_got = [swap(after(own_sums[r], dn2_far), "expert", r) for r in range(1, n_expert)]
        d_far = add_low(d_experts[2], after(step, dn2_far))
        y_sum = add_low(y_parts[0], swap(after(y_parts[1], dn2_far), "shard", 1))
        y_sum = y_sum.reshape((2, n_expert) + y_sum.shape[1:])
        far_early, near_early = after((d_far[:, :1], d_experts[1][:, :1]), dn2_got)
        own_got = [after(got, far_early, near_early, y_sum) for got in own_got]
        dn2 = sum([g.astype(F32) for g in own_got + [dn2_got]], own_sums[0].astype(F32))
    else:
        c_own = jnp.stack([c_pack] + over_columns(c_pack))
        c_groups = [c_own, swap(c_own, "shard", 1)]
        gate_here, slots = places_of(c_groups)
        n2_own = jnp.stack([n2] + over_columns(n2))
        n2_groups = [n2_own, swap(n2_own, "shard", 1)]
        c_rows, gate_rows = gather_rows(ids, slots, c_groups, gate_here)
        (x_rows,) = gather_rows(ids, slots, n2_groups)
        flat = (experts, slots.shape[0] * CAP)
        y_rows, dx_rows, grad_rows, d_experts = run_experts(
            ids,
            x_rows.reshape(flat + (width,)),
            c_rows.reshape(flat + (width,)),
            gate_rows.reshape(flat + (LANES,)),
            expert_w,
        )
        split = (experts, slots.shape[0], CAP)
        dn2_parts = spread_rows(ids, slots, dx_rows.reshape(split + (width,)), 2)
        y_parts = spread_rows(
            ids, slots, y_rows.reshape(split + (width,)), 2, grad_rows.reshape(split + (LANES,))
        )
        own_sums = add_low(dn2_parts[0], swap(dn2_parts[1], "shard", 1))
        own_got = [swap(own_sums[r], "expert", r) for r in range(1, n_expert)]
        dn2 = sum([g.astype(F32) for g in own_got], own_sums[0].astype(F32))
        y_sum = add_low(y_parts[0], swap(y_parts[1], "shard", 1))[None]

    dx2, d_mixed, d_out_w = project_out_back(ids, c, x2, gain_two, dn2, mixed_low, attn_w)
    args = (mixed, lse, k, v, key_extra, query_extra, cosine, sine)
    if fast:
        d_out_sums = add_low(d_out_w[0], swap(d_out_w[1], "shard", 1))
        far_a, near_a = swap(far_early, "shard", 4), swap(near_early, "shard", 2)
        y_sum = after(y_sum, dn2)
        got_a, got_b = sum_start(y_sum[1], 1), sum_start(y_sum[0], 2)
        done = attend_back(ids, q, after(d_mixed, d_out_sums), *args, 1)
        dq, far_a, near_a, got_a, got_b, *done = together(done[0], far_a, near_a, got_a, got_b, *done)
        far_b = swap(after(d_far[:, 1:], dq), "shard", 4)
        near_b = swap(after(d_experts[1][:, 1:], dq), "shard", 2)
        y_across, got_a = sum_next(y_sum[1], got_a, 1)
        y_out, got_b = sum_next(y_sum[0], got_b, 2)
        got_c = sum_start(after(d_out_sums, dq), 1)
        d_other = half_grads(ids, rows, gain_one, dq, done[1:], 1, nr, nh)
        dq, *dkv = attend_back(ids, q, after(d_mixed, d_other), *args, 0, done)
        dq, far_b, near_b, got_a, got_b, got_c, *dkv = together(
            dq, far_b, near_b, got_a, got_b, got_c, *dkv
        )
        y_across = (y_across + got_a.astype(F32)).astype(BF)
        y_far = swap(y_across, "shard", 4)
        d_other = swap(after(d_other, dq), "shard", 1)
        d_out_total, got_c = sum_next(d_out_sums, got_c, 1)
    else:
        dq, *dkv = attend_back(ids, q, d_mixed, *args)
        y_got = [swap(y_sum[0, r], "expert", r) for r in range(1, n_expert)]
    dkv_core = swap(dkv[1], "shard", 1)
    dkv_sums = add_low(dkv[0], dkv_core)
    if fast:
        dq = after(dq, dkv_sums, y_across)
    d_own = half_grads(ids, rows, gain_one, dq, dkv, 0, nr, nh)
    if fast:
        d_own, d_other, got_c = together(d_own, d_other, got_c)
    dkv_parts = [dkv_sums[:, r * length : (r + 1) * length] for r in range(chips)]
    if fast:
        sums = add_low(d_own, d_other)
        dkv_step = swap(dkv_parts[3], "shard", 2)
        dkv_far = add_low(dkv_parts[2], dkv_step)
        got = [swap(sums[r], "expert", r) for r in range(1, n_expert)]
        dkv_far, y_far = together(dkv_far, y_far)
        got = [after(g, dkv_far) for g in got]
        dkv_far, dkv_near = swap(dkv_far, "shard", 4), swap(after(dkv_parts[1], dkv_far), "shard", 2)
        d_out_total = (d_out_total + got_c.astype(F32)).astype(BF)
        y_out = y_out + got_b.astype(F32)
        cols = width // nh
        high = d_out_total.shape[0] - GATE_ROWS
        gain_grad = d_out_total[high, : width // n_expert]
        d_out_total = jnp.concatenate(
            [d_out_total[:high, f * cols : (f + 1) * cols] for f in range(nh)], axis=0
        )
        gain_grad = jnp.broadcast_to(gain_grad[:, None], (gain_grad.shape[0], LANES))
        d_out_total = jnp.concatenate([d_out_total, gain_grad], axis=1)
        d_total = add_low(sums[0], *got)
        total = jnp.concatenate([d_out_total, d_total], axis=1)
        total = total.reshape(chips, total.shape[0] // chips, total.shape[1])
        total = [pick(total, z ^ r) for r in range(chips)]
        step, near = swap(total[3], "shard", 2), swap(total[1], "shard", 2)
        dkv_far, dkv_near, step, near = together(dkv_far, dkv_near, step, near)
        dkv_own = sum([g.astype(F32) for g in (dkv_near, dkv_far)], dkv_parts[0].astype(F32))
        far = swap(add_low(total[2], step), "shard", 4)
        token_grad = rows_back(ids, dq, dkv_own, x, dx2, gain_one, attn_w)
        summed = total[0].astype(F32) + near.astype(F32) + after(far, token_grad).astype(F32)
        summed = summed.reshape(2, summed.shape[0] // 2, summed.shape[1])
        mine = pick(summed, core)
        other = swap(pick(summed, 1 - core).astype(BF), "shard", 1).astype(F32)
        parts = (jnp.where(core == 0, mine, other), jnp.where(core == 0, other, mine))
        out_sum = y_out + after(y_far, far).astype(F32)
    else:
        out_sum = sum([g.astype(F32) for g in y_got], y_sum[0, 0].astype(F32))
        dkv_own = scatter_z(dkv_parts)
        token_grad = rows_back(ids, dq, dkv_own, x, dx2, gain_one, attn_w)
        gain_grad = jnp.broadcast_to(d_out_w[0][0, width][:, None], (width, LANES))
        joined = jnp.concatenate([d_out_w[0][0, :width], gain_grad, d_own[0]], axis=1)
        joined = lax.psum_scatter(joined, ("expert", "shard"), scatter_dimension=0, tiled=True)
        parts = [joined.astype(F32)]

    on, qn, kn = width // nh, H * HD // nh, KVH * HD // nh
    start = on + LANES
    d_out_full = jnp.concatenate([p[:, :on] for p in parts], axis=1)
    d_gain_two = parts[0][:, on]
    d_query_w = jnp.concatenate([p[:, start : start + qn] for p in parts], axis=1)
    d_key_w = jnp.concatenate([p[:, start + qn : start + qn + kn] for p in parts], axis=1)
    d_value_w = jnp.concatenate([p[:, start + qn + kn :] for p in parts], axis=1)
    row_sums = (
        jnp.sum(w_query.astype(BF).astype(F32) * d_query_w, axis=1)
        + jnp.sum(w_key.astype(BF).astype(F32) * d_key_w, axis=1)
        + jnp.sum(w_value.astype(BF).astype(F32) * d_value_w, axis=1)
    )
    d_gain_one = row_sums / attn_gain.astype(BF).astype(F32)

    output = x2 + out_sum[:length]
    gate_sums = out_sum[length : length + lines].reshape(EXPERTS, length)
    gate_grad = jnp.sum(jnp.where(named_experts(routes), gate_sums[:, :, None], 0.0), axis=0)

    if fast:
        there_sum = jnp.concatenate([far_a, far_b], axis=1).astype(F32)
        here_sum = d_experts[0].astype(F32)
        here_sum = here_sum + jnp.concatenate([near_a, near_b], axis=1).astype(F32)
        d_chip = jnp.where(
            side == 0,
            jnp.concatenate([here_sum, there_sum], axis=0),
            jnp.concatenate([there_sum, here_sum], axis=0),
        )
    else:
        d_chip = scatter_z(d_experts)
    half = d_chip.shape[2] // 2
    d_chip = d_chip.astype(BF)
    if fast:
        d_chip = after(d_chip, *got)
    mine = lax.dynamic_slice_in_dim(d_chip, core * half, half, 2)
    other = swap(lax.dynamic_slice_in_dim(d_chip, (1 - core) * half, half, 2), "shard", 1)
    if fast:
        other = after(other, dkv_own)
    d_expert = in_order(mine, other, core, 0).astype(F32)

    return (
        output[None],
        token_grad[None],
        gate_grad[None],
        d_gain_one,
        d_query_w,
        d_key_w,
        d_value_w,
        d_out_full,
        d_gain_two,
        d_expert[:, 0],
        d_expert[:, 1],
        d_expert[:, 2],
    )


def solution(mesh):
    rows = P("expert", "shard", None)
    split = P(("expert", "shard"), None)
    gain = P(("expert", "shard"))
    in_specs = (
        rows, P("expert", None), rows, rows, gain, split, split, split, split, gain, rows, rows, rows, rows,
    )
    out_specs = (rows, rows, rows, gain, split, split, split, split, gain, rows, rows, rows)
    return jax.shard_map(body, mesh=mesh, in_specs=in_specs, out_specs=out_specs, check_vma=False)
```

```python
import functools

import jax
import jax.numpy as jnp
import numpy as np
from jax import lax
from jax.experimental import pallas as pl
from jax.experimental.pallas import tpu as pltpu
from jax.sharding import PartitionSpec as P

H = 16
KVH = 8
HD = 64
EXPERTS = 32
TOP = 8
CAP = 80
EPSILON = 1e-06
LANES = 128
PAIRS = KVH // 2
BLOCKS = 2
GATE_ROWS = 16

BF = jnp.bfloat16
F32 = jnp.float32
VMEM_BYTES = 56 * 1024 * 1024


def dot(left, right):
    return lax.dot_general(left, right, (((1,), (0,)), ((), ())), preferred_element_type=F32)


def dot_nt(left, right):
    return lax.dot_general(left, right, (((1,), (1,)), ((), ())), preferred_element_type=F32)


def dot_tn(left, right):
    return lax.dot_general(left, right, (((0,), (0,)), ((), ())), preferred_element_type=F32)


def call(kernel, grid, scalars, inputs, in_specs, out_shapes, out_specs, scratch=(), aliases=None):
    return pl.pallas_call(
        kernel,
        grid_spec=pltpu.PrefetchScalarGridSpec(
            num_scalar_prefetch=1,
            grid=grid,
            in_specs=in_specs,
            out_specs=out_specs,
            scratch_shapes=list(scratch),
        ),
        out_shape=out_shapes,
        input_output_aliases=aliases or {},
        compiler_params=pltpu.CompilerParams(vmem_limit_bytes=VMEM_BYTES),
        cost_estimate=pl.CostEstimate(flops=0, bytes_accessed=0, transcendentals=0),
    )(scalars, *inputs)


def whole_spec(shape):
    return pl.BlockSpec(tuple(shape), lambda *_: (0,) * len(shape))


def lane_ids(rows):
    return lax.broadcasted_iota(jnp.int32, (rows, LANES), 1)


def swap_halves(tile):
    first = lane_ids(tile.shape[0]) % HD < HD // 2
    return jnp.where(first, pltpu.roll(tile, LANES - HD // 2, 1), pltpu.roll(tile, HD // 2, 1))


def turn(value, cosine, signed_sine, direction):
    tiles = []
    for i in range(value.shape[1] // LANES):
        tile = value[:, i * LANES : (i + 1) * LANES]
        tiles.append(tile * cosine + direction * (swap_halves(tile) * signed_sine))
    return tiles[0] if len(tiles) == 1 else jnp.concatenate(tiles, axis=1)


def row_chunk(ids, r, count):
    return ids[0] ^ r if count > 1 else 0


def z_chunk(ids, r, count):
    return ids[1] ^ r if count > 1 else 0


def half_chunk(ids, h, count):
    return ids[2] ^ h if count > 1 else 0


def span(index, size):
    return pl.ds(pl.multiple_of(index * size, size), size)


def columns(nh, width):
    on, qn, kn = width // nh, H * HD // nh, KVH * HD // nh
    return on, on + qn, on + qn + kn, on + qn + 2 * kn


def frequencies():
    return np.tile(10000.0 ** (-np.arange(HD // 2) * 2.0 / HD), 2 * LANES // HD)


def place_tables(length):
    angles = np.arange(length)[:, None] * frequencies()[None, :]
    return np.cos(angles).astype(np.float32), np.sin(angles).astype(np.float32)


def qkv_kernel(nr, nh, ids, own_ref, other_ref, gain_ref, cos_ref, sin_ref, slot_cos, slot_sin, *rest):
    weights = rest[:nh]
    q_ref, k_ref, v_ref, cos_out, sin_out, normed_ref = rest[nh:]
    width = own_ref.shape[-1]
    chunk = width // nr
    qn, kn = H * HD // nh, KVH * HD // nh
    at_q, at_k, _, at_end = columns(nh, width)
    normalize(own_ref, other_ref, gain_ref, normed_ref)
    length = cos_ref.shape[0]
    sign = jnp.where(lane_ids(length) % HD < HD // 2, -1.0, 1.0)
    for b in range(cos_out.shape[0] // length):
        slot = pl.ds(pl.program_id(0) * (cos_out.shape[0] // length) + b, 1)
        c, s = slot_cos[slot], slot_sin[slot]
        at = slice(b * length, (b + 1) * length)
        cos_out[at] = cos_ref[...] * c - sin_ref[...] * s
        sin_out[at] = sign * (sin_ref[...] * c + cos_ref[...] * s)
    cosine, sine = cos_out[...], sin_out[...]
    for h in range(nh):
        total = None
        for r in range(nr):
            part = dot(
                normed_ref[:, span(row_chunk(ids, r, nr), chunk)],
                weights[h][r, :, at_k:at_end],
            )
            total = part if total is None else total + part
        here = span(half_chunk(ids, h, nh), kn)
        k_ref[:, here] = turn(total[:, :kn], cosine, sine, 1.0).astype(BF)
        v_ref[:, here] = total[:, kn:].astype(BF)

    rows = q_ref.shape[0]

    @pl.when(pl.program_id(0) == 0)
    def _():
        for h in range(nh):
            total = None
            for r in range(nr):
                part = dot(
                    normed_ref[:rows, span(row_chunk(ids, r, nr), chunk)], weights[h][r, :, at_q:at_k]
                )
                total = part if total is None else total + part
            turned = turn(total, cosine[:rows], sine[:rows], 1.0).astype(BF).astype(F32) * HD**-0.5
            q_ref[:, span(half_chunk(ids, h, nh), qn)] = turned.astype(BF)


def normalize(own_ref, other_ref, gain_ref, normed_ref):
    own = pl.program_id(0) < pl.num_programs(0) // 2
    rows = jnp.where(own, own_ref[...], other_ref[...])
    normed_ref[...] = (rows.astype(F32) * gain_ref[...]).astype(BF)


def rows_specs(steps, shape):
    half = steps // 2
    return [
        pl.BlockSpec(shape, lambda i, _: (jnp.minimum(i, half - 1), 0)),
        pl.BlockSpec(shape, lambda i, _: (jnp.maximum(i - half, 0), 0)),
    ]


def flat_rows(rows):
    return [part.reshape(-1, part.shape[-1]) for part in rows]


def project(ids, rows, gain, cosine, sine, weights):
    slots, (length, width) = 2 * rows[0].shape[0], rows[0].shape[1:]
    nr, nh = weights[0].shape[0], len(weights)
    tile, steps = BLOCKS * length, slots // BLOCKS
    tables = [jnp.asarray(t) for t in place_tables(length)]
    return call(
        functools.partial(qkv_kernel, nr, nh),
        (steps,),
        ids,
        [*flat_rows(rows), gain, *tables, cosine, sine, *weights],
        [
            *rows_specs(steps, (tile, width)),
            whole_spec(gain.shape),
            *[whole_spec(t.shape) for t in tables],
            whole_spec(cosine.shape),
            whole_spec(sine.shape),
            *[whole_spec(w.shape) for w in weights],
        ],
        [
            jax.ShapeDtypeStruct((length, H * HD), BF),
            jax.ShapeDtypeStruct((slots * length, KVH * HD), BF),
            jax.ShapeDtypeStruct((slots * length, KVH * HD), BF),
            jax.ShapeDtypeStruct((slots * length, LANES), F32),
            jax.ShapeDtypeStruct((slots * length, LANES), F32),
        ],
        [
            whole_spec((length, H * HD)),
            pl.BlockSpec((tile, KVH * HD), lambda i, _: (i, 0)),
            pl.BlockSpec((tile, KVH * HD), lambda i, _: (i, 0)),
            pl.BlockSpec((tile, LANES), lambda i, _: (i, 0)),
            pl.BlockSpec((tile, LANES), lambda i, _: (i, 0)),
        ],
        [pltpu.VMEM((tile, width), BF)],
    )


def to_half(tile, which, wanted):
    if which != wanted:
        tile = pltpu.roll(tile, HD, 1)
    return jnp.where(lane_ids(tile.shape[0]) // HD == wanted, tile, 0.0)


def attend_kernel(ids, q_ref, k_ref, v_ref, kx_ref, qx_ref, o_ref, low_ref, lse_ref):
    keys = jnp.concatenate([k_ref[...], kx_ref[...]], axis=1)
    values = v_ref[...]
    extra = qx_ref[...]
    rows = q_ref.shape[0]
    lanes = lane_ids(rows)
    sums = jnp.zeros((rows, LANES), F32)
    for t in range(2):
        tile = q_ref[:, t * LANES : (t + 1) * LANES].astype(F32)
        mixed = jnp.zeros((rows, LANES), F32)
        for w in range(2):
            query = jnp.concatenate([to_half(tile, w, t).astype(BF), extra], axis=1)
            scores = dot_nt(query, keys)
            highest = jnp.max(scores, axis=1, keepdims=True)
            weights = jnp.exp(scores - highest)
            total = jnp.sum(weights, axis=1, keepdims=True)
            out = dot(weights.astype(BF), values) / total
            mixed = mixed + to_half(out, t, w)
            sums = jnp.where(lanes == 2 * t + w, highest + jnp.log(total), sums)
        o_ref[:, t * LANES : (t + 1) * LANES] = mixed
        low_ref[:, t * LANES : (t + 1) * LANES] = mixed.astype(BF)
    lse_ref[0] = sums


def attend(ids, q, k, v, key_extra, query_extra):
    length, keys = q.shape[0], k.shape[0]
    quad = pl.BlockSpec((length, 2 * LANES), lambda p, _: (0, p))
    pair = pl.BlockSpec((keys, LANES), lambda p, _: (0, p))
    return call(
        attend_kernel,
        (PAIRS,),
        ids,
        [q, k, v, key_extra, query_extra],
        [quad, pair, pair, whole_spec(key_extra.shape), whole_spec(query_extra.shape)],
        [
            jax.ShapeDtypeStruct((length, H * HD), F32),
            jax.ShapeDtypeStruct((length, H * HD), BF),
            jax.ShapeDtypeStruct((PAIRS, length, LANES), F32),
        ],
        [quad, quad, pl.BlockSpec((1, length, LANES), lambda p, _: (p, 0, 0))],
    )


def three_parts(value):
    high = value.astype(BF)
    rest = value - high.astype(F32)
    middle = rest.astype(BF)
    return high.astype(F32), middle.astype(F32), (rest - middle.astype(F32))


def with_parts(base, value, lanes):
    high, middle, low = three_parts(value)
    base = jnp.where(lanes == 16, high, base)
    base = jnp.where(lanes == 17, middle, base)
    return jnp.where(lanes == 18, low, base).astype(BF)


def attend_back_kernel(
    span_rows, ids, q_ref, do_ref, o_ref, lse_ref, k_ref, v_ref, kx_ref, qx_ref, cos_ref, sin_ref,
    dq_ref, own_ref, other_ref, sum_ref,
):
    rows = q_ref.shape[0]
    lanes = lane_ids(rows)
    extra = qx_ref[...].astype(F32)
    nothing = jnp.zeros((rows, LANES), F32)
    sums = lse_ref[0]
    queries, outs, pads_q, pads_o = [], [], [], []
    for t in range(2):
        at = slice(t * LANES, (t + 1) * LANES)
        tile, grad = q_ref[:, at].astype(F32), do_ref[:, at].astype(F32)
        product = grad * o_ref[:, at]
        for w in range(2):
            here = lanes // HD == w
            delta = jnp.sum(jnp.where(here, product, 0.0), axis=1, keepdims=True)
            log_sum = jnp.sum(jnp.where(lanes == 2 * t + w, sums, 0.0), axis=1, keepdims=True)
            q_pad = to_half(tile, w, t).astype(BF)
            o_pad = to_half(grad, w, t).astype(BF)
            queries.append(jnp.concatenate([q_pad, with_parts(extra, -log_sum, lanes)], axis=1))
            outs.append(jnp.concatenate([o_pad, with_parts(nothing, -delta, lanes)], axis=1))
            pads_q.append(q_pad)
            pads_o.append(o_pad)
    all_q = jnp.concatenate(pads_q, axis=0)
    every_q = jnp.concatenate(queries, axis=0)
    every_o = jnp.concatenate(outs, axis=0)
    all_o = jnp.concatenate(pads_o, axis=0)
    sum_ref[...] = jnp.zeros_like(sum_ref)

    spans = k_ref.shape[0] // 2 // span_rows

    def one_span(i, _, part, out_ref):
        put = pl.ds(pl.multiple_of(i * span_rows, span_rows), span_rows)
        first = part * spans * span_rows
        at = pl.ds(pl.multiple_of(first + i * span_rows, span_rows), span_rows)
        k_here, x_here = k_ref[at, :], kx_ref[at, :]
        keys = jnp.concatenate([k_here, x_here], axis=1)
        values = jnp.concatenate([v_ref[at, :], x_here], axis=1)
        probs = jnp.exp(dot_nt(keys, every_q))
        d_scores = (probs * dot_nt(values, every_o)).astype(BF)
        sum_ref[...] += dot_tn(k_here, d_scores)
        out_ref[1, put, :] = dot(probs.astype(BF), all_o).astype(BF)
        d_key = dot(d_scores, all_q)
        d_key = turn(d_key, cos_ref[at, :], sin_ref[at, :], -1.0)
        out_ref[0, put, :] = d_key.astype(BF)
        return 0

    for part, out_ref in enumerate((own_ref, other_ref)):
        lax.fori_loop(0, spans, functools.partial(one_span, part=part, out_ref=out_ref), 0)
    cosine, sine = cos_ref[:rows, :], sin_ref[:rows, :]
    for t in range(2):
        d_query = [sum_ref[:, n * rows : (n + 1) * rows].T for n in (2 * t, 2 * t + 1)]
        tile = to_half(d_query[0], t, 0) + to_half(d_query[1], t, 1)
        turned = turn(tile * HD**-0.5, cosine, sine, -1.0)
        dq_ref[:, t * LANES : (t + 1) * LANES] = turned.astype(BF)


def attend_back_part(*refs):
    attend_back_kernel(1024, *refs[:11], *refs[14:])


def attend_back(ids, q, d_out, out, lse, k, v, key_extra, query_extra, cosine, sine, half=None, done=None):
    length, keys = q.shape[0], k.shape[0]
    count = PAIRS if half is None else PAIRS // 2

    def at(p, ids):
        return p if half is None else (ids[2] ^ half) * count + p

    quad = pl.BlockSpec((length, 2 * LANES), lambda p, ids: (0, at(p, ids)))
    pair = pl.BlockSpec((keys, LANES), lambda p, ids: (0, at(p, ids)))
    ins = [q, d_out, out, lse, k, v, key_extra, query_extra, cosine, sine]
    specs = [
        quad,
        quad,
        quad,
        pl.BlockSpec((1, length, LANES), lambda p, ids: (at(p, ids), 0, 0)),
        pair,
        pair,
        whole_spec(key_extra.shape),
        whole_spec(query_extra.shape),
        whole_spec(cosine.shape),
        whole_spec(sine.shape),
    ]
    if done is not None:
        ins += done
        specs += [pl.BlockSpec(memory_space=pl.ANY)] * 3
    return call(
        attend_back_part if done is not None else functools.partial(attend_back_kernel, 1024),
        (count,),
        ids,
        ins,
        specs,
        [
            jax.ShapeDtypeStruct((length, H * HD), BF),
            jax.ShapeDtypeStruct((2, keys // 2, KVH * HD), BF),
            jax.ShapeDtypeStruct((2, keys // 2, KVH * HD), BF),
        ],
        [quad] + [pl.BlockSpec((2, keys // 2, LANES), lambda p, ids: (0, 0, at(p, ids)))] * 2,
        [pltpu.VMEM((LANES, 4 * length), F32)],
        aliases={11: 0, 12: 1, 13: 2} if done is not None else None,
    )


def out_kernel(nr, nh, ids, x_ref, o_ref, gain_ref, *rest):
    weights = rest[:nh]
    x2_ref, n2_ref = rest[nh:]
    width = x_ref.shape[1]
    chunk, cols = H * HD // nr, width // nh
    for h in range(nh):
        at = span(half_chunk(ids, h, nh), cols)
        total = x_ref[:, at]
        for r in range(nr):
            total = total + dot(
                o_ref[:, span(row_chunk(ids, r, nr), chunk)], weights[h][r]
            )
        x2_ref[:, at] = total
    middle = x2_ref[...]
    inverse = lax.rsqrt(jnp.mean(middle * middle, axis=1, keepdims=True) + EPSILON)
    n2_ref[...] = (middle * inverse * gain_ref[...]).astype(BF)


def out_spec(weight, cols):
    return pl.BlockSpec(weight.shape[:2] + (cols,), lambda *_: (0, 0, 0))


def project_out(ids, x, low, gain, weights):
    nr, nh = weights[0].shape[0], len(weights)
    ins = [x, low, gain, *weights]
    outs = [jax.ShapeDtypeStruct(x.shape, F32), jax.ShapeDtypeStruct(x.shape, BF)]
    return call(
        functools.partial(out_kernel, nr, nh),
        (1,),
        ids,
        ins,
        [whole_spec(i.shape) for i in ins[:3]] + [out_spec(w, x.shape[1] // nh) for w in weights],
        outs,
        [whole_spec(o.shape) for o in outs],
    )


def out_back_kernel(nr, nh, ids, c_ref, x2_ref, gain_ref, dn2_ref, low_ref, *rest):
    weights = rest[:nh]
    dx2_ref, do_ref = rest[nh : nh + 2]
    grads = rest[nh + 2 : 2 * nh + 2]
    dr_ref, term_ref = rest[2 * nh + 2 :]
    width = c_ref.shape[1]
    chunk, cols = H * HD // nr, width // nh
    middle, d_normed = x2_ref[...], dn2_ref[...]
    inverse = lax.rsqrt(jnp.mean(middle * middle, axis=1, keepdims=True) + EPSILON)
    scaled = d_normed * gain_ref[...]
    inner = jnp.mean(scaled * middle, axis=1, keepdims=True)
    d_middle = c_ref[...] + inverse * scaled - middle * (inverse * inverse * inverse * inner)
    dx2_ref[...] = d_middle
    dr_ref[...] = d_middle.astype(BF)
    term_ref[...] = d_normed * middle * inverse
    fold = width // cols
    rows = chunk // fold
    for r in range(nr):
        at = span(row_chunk(ids, r, nr), chunk)
        low = low_ref[:, at]
        gain_grad = jnp.sum(term_ref[:, at], axis=0, keepdims=True)
        gain_grad = jnp.concatenate([gain_grad] * (width // chunk), axis=1)
        total = None
        for h in range(nh):
            branch = dr_ref[:, span(half_chunk(ids, h, nh), cols)]
            part = dot_nt(branch, weights[h][r])
            total = part if total is None else total + part
            grad = dot_tn(low, branch).astype(BF)
            for f in range(fold):
                grads[h][r, :rows, f * cols : (f + 1) * cols] = grad[f * rows : (f + 1) * rows]
            grads[h][r, rows:] = jnp.broadcast_to(gain_grad, (GATE_ROWS, width)).astype(BF)
        do_ref[:, at] = total.astype(BF)


def project_out_back(ids, c, x2, gain, dn2, low, weights):
    nr, nh = weights[0].shape[0], len(weights)
    ins = [c, x2, gain, dn2, low, *weights]
    rows, cols = H * HD // nr, c.shape[1] // nh
    outs = [jax.ShapeDtypeStruct(c.shape, F32), jax.ShapeDtypeStruct((c.shape[0], H * HD), BF)]
    high = rows * cols // c.shape[1] + GATE_ROWS
    outs += [jax.ShapeDtypeStruct((nr, high, c.shape[1]), BF)] * nh
    got = call(
        functools.partial(out_back_kernel, nr, nh),
        (1,),
        ids,
        ins,
        [whole_spec(i.shape) for i in ins[:5]] + [out_spec(w, cols) for w in weights],
        outs,
        [whole_spec(o.shape) for o in outs],
        [pltpu.VMEM(c.shape, BF), pltpu.VMEM(c.shape, F32)],
    )
    return got[0], got[1], got[2:]


def picks(slot_ref, experts):
    tokens = slot_ref.shape[-1]
    places = lax.broadcasted_iota(jnp.int32, (CAP, tokens), 0).astype(F32)
    rows = [places == slot_ref[0, j : j + 1, :] for j in range(experts)]
    return rows[0] if experts == 1 else jnp.concatenate(rows, axis=0)


def gather_kernel(groups, per, experts, with_gates, ids, slot_ref, *rest):
    if with_gates:
        gate_ref, rest = rest[0], rest[1:]
    tokens, out_ref = rest[:groups], rest[groups]
    chosen = picks(slot_ref, experts)
    low = chosen.astype(F32).astype(BF)
    for g in range(groups):

        @pl.when(pl.program_id(0) // per == g)
        def _(g=g):
            rows = dot(low, tokens[g][0, : slot_ref.shape[-1]]).astype(BF)
            for j in range(experts):
                out_ref[j, 0] = rows[j * CAP : (j + 1) * CAP]

    if with_gates:
        for j in range(experts):
            mine = chosen[j * CAP : (j + 1) * CAP]
            gates = jnp.sum(jnp.where(mine, gate_ref[0, j : j + 1, :], 0.0), axis=1, keepdims=True)
            rest[groups + 1][j, 0] = jnp.broadcast_to(gates, (CAP, LANES))


def gather_rows(ids, slots, groups, gates=None):
    blocks, experts, length = slots.shape
    per, width = groups[0].shape[0], groups[0].shape[-1]
    ins, specs = [slots], [pl.BlockSpec((1, experts, length), lambda i, _: (i, 0, 0))]
    if gates is not None:
        ins.append(gates)
        specs.append(specs[0])
    for g, tokens in enumerate(groups):
        ins.append(tokens)
        specs.append(
            pl.BlockSpec(
                (1,) + tokens.shape[1:], lambda i, _, g=g: (jnp.clip(i - g * per, 0, per - 1), 0, 0)
            )
        )
    outs = [jax.ShapeDtypeStruct((experts, blocks, CAP, width), BF)]
    out_specs = [pl.BlockSpec((experts, 1, CAP, width), lambda i, _: (0, i, 0, 0))]
    if gates is not None:
        outs.append(jax.ShapeDtypeStruct((experts, blocks, CAP, LANES), F32))
        out_specs.append(pl.BlockSpec((experts, 1, CAP, LANES), lambda i, _: (0, i, 0, 0)))
    return call(
        functools.partial(gather_kernel, len(groups), per, experts, gates is not None),
        (blocks,),
        ids,
        ins,
        specs,
        outs,
        out_specs,
    )


def expert_kernel(nz, ids, x_ref, c_ref, gate_ref, *rest):
    weights, rest = rest[:nz], rest[nz:]
    y_ref, dx_ref, gg_ref = rest[:3]
    grads, acc_ref = rest[3 : 3 + nz], rest[3 + nz]
    chunk = x_ref.shape[-1] // nz
    step, last = pl.program_id(1), pl.num_programs(1) - 1
    a = b = ch = None
    for r in range(nz):
        at = span(z_chunk(ids, r, nz), chunk)
        x, c = x_ref[0, :, at], c_ref[0, :, at]
        parts = (
            dot(x, weights[r][0, 0]),
            dot(x, weights[r][0, 1]),
            dot(c, weights[r][0, 2]),
        )
        a, b, ch = parts if a is None else (a + parts[0], b + parts[1], ch + parts[2])
    gate = gate_ref[0][:, :1]
    sig = 1.0 / (1.0 + jnp.exp(-a))
    act = a * sig
    hidden = (act * b).astype(BF).astype(F32)
    gg_ref[0] = jnp.broadcast_to(jnp.sum(hidden * ch, axis=1, keepdims=True), gg_ref.shape[1:])
    hg = (hidden * gate).astype(BF)
    dh = ch * gate
    da = (dh * b * sig * (1.0 + a * (1.0 - sig))).astype(BF)
    db = (dh * act).astype(BF)

    @pl.when(step == 0)
    def _():
        acc_ref[...] = jnp.zeros_like(acc_ref)

    for r in range(nz):
        at = span(z_chunk(ids, r, nz), chunk)
        x, c = x_ref[0, :, at], c_ref[0, :, at]
        y_ref[0, :, at] = dot_nt(hg, weights[r][0, 2]).astype(BF)
        dx_ref[0, :, at] = (dot_nt(da, weights[r][0, 0]) + dot_nt(db, weights[r][0, 1])).astype(BF)
        acc_ref[r, 0] += dot_tn(x, da)
        acc_ref[r, 1] += dot_tn(x, db)
        acc_ref[r, 2] += dot_tn(c, hg)

    @pl.when(step == last)
    def _():
        for r in range(nz):
            grads[r][0] = acc_ref[r].astype(BF)


def run_experts(ids, x_rows, c_rows, gate_rows, weights):
    experts, rows, width = x_rows.shape
    nz = len(weights)
    hidden = weights[0].shape[-1]
    tile = 256
    block = pl.BlockSpec((1, tile, width), lambda j, i, _: (j, i, 0))
    narrow = pl.BlockSpec((1, tile, LANES), lambda j, i, _: (j, i, 0))
    matrix = pl.BlockSpec((1,) + weights[0].shape[1:], lambda j, i, _: (j, 0, 0, 0))
    got = call(
        functools.partial(expert_kernel, nz),
        (experts, rows // tile),
        ids,
        [x_rows, c_rows, gate_rows, *weights],
        [block, block, narrow] + [matrix] * nz,
        [
            jax.ShapeDtypeStruct(x_rows.shape, BF),
            jax.ShapeDtypeStruct(x_rows.shape, BF),
            jax.ShapeDtypeStruct((experts, rows, LANES), F32),
        ]
        + [jax.ShapeDtypeStruct(w.shape, BF) for w in weights],
        [block, block, narrow] + [matrix] * nz,
        [pltpu.VMEM((nz,) + weights[0].shape[1:], F32)],
    )
    return got[0], got[1], got[2], got[3:]


def spread_kernel(groups, per, experts, with_grads, ids, slot_ref, rows_ref, *rest):
    if with_grads:
        grad_ref, rest = rest[0], rest[1:]
    chosen = picks(slot_ref, experts)
    low = chosen.astype(F32).astype(BF)
    rows = [rows_ref[j, 0] for j in range(experts)]
    rows = rows[0] if experts == 1 else jnp.concatenate(rows, axis=0)
    total = dot_tn(low, rows).astype(BF)
    length, width = total.shape
    tail = None
    if with_grads:
        fit = width // length
        line = lax.broadcasted_iota(jnp.int32, (GATE_ROWS, width), 0)
        place = lax.broadcasted_iota(jnp.int32, (GATE_ROWS, width), 1) // length
        tail = jnp.zeros((GATE_ROWS, width), F32)
        for j in range(experts):
            mine = chosen[j * CAP : (j + 1) * CAP]
            sums = jnp.sum(jnp.where(mine, grad_ref[j, 0][:, :1], 0.0), axis=0, keepdims=True)
            wide = jnp.concatenate([sums] * fit, axis=1)
            number = ids[3] + j
            tail = tail + jnp.where((line == number // fit) & (place == number % fit), wide, 0.0)
    for g in range(groups):

        @pl.when(pl.program_id(0) // per == g)
        def _(g=g):
            rest[g][0, :length] = total
            if with_grads:
                rest[g][0, length:] = tail.astype(BF)


def spread_rows(ids, slots, rows, groups, grads=None):
    blocks, experts, length = slots.shape
    per, width = blocks // groups, rows.shape[-1]
    high = length + (GATE_ROWS if grads is not None else 0)
    ins = [slots, rows]
    specs = [
        pl.BlockSpec((1, experts, length), lambda i, _: (i, 0, 0)),
        pl.BlockSpec((experts, 1, CAP, width), lambda i, _: (0, i, 0, 0)),
    ]
    if grads is not None:
        ins.append(grads)
        specs.append(pl.BlockSpec((experts, 1, CAP, LANES), lambda i, _: (0, i, 0, 0)))
    return call(
        functools.partial(spread_kernel, groups, per, experts, grads is not None),
        (blocks,),
        ids,
        ins,
        specs,
        [jax.ShapeDtypeStruct((per, high, width), BF)] * groups,
        [
            pl.BlockSpec(
                (1, high, width), lambda i, _, g=g: (jnp.clip(i - g * per, 0, per - 1), 0, 0)
            )
            for g in range(groups)
        ],
    )


def mixture_kernel(nz, w_parts, groups, per, experts, tile, ids, slot_ref, gate_ref, *rest):
    n2_in, rest = rest[:groups], rest[groups:]
    c_in, rest = rest[:groups], rest[groups:]
    w_in, rest = rest[: len(w_parts)], rest[len(w_parts) :]
    dn2_out, rest = rest[:groups], rest[groups:]
    y_out, rest = rest[: groups // 2], rest[groups // 2 :]
    dw_out, rest = rest[:nz], rest[nz:]
    n2_ref, c_ref, wide_ref, down_ref, x_rows, c_rows, gate_rows, grad_rows = rest[:8]
    inner_ref, hg_ref, dwide_ref, ddown_ref = rest[8:12]
    n2_sem, c_sem, w_sem, dn2_sem, y_sem, dw_sem = rest[12:]
    hidden_size = down_ref.shape[-1]
    length = slot_ref.shape[-1]
    width = n2_ref.shape[-1]
    chunk = width // nz
    blocks = groups * per

    def n2_copy(g):
        return pltpu.make_async_copy(n2_in[g], n2_ref.at[pl.ds(g * per, per)], n2_sem.at[g])

    def c_copy(g):
        return pltpu.make_async_copy(c_in[g], c_ref.at[pl.ds(g * per, per)], c_sem.at[g])

    def matrix_of(k, wide, down, rows):
        if k == 2:
            return down.at[rows]
        return wide.at[rows + (pl.ds(k * hidden_size, hidden_size),)]

    def w_copy(n, i):
        r, first, _ = w_parts[n]
        rows = (slice(None), span(z_chunk(ids, r, nz), chunk))
        to = matrix_of(first + i, wide_ref, down_ref, rows)
        return pltpu.make_async_copy(w_in[n].at[:, i], to, w_sem.at[n, i])

    for g in range(groups):
        c_copy(g).start()
        n2_copy(g).start()
    for n, (_, _, count) in enumerate(w_parts):
        for i in range(count):
            w_copy(n, i).start()

    def chosen_rows(i):
        places = lax.broadcasted_iota(jnp.int32, (CAP, length), 0).astype(F32)
        return [places == slot_ref[i, j : j + 1, :] for j in range(experts)]

    def one_hot(chosen):
        chosen = [jnp.where(c, 1.0, 0.0).astype(BF) for c in chosen]
        return chosen[0] if experts == 1 else jnp.concatenate(chosen, axis=0)

    def gather(i, _):
        chosen = chosen_rows(i)
        low = one_hot(chosen)
        at = pl.ds(pl.multiple_of(i * CAP, CAP), CAP)
        got_x = dot(low, n2_ref[i]).astype(BF)
        got_c = dot(low, c_ref[i, :length]).astype(BF)
        for j in range(experts):
            x_rows[j, at] = got_x[j * CAP : (j + 1) * CAP]
            c_rows[j, at] = got_c[j * CAP : (j + 1) * CAP]
            gates = jnp.where(chosen[j], gate_ref[i, j : j + 1, :], 0.0)
            gate_rows[j, at] = jnp.broadcast_to(jnp.sum(gates, axis=1, keepdims=True), (CAP, LANES))
        return 0

    for g in range(groups):
        c_copy(g).wait()
        n2_copy(g).wait()
        lax.fori_loop(g * per, (g + 1) * per, gather, 0, unroll=True)
    for n, (_, _, count) in enumerate(w_parts):
        for i in range(count):
            w_copy(n, i).wait()

    def dw_copy(j, r, k):
        rows = (j, span(z_chunk(ids, r, nz), chunk))
        source = matrix_of(k, dwide_ref, ddown_ref, rows)
        return pltpu.make_async_copy(source, dw_out[r].at[j, k], dw_sem.at[j, r, k])

    for j in range(experts):

        def one_tile(i, _, j=j):
            at = pl.ds(pl.multiple_of(i * tile, tile), tile)
            x, c = x_rows[j, at], c_rows[j, at]
            wide, ch = dot(x, wide_ref[j]), dot(c, down_ref[j])
            a, b = wide[:, :hidden_size], wide[:, hidden_size:]
            gate = gate_rows[j, at][:, :1]
            sig = 1.0 / (1.0 + jnp.exp(-a))
            act = a * sig
            hidden = (act * b).astype(BF).astype(F32)
            grad = jnp.sum(hidden * ch, axis=1, keepdims=True)
            grad_rows[j, at] = jnp.broadcast_to(grad, (tile, LANES))
            hg = (hidden * gate).astype(BF)
            dh = ch * gate
            da = (dh * b * sig * (1.0 + a * (1.0 - sig))).astype(BF)
            db = (dh * act).astype(BF)
            inner_ref[at, :hidden_size], inner_ref[at, hidden_size:] = da, db
            hg_ref[at] = hg
            return 0

        lax.fori_loop(0, blocks * CAP // tile, one_tile, 0)
        for part in range(width // chunk):
            cols = slice(part * chunk, (part + 1) * chunk)
            dwide_ref[j, cols] = dot_tn(x_rows[j, :, cols], inner_ref[...]).astype(BF)
            ddown_ref[j, cols] = dot_tn(c_rows[j, :, cols], hg_ref[...]).astype(BF)
        for r in range(nz):
            for k in range(3):
                dw_copy(j, r, k).start()

        def back_tile(i, _, j=j):
            at = pl.ds(pl.multiple_of(i * tile, tile), tile)
            c_rows[j, at] = dot_nt(hg_ref[at], down_ref[j]).astype(BF)
            x_rows[j, at] = dot_nt(inner_ref[at], wide_ref[j]).astype(BF)
            return 0

        lax.fori_loop(0, blocks * CAP // tile, back_tile, 0)

    fit = width // length
    line = lax.broadcasted_iota(jnp.int32, (GATE_ROWS, width), 0)
    place = lax.broadcasted_iota(jnp.int32, (GATE_ROWS, width), 1) // length

    def spread(i, _):
        chosen = chosen_rows(i)
        low = one_hot(chosen)
        at = pl.ds(pl.multiple_of(i * CAP, CAP), CAP)
        both = []
        for rows_ref in (x_rows, c_rows):
            rows = [rows_ref[j, at] for j in range(experts)]
            both.append(rows[0] if experts == 1 else jnp.concatenate(rows, axis=0))
        n2_ref[i] = dot_tn(low, both[0]).astype(BF)
        c_ref[i, :length] = dot_tn(low, both[1]).astype(BF)
        tail = jnp.zeros((GATE_ROWS, width), F32)
        for j in range(experts):
            sums = jnp.where(chosen[j], grad_rows[j, at][:, :1], 0.0)
            wide = jnp.concatenate([jnp.sum(sums, axis=0, keepdims=True)] * fit, axis=1)
            number = ids[3] + j
            tail = tail + jnp.where((line == number // fit) & (place == number % fit), wide, 0.0)
        c_ref[i, length:] = tail.astype(BF)
        return 0

    def dn2_copy(g):
        return pltpu.make_async_copy(n2_ref.at[pl.ds(g * per, per)], dn2_out[g], dn2_sem.at[g])

    def y_copy(g):
        here = pl.ds((g % (groups // 2)) * per, per)
        return pltpu.make_async_copy(
            c_ref.at[pl.ds(g * per, per)], y_out[g // (groups // 2)].at[here], y_sem.at[g]
        )

    for g in range(groups):
        lax.fori_loop(g * per, (g + 1) * per, spread, 0, unroll=True)
        dn2_copy(g).start()
        y_copy(g).start()
    for g in range(groups):
        dn2_copy(g).wait()
        y_copy(g).wait()
    for j in range(experts):
        for r in range(nz):
            for k in range(3):
                dw_copy(j, r, k).wait()


def mixture(ids, slots, gates, n2_groups, c_groups, weights):
    groups, nz = len(n2_groups), len(weights)
    per, length, width = n2_groups[0].shape
    blocks, experts, _ = slots.shape
    high, rows = c_groups[0].shape[1], blocks * CAP
    flat = [w for row in weights for w in row]
    w_parts = []
    for r, row in enumerate(weights):
        first = 0
        for w in row:
            w_parts.append((r, first, w.shape[1]))
            first += w.shape[1]
    part = flat[0].shape
    matrices = (part[0], 3) + part[2:]
    anywhere = pl.BlockSpec(memory_space=pl.ANY)
    outs = [jax.ShapeDtypeStruct((per, length, width), BF)] * groups
    outs += [jax.ShapeDtypeStruct((groups // 2 * per, high, width), BF)] * 2
    outs += [jax.ShapeDtypeStruct(matrices, BF)] * nz
    got = call(
        functools.partial(mixture_kernel, nz, tuple(w_parts), groups, per, experts, 640),
        (1,),
        ids,
        [slots, gates, *n2_groups, *c_groups, *flat],
        [whole_spec(slots.shape), whole_spec(gates.shape)] + [anywhere] * (2 * groups + len(flat)),
        outs,
        [anywhere] * len(outs),
        [
            pltpu.VMEM((blocks, length, width), BF),
            pltpu.VMEM((blocks, high, width), BF),
            pltpu.VMEM((experts, width, 2 * part[-1]), BF),
            pltpu.VMEM((experts, width, part[-1]), BF),
            pltpu.VMEM((experts, rows, width), BF),
            pltpu.VMEM((experts, rows, width), BF),
            pltpu.VMEM((experts, rows, LANES), F32),
            pltpu.VMEM((experts, rows, LANES), F32),
            pltpu.VMEM((rows, 2 * part[-1]), BF),
            pltpu.VMEM((rows, part[-1]), BF),
            pltpu.VMEM((experts, width, 2 * part[-1]), BF),
            pltpu.VMEM((experts, width, part[-1]), BF),
            pltpu.SemaphoreType.DMA((groups,)),
            pltpu.SemaphoreType.DMA((groups,)),
            pltpu.SemaphoreType.DMA((len(flat), 3)),
            pltpu.SemaphoreType.DMA((groups,)),
            pltpu.SemaphoreType.DMA((groups,)),
            pltpu.SemaphoreType.DMA((experts, nz, 3)),
        ],
    )
    return got[:groups], got[groups : groups + 2], got[groups + 2 :]


def half_grads_kernel(nr, ids, own_rows, other_rows, gain_ref, dq_ref, own_ref, other_ref, grad_ref, normed_ref, acc_ref):
    chunk, qn, kn = grad_ref.shape[1], dq_ref.shape[1], own_ref.shape[2]
    step, count = pl.program_id(0), pl.num_programs(0)
    normalize(own_rows, other_rows, gain_ref, normed_ref)

    @pl.when(step == 0)
    def _():
        for r in range(nr):
            x = normed_ref[:, span(row_chunk(ids, r, nr), chunk)]
            grad_ref[r, :, :qn] = dot_tn(x[: dq_ref.shape[0]], dq_ref[...]).astype(BF)
        acc_ref[...] = jnp.zeros_like(acc_ref)

    def add(dkv_ref):
        grad = jnp.concatenate([dkv_ref[0], dkv_ref[1]], axis=1)
        for r in range(nr):
            acc_ref[r] += dot_tn(normed_ref[:, span(row_chunk(ids, r, nr), chunk)], grad)

    pl.when(step < count // 2)(lambda: add(own_ref))
    pl.when(step >= count // 2)(lambda: add(other_ref))

    @pl.when(step == count - 1)
    def _():
        for r in range(nr):
            grad_ref[r, :, qn:] = acc_ref[r].astype(BF)


def half_grads(ids, rows, gain, dq, dkv, half, nr, nh):
    slots, (length, width) = 2 * rows[0].shape[0], rows[0].shape[1:]
    qn, kn = H * HD // nh, KVH * HD // nh

    def body(ids, own_rows, other_rows, gain_ref, dq_ref, own_ref, other_ref, grad_ref, normed_ref, acc_ref):
        half_grads_kernel(
            nr, ids, own_rows, other_rows, gain_ref, dq_ref, own_ref, other_ref, grad_ref, normed_ref, acc_ref
        )

    def at(ids):
        return half_chunk(ids, half, nh)

    out = jax.ShapeDtypeStruct((nr, width // nr, qn + 2 * kn), BF)
    tile, steps = BLOCKS * length, slots // BLOCKS
    middle = steps // 2
    return call(
        body,
        (steps,),
        ids,
        [*flat_rows(rows), gain, dq, *dkv],
        [
            *rows_specs(steps, (tile, width)),
            whole_spec(gain.shape),
            pl.BlockSpec((length, qn), lambda i, ids: (0, at(ids))),
            pl.BlockSpec((2, tile, kn), lambda i, ids: (0, jnp.minimum(i, middle - 1), at(ids))),
            pl.BlockSpec((2, tile, kn), lambda i, ids: (0, jnp.maximum(i - middle, 0), at(ids))),
        ],
        out,
        whole_spec(out.shape),
        [pltpu.VMEM((tile, width), BF), pltpu.VMEM((nr, width // nr, 2 * kn), F32)],
    )


def rows_back_kernel(nr, nh, ids, dq_ref, dkv_ref, x_ref, dx2_ref, gain_ref, *rest):
    weights = rest[:nh]
    out_ref, grad_ref, low_ref = rest[nh:]
    width = x_ref.shape[1]
    chunk = width // nr
    qn, kn = H * HD // nh, KVH * HD // nh
    at_q, at_k, at_v, at_end = columns(nh, width)
    low_ref[...] = dkv_ref[...].astype(BF)
    for r in range(nr):
        total = None
        for h in range(nh):
            at = half_chunk(ids, h, nh)
            weight = weights[h]
            part = dot_nt(dq_ref[:, span(at, qn)], weight[r, :, at_q:at_k])
            part = part + dot_nt(low_ref[0, :, span(at, kn)], weight[r, :, at_k:at_v])
            part = part + dot_nt(low_ref[1, :, span(at, kn)], weight[r, :, at_v:at_end])
            total = part if total is None else total + part
        grad_ref[:, span(row_chunk(ids, r, nr), chunk)] = total
    x = x_ref[...]
    scaled = grad_ref[...] * gain_ref[...]
    inverse = lax.rsqrt(jnp.mean(x * x, axis=1, keepdims=True) + EPSILON)
    inner = jnp.mean(scaled * x, axis=1, keepdims=True)
    out_ref[...] = dx2_ref[...] + inverse * scaled - x * (inverse * inverse * inverse * inner)


def rows_back(ids, dq, dkv, x, dx2, gain, weights):
    nr, nh = weights[0].shape[0], len(weights)
    ins = [dq, dkv, x, dx2, gain, *weights]
    return call(
        functools.partial(rows_back_kernel, nr, nh),
        (1,),
        ids,
        ins,
        [whole_spec(i.shape) for i in ins],
        jax.ShapeDtypeStruct(x.shape, F32),
        whole_spec(x.shape),
        [pltpu.VMEM(x.shape, F32), pltpu.VMEM(dkv.shape, BF)],
    )


def swap(value, axis, distance):
    count = lax.axis_size(axis)
    return lax.ppermute(value, axis, [(i, i ^ distance) for i in range(count)])


def after(value, *done):
    return lax.optimization_barrier((value,) + done)[0]


def together(*values):
    return lax.optimization_barrier(values)


def pick(array, index):
    return lax.dynamic_index_in_dim(array, index, 0, keepdims=False)


def gather_z(value):
    chips = lax.axis_size("shard") // 2
    if chips != 4:
        return [value] + [swap(value, "shard", 2 * r) for r in range(1, chips)]
    near, far = swap(value, "shard", 2), swap(value, "shard", 4)
    return [value, near, far, swap(far, "shard", 2)]


def scatter_z(parts):
    total = parts[0].astype(F32)
    for r in range(1, len(parts)):
        total = total + swap(parts[r], "shard", 2 * r).astype(F32)
    return total


def in_order(mine, other, core, axis):
    return jnp.where(
        core == 0,
        jnp.concatenate([mine, other], axis=axis),
        jnp.concatenate([other, mine], axis=axis),
    )


def add_low(*values):
    total = values[0].astype(F32)
    for value in values[1:]:
        total = total + value.astype(F32)
    return total.astype(BF)


def sum_start(blocks, first):
    return swap(jnp.stack([blocks[first], blocks[3]]), "expert", first)


def sum_next(blocks, got, first):
    mine = blocks[0].astype(F32) + got[0].astype(F32)
    return mine, swap(add_low(blocks[3 - first], got[1]), "expert", 3 - first)


def body(
    tokens,
    block_ids,
    routes,
    gates,
    attn_gain,
    w_query,
    w_key,
    w_value,
    w_out,
    moe_gain,
    w_gate,
    w_up,
    w_down,
    cotangent,
):
    length, width = tokens.shape[1], tokens.shape[2]
    n_expert, n_shard = lax.axis_size("expert"), lax.axis_size("shard")
    chips = n_shard // 2
    local = w_gate.shape[0]
    fast = n_expert == 4 and n_shard == 8 and local % 4 == 0
    sides = 2 if fast else 1
    experts = local // (2 * sides)
    e, s = lax.axis_index("expert"), lax.axis_index("shard")
    z, core = s // 2, s % 2
    side = z // 2 if fast else 0
    first_expert = e * local + core * (local // 2) + side * experts
    ids = jnp.stack([e, z, core, first_expert]).astype(jnp.int32)
    nh = 2 if fast else 1

    x = tokens[0]
    c = cotangent[0]

    inverse_one = lax.rsqrt(jnp.mean(x * x, axis=-1, keepdims=True) + EPSILON)
    scaled_rows = (x * inverse_one).astype(BF)

    def halves(matrix):
        low = matrix.astype(BF)
        return low.reshape(low.shape[0], nh, low.shape[1] // nh).transpose(1, 0, 2)

    def column(gain):
        return jnp.broadcast_to(gain.astype(BF)[None, :, None], (nh, gain.shape[0], LANES // 2))

    packed = jnp.concatenate(
        [halves(w_out), halves(w_query), halves(w_key), halves(w_value), column(attn_gain), column(moe_gain)],
        axis=2,
    )
    at_q, at_k, at_v, at_end = columns(nh, width)

    numbers = jnp.arange(EXPERTS, dtype=jnp.int32)
    lines = EXPERTS * length // width

    def positions(start):
        s_late = after(s, start)
        owners = jnp.stack([s_late ^ (2 * r + k) for k in range(2) for r in range(chips)])
        angles = (owners * length).astype(F32)[:, None] * jnp.asarray(frequencies(), F32)[None, :]
        cosine, sine = jnp.cos(angles), jnp.sin(angles)
        every = block_ids[0].reshape(n_shard, length)
        key_blocks = jnp.concatenate(
            [pick(every, s_late ^ (2 * r + k)) for k in range(2) for r in range(chips)]
        )
        own_blocks = pick(every, s_late)
        lanes = jnp.arange(LANES, dtype=jnp.int32)[None, :]
        key_extra = ((lanes == key_blocks[:, None]) | ((lanes >= 16) & (lanes < 19))).astype(BF)
        query_extra = jnp.where((lanes < 16) & (lanes > own_blocks[:, None]), -1e30, 0.0).astype(BF)
        return cosine, sine, key_extra, query_extra

    def named_experts(routed):
        return routed[0][None, :, :] == numbers[:, None, None]

    def cotangent_rows(start):
        value, routed, gated = after((c, routes, gates), start)
        dense = jnp.sum(jnp.where(named_experts(routed), gated[0][None, :, :], 0.0), axis=-1)
        dense = dense.reshape(lines, width)
        high = dense.astype(BF)
        low = (dense - high.astype(F32)).astype(BF)
        return jnp.concatenate([value.astype(BF), high, low], axis=0)

    def own_experts(start):
        low = jnp.stack([m.astype(BF) for m in after((w_gate, w_up, w_down), start)], axis=1)
        low = low.reshape((2, local // 2) + low.shape[1:])
        return pick(low, core), swap(pick(low, 1 - core), "shard", 1)

    def over_columns(value):
        return [swap(value, "expert", r) for r in range(1, n_expert)]

    if fast:
        mine, other = pick(packed, core), pick(packed, 1 - core)
        chip = in_order(mine, swap(other, "shard", 1), core, 0)

    if fast:
        w_near, w_far = swap(chip, "shard", 2), swap(chip, "shard", 4)
        stacked = jnp.stack([chip, w_near, w_far, swap(w_far, "shard", 2)])
        block = jnp.concatenate([pick(stacked, z ^ i) for i in range(chips)], axis=0)
        c_pack = cotangent_rows(chip)
        w_mine, w_other = own_experts(chip)
        cosine, sine, key_extra, query_extra = positions(chip)
        w_got = over_columns(after(block, w_other))
        x_late = after(scaled_rows, block)
        x_near, x_far = swap(x_late, "shard", 2), swap(x_late, "shard", 4)
        x_cross = swap(x_far, "shard", 2)
        c_far = swap(after(c_pack, x_far), "shard", 4)
        chip_w = in_order(after(w_mine, x_cross), w_other, core, 2)
        chip_w = chip_w.reshape((2, experts, 3, 2 * w_gate.shape[1], w_gate.shape[2]))
        here, there = pick(chip_w, side), pick(chip_w, 1 - side)
        there = [there[:, k : k + 1] for k in range(3)]
        own_core = jnp.stack([scaled_rows, x_near, x_far, x_cross])
        x_other = swap(own_core, "shard", 1)
        rows = [own_core, x_other]
        early = (own_core, c_far, cosine, sine, key_extra, query_extra)
        w_got = [after(got, *early) for got in w_got]
        blocks = jnp.stack([block] + w_got)
        gain_cols = blocks[:, :, at_end:]
        gain_cols = jnp.concatenate([pick(gain_cols, e ^ i) for i in range(n_expert)], axis=0)
        attn_other, near_a, far_a, gain_one, gain_two, ids = together(
            swap(blocks, "shard", 1),
            here[:, :1],
            there[0],
            gain_cols[:, 0].astype(F32)[None],
            gain_cols[:, LANES // 2].astype(F32)[None],
            ids,
        )
        attn_w = [blocks, attn_other]
        near_a, far_a = swap(near_a, "shard", 2), swap(far_a, "shard", 4)
        c_own_got = over_columns(after(c_pack, attn_w[1]))
    else:
        c_pack = cotangent_rows(packed)
        own_core = jnp.stack(gather_z(scaled_rows))
        rows = [own_core, swap(own_core, "shard", 1)]
        cosine, sine, key_extra, query_extra = positions(packed)
        blocks = lax.all_gather(packed[0], ("expert", "shard"), axis=0, tiled=True)
        attn_w = [blocks[None]]
        gain_cols = blocks[:, at_end:]
        expert_w = gather_z(in_order(*own_experts(packed), core, 2))
        gain_one = gain_cols[:, 0].astype(F32)[None]
        gain_two = gain_cols[:, LANES // 2].astype(F32)[None]
    nr = attn_w[0].shape[0]

    q, k, v, cosine, sine = project(ids, rows, gain_one, cosine, sine, attn_w)
    if fast:
        c_far_got = over_columns(after(c_far, q))
        q, near_a, far_a, *c_own_got = together(q, near_a, far_a, *c_own_got)
        near_b = swap(after(here[:, 1:], q), "shard", 2)
        far_b = swap(after(there[1], q), "shard", 4)
        c_own = jnp.stack([c_pack] + c_own_got)
    mixed, mixed_low, lse = attend(ids, q, k, v, key_extra, query_extra)
    x2, n2 = project_out(ids, x, mixed_low, gain_two, attn_w)

    def places_of(groups):
        tails = jnp.concatenate([group[:, length:] for group in groups], axis=0).astype(F32)
        dense = (tails[:, :lines] + tails[:, lines:]).reshape(-1, EXPERTS, length)
        gate_here = lax.dynamic_slice_in_dim(dense, first_expert, experts, 1)
        chosen = gate_here > 0.0
        before = jnp.triu(jnp.ones((length, length), BF), 1)
        ranks = jnp.einsum("net,tu->neu", chosen.astype(BF), before, preferred_element_type=F32)
        return gate_here, jnp.where(chosen, ranks, -1.0)

    if fast:
        n2, near_b, far_b, *c_far_got = together(n2, near_b, far_b, *c_far_got)
        n2_far = swap(n2, "shard", 4)
        n2_own_got = over_columns(n2)
        cross_a = swap(after(far_a, n2), "shard", 2)
        n2_far, cross_a, *n2_own_got = together(n2_far, cross_a, *n2_own_got)
        cross_b = swap(after(far_b, n2_far), "shard", 2)
        n2_far_got = over_columns(n2_far)
        far_c = swap(after(there[2], n2_far), "shard", 4)
        n2_own = jnp.stack([n2] + n2_own_got)
        c_across = jnp.stack([after(piece, n2_far) for piece in [c_far, *c_far_got]])
        far_c, cross_b, n2_own, c_across, *n2_far_got = together(
            far_c, cross_b, n2_own, c_across, *n2_far_got
        )
        n2_across = jnp.stack([n2_far] + n2_far_got)
        cross_c = swap(far_c, "shard", 2)
        n2_groups = [n2_own, n2_across, swap(n2_own, "shard", 1), swap(n2_across, "shard", 1)]
        c_groups = [c_own, c_across] + [swap(after(g, far_c), "shard", 1) for g in (c_own, c_across)]
        gate_here, slots = places_of(c_groups)
        expert_w = [[here], [near_a, near_b], [far_a, far_b, far_c], [cross_a, cross_b, cross_c]]
        dn2_parts, y_parts, d_experts = mixture(
            ids, slots, gate_here, n2_groups, c_groups, expert_w
        )
        step = swap(d_experts[3], "shard", 2)
        dn2_other = [swap(dn2_parts[3], "shard", 1), swap(dn2_parts[2], "shard", 1)][::-1]
        far_sums = add_low(dn2_parts[1], dn2_other[1])
        own_sums = add_low(dn2_parts[0], dn2_other[0])
        far_got = [swap(far_sums[r], "expert", r) for r in range(1, n_expert)]
        dn2_far = add_low(far_sums[0], *[after(got, own_sums, step) for got in far_got])
        dn2_got = swap(dn2_far, "shard", 4)
        own_got = [swap(after(own_sums[r], dn2_far), "expert", r) for r in range(1, n_expert)]
        d_far = add_low(d_experts[2], after(step, dn2_far))
        y_sum = add_low(y_parts[0], swap(after(y_parts[1], dn2_far), "shard", 1))
        y_sum = y_sum.reshape((2, n_expert) + y_sum.shape[1:])
        far_early, near_early = after((d_far[:, :1], d_experts[1][:, :1]), dn2_got)
        own_got = [after(got, far_early, near_early, y_sum) for got in own_got]
        dn2 = sum([g.astype(F32) for g in own_got + [dn2_got]], own_sums[0].astype(F32))
    else:
        c_own = jnp.stack([c_pack] + over_columns(c_pack))
        c_groups = [c_own, swap(c_own, "shard", 1)]
        gate_here, slots = places_of(c_groups)
        n2_own = jnp.stack([n2] + over_columns(n2))
        n2_groups = [n2_own, swap(n2_own, "shard", 1)]
        c_rows, gate_rows = gather_rows(ids, slots, c_groups, gate_here)
        (x_rows,) = gather_rows(ids, slots, n2_groups)
        flat = (experts, slots.shape[0] * CAP)
        y_rows, dx_rows, grad_rows, d_experts = run_experts(
            ids,
            x_rows.reshape(flat + (width,)),
            c_rows.reshape(flat + (width,)),
            gate_rows.reshape(flat + (LANES,)),
            expert_w,
        )
        split = (experts, slots.shape[0], CAP)
        dn2_parts = spread_rows(ids, slots, dx_rows.reshape(split + (width,)), 2)
        y_parts = spread_rows(
            ids, slots, y_rows.reshape(split + (width,)), 2, grad_rows.reshape(split + (LANES,))
        )
        own_sums = add_low(dn2_parts[0], swap(dn2_parts[1], "shard", 1))
        own_got = [swap(own_sums[r], "expert", r) for r in range(1, n_expert)]
        dn2 = sum([g.astype(F32) for g in own_got], own_sums[0].astype(F32))
        y_sum = add_low(y_parts[0], swap(y_parts[1], "shard", 1))[None]

    dx2, d_mixed, d_out_w = project_out_back(ids, c, x2, gain_two, dn2, mixed_low, attn_w)
    args = (mixed, lse, k, v, key_extra, query_extra, cosine, sine)
    if fast:
        d_out_sums = add_low(d_out_w[0], swap(d_out_w[1], "shard", 1))
        far_a, near_a = swap(far_early, "shard", 4), swap(near_early, "shard", 2)
        y_sum = after(y_sum, dn2)
        got_a, got_b = sum_start(y_sum[1], 1), sum_start(y_sum[0], 2)
        done = attend_back(ids, q, after(d_mixed, d_out_sums), *args, 1)
        dq, far_a, near_a, got_a, got_b, *done = together(done[0], far_a, near_a, got_a, got_b, *done)
        far_b = swap(after(d_far[:, 1:], dq), "shard", 4)
        near_b = swap(after(d_experts[1][:, 1:], dq), "shard", 2)
        y_across, got_a = sum_next(y_sum[1], got_a, 1)
        y_out, got_b = sum_next(y_sum[0], got_b, 2)
        got_c = sum_start(after(d_out_sums, dq), 1)
        d_other = half_grads(ids, rows, gain_one, dq, done[1:], 1, nr, nh)
        dq, *dkv = attend_back(ids, q, after(d_mixed, d_other), *args, 0, done)
        dq, far_b, near_b, got_a, got_b, got_c, *dkv = together(
            dq, far_b, near_b, got_a, got_b, got_c, *dkv
        )
        y_across = (y_across + got_a.astype(F32)).astype(BF)
        y_far = swap(y_across, "shard", 4)
        d_other = swap(after(d_other, dq), "shard", 1)
        d_out_total, got_c = sum_next(d_out_sums, got_c, 1)
    else:
        dq, *dkv = attend_back(ids, q, d_mixed, *args)
        y_got = [swap(y_sum[0, r], "expert", r) for r in range(1, n_expert)]
    dkv_core = swap(dkv[1], "shard", 1)
    dkv_sums = add_low(dkv[0], dkv_core)
    if fast:
        dq = after(dq, dkv_sums, y_across)
    d_own = half_grads(ids, rows, gain_one, dq, dkv, 0, nr, nh)
    if fast:
        d_own, d_other, got_c = together(d_own, d_other, got_c)
    dkv_parts = [dkv_sums[:, r * length : (r + 1) * length] for r in range(chips)]
    if fast:
        sums = add_low(d_own, d_other)
        dkv_step = swap(dkv_parts[3], "shard", 2)
        dkv_far = add_low(dkv_parts[2], dkv_step)
        got = [swap(sums[r], "expert", r) for r in range(1, n_expert)]
        dkv_far, y_far = together(dkv_far, y_far)
        got = [after(g, dkv_far) for g in got]
        dkv_far, dkv_near = swap(dkv_far, "shard", 4), swap(after(dkv_parts[1], dkv_far), "shard", 2)
        d_out_total = (d_out_total + got_c.astype(F32)).astype(BF)
        y_out = y_out + got_b.astype(F32)
        cols = width // nh
        high = d_out_total.shape[0] - GATE_ROWS
        gain_grad = d_out_total[high, : width // n_expert]
        d_out_total = jnp.concatenate(
            [d_out_total[:high, f * cols : (f + 1) * cols] for f in range(nh)], axis=0
        )
        gain_grad = jnp.broadcast_to(gain_grad[:, None], (gain_grad.shape[0], LANES))
        d_out_total = jnp.concatenate([d_out_total, gain_grad], axis=1)
        d_total = add_low(sums[0], *got)
        total = jnp.concatenate([d_out_total, d_total], axis=1)
        total = total.reshape(chips, total.shape[0] // chips, total.shape[1])
        total = [pick(total, z ^ r) for r in range(chips)]
        step, near = swap(total[3], "shard", 2), swap(total[1], "shard", 2)
        dkv_far, dkv_near, step, near = together(dkv_far, dkv_near, step, near)
        dkv_own = sum([g.astype(F32) for g in (dkv_near, dkv_far)], dkv_parts[0].astype(F32))
        far = swap(add_low(total[2], step), "shard", 4)
        token_grad = rows_back(ids, dq, dkv_own, x, dx2, gain_one, attn_w)
        summed = total[0].astype(F32) + near.astype(F32) + after(far, token_grad).astype(F32)
        summed = summed.reshape(2, summed.shape[0] // 2, summed.shape[1])
        mine = pick(summed, core)
        other = swap(pick(summed, 1 - core).astype(BF), "shard", 1).astype(F32)
        parts = (jnp.where(core == 0, mine, other), jnp.where(core == 0, other, mine))
        out_sum = y_out + after(y_far, far).astype(F32)
    else:
        out_sum = sum([g.astype(F32) for g in y_got], y_sum[0, 0].astype(F32))
        dkv_own = scatter_z(dkv_parts)
        token_grad = rows_back(ids, dq, dkv_own, x, dx2, gain_one, attn_w)
        gain_grad = jnp.broadcast_to(d_out_w[0][0, width][:, None], (width, LANES))
        joined = jnp.concatenate([d_out_w[0][0, :width], gain_grad, d_own[0]], axis=1)
        joined = lax.psum_scatter(joined, ("expert", "shard"), scatter_dimension=0, tiled=True)
        parts = [joined.astype(F32)]

    on, qn, kn = width // nh, H * HD // nh, KVH * HD // nh
    start = on + LANES
    d_out_full = jnp.concatenate([p[:, :on] for p in parts], axis=1)
    d_gain_two = parts[0][:, on]
    d_query_w = jnp.concatenate([p[:, start : start + qn] for p in parts], axis=1)
    d_key_w = jnp.concatenate([p[:, start + qn : start + qn + kn] for p in parts], axis=1)
    d_value_w = jnp.concatenate([p[:, start + qn + kn :] for p in parts], axis=1)
    row_sums = (
        jnp.sum(w_query.astype(BF).astype(F32) * d_query_w, axis=1)
        + jnp.sum(w_key.astype(BF).astype(F32) * d_key_w, axis=1)
        + jnp.sum(w_value.astype(BF).astype(F32) * d_value_w, axis=1)
    )
    d_gain_one = row_sums / attn_gain.astype(BF).astype(F32)

    output = x2 + out_sum[:length]
    gate_sums = out_sum[length : length + lines].reshape(EXPERTS, length)
    gate_grad = jnp.sum(jnp.where(named_experts(routes), gate_sums[:, :, None], 0.0), axis=0)

    if fast:
        there_sum = jnp.concatenate([far_a, far_b], axis=1).astype(F32)
        here_sum = d_experts[0].astype(F32)
        here_sum = here_sum + jnp.concatenate([near_a, near_b], axis=1).astype(F32)
        d_chip = jnp.where(
            side == 0,
            jnp.concatenate([here_sum, there_sum], axis=0),
            jnp.concatenate([there_sum, here_sum], axis=0),
        )
    else:
        d_chip = scatter_z(d_experts)
    half = d_chip.shape[2] // 2
    d_chip = d_chip.astype(BF)
    if fast:
        d_chip = after(d_chip, *got)
    mine = lax.dynamic_slice_in_dim(d_chip, core * half, half, 2)
    other = swap(lax.dynamic_slice_in_dim(d_chip, (1 - core) * half, half, 2), "shard", 1)
    if fast:
        other = after(other, dkv_own)
    d_expert = in_order(mine, other, core, 0).astype(F32)

    return (
        output[None],
        token_grad[None],
        gate_grad[None],
        d_gain_one,
        d_query_w,
        d_key_w,
        d_value_w,
        d_out_full,
        d_gain_two,
        d_expert[:, 0],
        d_expert[:, 1],
        d_expert[:, 2],
    )


def solution(mesh):
    rows = P("expert", "shard", None)
    split = P(("expert", "shard"), None)
    gain = P(("expert", "shard"))
    in_specs = (
        rows, P("expert", None), rows, rows, gain, split, split, split, split, gain, rows, rows, rows, rows,
    )
    out_specs = (rows, rows, rows, gain, split, split, split, split, gain, rows, rows, rows)
    return jax.shard_map(body, mesh=mesh, in_specs=in_specs, out_specs=out_specs, check_vma=False)
```
